128 devices in a mesh: grp: 2 (over core), vocab: 32 (over x, y_hi, z), tok: 2 (over y_lo).
Axes of the slice: x: 4, y: 4 (y_hi: 2, y_lo: 2; y = y_hi * 2 + y_lo), z: 4, core: 2. Of those that a mesh axis runs over, the one named last changes fastest.
Arguments:
- teacher_states: bfloat16 [256, 16384], P(('grp', 'vocab', 'tok')), may hold values from -80 to 80
- teacher_gain: bfloat16 [16384], replicated, may hold values from 0.5 to 1.5
- teacher_head: bfloat16 [16384, 64128], P(None, ('grp', 'vocab', 'tok')), may hold values from -30 to 30
- student_states: bfloat16 [256, 4096], P(('grp', 'vocab', 'tok')), may hold values from -80 to 80
- student_gain: bfloat16 [4096], replicated, may hold values from 0.5 to 1.5
- student_head: bfloat16 [4096, 64128], P(None, ('grp', 'vocab', 'tok')), may hold values from -30 to 30
- token_ids: int32 [256], replicated, may hold values from 0 to 64127
- ffn_gain: bfloat16 [4096], replicated, may hold values from 0.5 to 1.5
- gate_weight: bfloat16 [4096, 14336], P(None, ('grp', 'vocab', 'tok')), may hold values from -0.09375 to 0.09375
- up_weight: bfloat16 [4096, 14336], P(None, ('grp', 'vocab', 'tok')), may hold values from -0.09375 to 0.09375
- down_weight: bfloat16 [14336, 4096], P(('grp', 'vocab', 'tok')), may hold values from -0.046875 to 0.046875
- token_weight: float32 [256], replicated, may hold values from 300 to 3000
Outputs:
- divergence: float32 [256], replicated
- state_grad: float32 [256, 4096], P(('grp', 'vocab', 'tok'))
The draws below stay inside these ranges and needn't reach their ends.
All inputs are finite; a program needn't handle non-finite values.
Results may differ from the reference program's by a relative error of at most 0.008.
Values may be sent and summed in bfloat16 or wider, within the bound.
No kernel may reach another device: no remote copies, remote signals or barrier semaphores. Data moves between devices by JAX's collectives and lax.ppermute only.
A program may use at most 128 MiB of HBM per device.

```python
import math
import jax
import jax.numpy as jnp
import numpy as np
from jax import lax

HT = 16384
DS = 4096
FF = 14336
V = 64128
TOK = 256


def clipped_normal(key, shape):
    return jnp.clip(jax.random.normal(key, shape, jnp.float32), -5.0, 5.0)


def column_places(cols):
    return jnp.arange(3, dtype=jnp.int32) * (cols // 3) + cols // 7


def row_places(rows):
    return jnp.arange(3, dtype=jnp.int32) * (rows // 3) + rows // 5


def paired_rows(key, width, salt):
    return jnp.clip(jax.random.normal(jax.random.fold_in(key, salt), (3, width), jnp.float32), -3.0, 3.0)


def head_matrix(key, rows, cols, col_scale):
    normal = clipped_normal(key, (rows, cols))
    ramp = 0.6 + 1.2 * jnp.arange(cols, dtype=jnp.float32) / cols
    return normal * (0.9 / math.sqrt(rows) * col_scale * ramp)[None, :]


def raised_pairs(matrix, noise_key, shared, target):
    rows, cols = matrix.shape
    places = column_places(cols)
    first = shared.T * (target / rows)
    second = 1.01 * first + 1.5 / math.sqrt(rows) * clipped_normal(noise_key, (rows, 3))
    return matrix.at[:, places].set(first).at[:, places + 1].set(second)


def row_states(key, rows, cols, highest):
    first_key, second_key = jax.random.split(key, 2)
    normal = jax.random.normal(first_key, (rows, cols), jnp.float32)
    mixed = normal
    scales = jnp.exp(jax.random.uniform(second_key, (rows, 1), jnp.float32, 0.0, math.log(highest)))
    return (mixed, scales)


def aligned_rows(mixed, shared, key):
    rows, cols = mixed.shape
    places = row_places(rows)
    strengths = jnp.array([0.45, 0.7, 1.0], jnp.float32)[:, None]
    noise = clipped_normal(jax.random.fold_in(key, 7), (3, cols))
    fresh = strengths * shared + jnp.sqrt(1.0 - strengths * strengths) * noise
    return mixed.at[places].set(fresh)


def draw_teacher_states(key, part):
    key, base = (jax.random.fold_in(key, 11), key)
    mixed, scales = row_states(key, TOK, HT, 10.0)
    mixed = aligned_rows(mixed, paired_rows(base, HT, 101), key)
    return (jnp.clip(mixed, -5.0, 5.0) * scales).astype(jnp.bfloat16)


def draw_student_states(key, part):
    key, base = (jax.random.fold_in(key, 13), key)
    mixed, scales = row_states(key, TOK, DS, 10.0)
    mixed = aligned_rows(mixed, paired_rows(base, DS, 103), key)
    return (jnp.clip(mixed, -5.0, 5.0) * scales).astype(jnp.bfloat16)


def draw_teacher_head(key, part):
    key, base = (jax.random.fold_in(key, 21), key)
    scale_key, matrix_key, noise_key = jax.random.split(key, 3)
    col_scale = jnp.exp(jax.random.uniform(scale_key, (V,), jnp.float32, math.log(0.5), math.log(2.0)))
    matrix = head_matrix(matrix_key, HT, V, col_scale)
    matrix = raised_pairs(matrix, noise_key, paired_rows(base, HT, 101), 260.0)
    return matrix.astype(jnp.bfloat16)


def draw_student_head(key, part):
    key, base = (jax.random.fold_in(key, 23), key)
    scale_key, matrix_key, noise_key = jax.random.split(key, 3)
    col_scale = jnp.exp(jax.random.uniform(scale_key, (V,), jnp.float32, math.log(0.5), math.log(2.0)))
    matrix = head_matrix(matrix_key, DS, V, col_scale)
    matrix = raised_pairs(matrix, noise_key, paired_rows(base, DS, 103), 260.0)
    return matrix.astype(jnp.bfloat16)


def with_ends(values, key, least, top_value):
    shape = values.shape
    spot = [jax.random.randint(jax.random.fold_in(key, axis), (), 0, shape[axis]) for axis in range(len(shape))]
    values = values.at[tuple(spot)].set(least)
    longest = shape.index(max(shape))
    spot[longest] = (spot[longest] + 1) % shape[longest]
    return values.at[tuple(spot)].set(top_value)


def shard_levels(key, dims, pieces, low, largest):
    def one(position, shards_of):
        heights = jax.random.uniform(jax.random.fold_in(jax.random.fold_in(key, 6), position), (shards_of,), jnp.float32, low / len(pieces), largest / len(pieces))
        return jnp.repeat(jnp.exp(heights), dims[position] // shards_of).reshape((-1,) + (1,) * (len(dims) - position - 1))

    factor_of = one(*pieces[0])
    for cut in pieces[1:]:
        factor_of = factor_of * one(*cut)
    return factor_of


def cumulative_ranks(count, slope):
    loads = [(1 << 20) // math.isqrt(standing ** slope) + 1 for standing in range(1, count + 1)]
    spread = 1 + sum(loads) // (1 << 30)
    return np.cumsum(np.array([max(1, weight // spread) for weight in loads]))


def ranked_ids(own_key, extent, number_of, lean):
    grid = cumulative_ranks(number_of, lean)
    lot = jax.random.randint(jax.random.fold_in(own_key, 1), extent, 0, int(grid[number_of - 1]))
    grade = jnp.searchsorted(jnp.asarray(grid, jnp.int32), lot, side="right")
    return jax.random.permutation(jax.random.fold_in(own_key, 2), number_of)[grade].astype(jnp.int32)


def scatter_about(rng, extent, spread, limit, cuts=(), kind=jnp.bfloat16):
    level = shard_levels(rng, extent, cuts, -0.22, 0.18) if cuts else 1.0
    values = jax.random.normal(rng, extent, jnp.float32) * spread * level
    return jnp.minimum(jnp.maximum(values, -limit), limit).astype(kind)


def setup_inputs(seed: int = 0) -> dict:
    arg_keys = jax.random.split(jax.random.key(seed), 13)
    return {
        "teacher_states": draw_teacher_states(jax.random.fold_in(arg_keys[12], 71), 0),
        "teacher_gain": jnp.clip(1.0 + 0.1 * jax.random.normal(arg_keys[1], (HT,), jnp.float32), 0.5, 1.5).astype(jnp.bfloat16),
        "teacher_head": draw_teacher_head(jax.random.fold_in(arg_keys[12], 71), 0),
        "student_states": draw_student_states(jax.random.fold_in(arg_keys[12], 71), 0),
        "student_gain": jnp.clip(1.0 + 0.1 * jax.random.normal(arg_keys[4], (DS,), jnp.float32), 0.5, 1.5).astype(jnp.bfloat16),
        "student_head": draw_student_head(jax.random.fold_in(arg_keys[12], 71), 0),
        "token_ids": with_ends(ranked_ids(arg_keys[6], (TOK,), V, 2), jax.random.fold_in(arg_keys[6], 3), 0, V - 1).astype(jnp.int32),
        "ffn_gain": jnp.clip(1.0 + 0.1 * jax.random.normal(arg_keys[7], (DS,), jnp.float32), 0.5, 1.5).astype(jnp.bfloat16),
        "gate_weight": scatter_about(arg_keys[8], (DS, FF), DS ** -0.5, 0.09375, ((1, 128),)),
        "up_weight": scatter_about(arg_keys[9], (DS, FF), DS ** -0.5, 0.09375, ((1, 128),)),
        "down_weight": scatter_about(arg_keys[10], (FF, DS), FF ** -0.5, 0.046875, ((0, 128),)),
        "token_weight": jnp.clip(jnp.exp(jax.random.uniform(arg_keys[11], (TOK,), jnp.float32, math.log(300.0), math.log(3000.0))), 300.0, 3000.0),
    }


eps = 1e-05

def scaled_rows(values, gain):
    inverse = lax.rsqrt(lax.optimization_barrier(jnp.mean(values * values, axis=-1, keepdims=True)) + eps)
    return values * inverse * gain.astype(jnp.float32)

def norm_back(upstream, values, gain):
    inverse = lax.rsqrt(lax.optimization_barrier(jnp.mean(values * values, axis=-1, keepdims=True)) + eps)
    gained = upstream * gain.astype(jnp.float32)
    return inverse * gained - values * inverse ** 3 * lax.optimization_barrier(jnp.mean(gained * values, axis=-1, keepdims=True))

def row_product(left, right):
    return lax.dot_general(left, right, (((1,), (1,)), ((), ())), preferred_element_type=jnp.float32)

def reference(teacher_states, teacher_gain, teacher_head, student_states, student_gain, student_head, token_ids, ffn_gain, gate_weight, up_weight, down_weight, token_weight):
    teacher_rows = scaled_rows(teacher_states.astype(jnp.float32), teacher_gain).astype(jnp.bfloat16)
    student_rows = scaled_rows(student_states.astype(jnp.float32), student_gain).astype(jnp.bfloat16)
    teacher_logits = jnp.dot(teacher_rows, teacher_head, preferred_element_type=jnp.float32)
    student_logits = jnp.dot(student_rows, student_head, preferred_element_type=jnp.float32)
    teacher_peak = lax.optimization_barrier(jnp.max(teacher_logits, axis=1))
    student_peak = lax.optimization_barrier(jnp.max(student_logits, axis=1))
    teacher_exp = jnp.exp(teacher_logits - teacher_peak[:, None])
    student_exp = jnp.exp(student_logits - student_peak[:, None])
    teacher_total = lax.optimization_barrier(jnp.sum(teacher_exp, axis=1))
    student_total = lax.optimization_barrier(jnp.sum(student_exp, axis=1))
    cross = lax.optimization_barrier(jnp.sum(teacher_exp * (teacher_logits - student_logits), axis=1))
    divergence = cross / teacher_total - teacher_peak - jnp.log(teacher_total) + student_peak + jnp.log(student_total)
    teacher_prob = teacher_exp / teacher_total[:, None]
    student_prob = student_exp / student_total[:, None]
    logit_grad = (token_weight[:, None] * (student_prob - teacher_prob)).astype(jnp.bfloat16)
    row_grad = row_product(logit_grad, student_head)
    final_grad = norm_back(row_grad, student_states.astype(jnp.float32), student_gain)
    embedded = jnp.take(student_head, token_ids.astype(jnp.int32), axis=1).T.astype(jnp.float32)
    ffn_rows = scaled_rows(embedded, ffn_gain).astype(jnp.bfloat16)
    gate = jnp.dot(ffn_rows, gate_weight, preferred_element_type=jnp.float32)
    upper = jnp.dot(ffn_rows, up_weight, preferred_element_type=jnp.float32)
    final_half = final_grad.astype(jnp.bfloat16)
    act_grad = row_product(final_half, down_weight)
    sigmoid_gate = jax.nn.sigmoid(gate)
    gate_grad = (act_grad * upper * sigmoid_gate * (1.0 + gate * (1.0 - sigmoid_gate))).astype(jnp.bfloat16)
    upper_grad = (act_grad * gate * sigmoid_gate).astype(jnp.bfloat16)
    ffn_grad = row_product(gate_grad, gate_weight) + row_product(upper_grad, up_weight)
    state_grad = final_grad + norm_back(ffn_grad, embedded, ffn_gain)
    return (divergence, state_grad)
```

```python
import jax
import jax.numpy as jnp
from jax import lax
from jax.sharding import PartitionSpec as P

eps = 1e-05
AXES = ("grp", "vocab", "tok")
DEVICES = 128
Z_MASKS = (2, 4, 6)
Y_MASKS = (1, 8, 9)
X_MASKS = (16, 32, 48)
CORE_MASKS = (64,)
STAGES = (Y_MASKS, Z_MASKS, X_MASKS, CORE_MASKS)


def scaled_rows(values, gain):
    inverse = lax.rsqrt(jnp.mean(values * values, axis=-1, keepdims=True) + eps)
    return values * inverse * gain.astype(jnp.float32)


def norm_back(upstream, values, gain):
    inverse = lax.rsqrt(jnp.mean(values * values, axis=-1, keepdims=True) + eps)
    gained = upstream * gain.astype(jnp.float32)
    return inverse * gained - values * inverse**3 * jnp.mean(
        gained * values, axis=-1, keepdims=True
    )


def row_product(left, right):
    return lax.dot_general(
        left, right, (((1,), (1,)), ((), ())), preferred_element_type=jnp.float32
    )


def swap(values, mask):
    return lax.ppermute(values, AXES, [(i, i ^ mask) for i in range(DEVICES)])


def gather_rows(block):
    for masks in STAGES:
        block = jnp.concatenate([block] + [swap(block, m) for m in masks], axis=0)
    return block


def scatter_sum(block, dtype):
    for masks in reversed(STAGES):
        rows = block.shape[0] // (len(masks) + 1)
        got = [
            swap(block[(i + 1) * rows : (i + 2) * rows].astype(dtype), m)
            for i, m in enumerate(masks)
        ]
        block = sum((g.astype(jnp.float32) for g in got), block[:rows].astype(jnp.float32))
    return block


def place_masks():
    order = [0]
    for masks in STAGES:
        order = order + [m ^ o for m in masks for o in order]
    return order


def combined(parts):
    teacher_peak = jnp.max(jnp.stack([p[0] for p in parts]), axis=0)
    student_peak = jnp.max(jnp.stack([p[1] for p in parts]), axis=0)
    teacher_total, student_total, cross = 0.0, 0.0, 0.0
    for p in parts:
        teacher_factor = jnp.exp(p[0] - teacher_peak)
        student_factor = jnp.exp(p[1] - student_peak)
        teacher_total = teacher_total + p[2] * teacher_factor
        student_total = student_total + p[3] * student_factor
        cross = cross + p[4] * teacher_factor
    return jnp.stack([teacher_peak, student_peak, teacher_total, student_total, cross])


def shards(
    teacher_states,
    teacher_gain,
    teacher_head,
    student_states,
    student_gain,
    student_head,
    token_ids,
    ffn_gain,
    gate_weight,
    up_weight,
    down_weight,
    token_weight,
):
    device = lax.axis_index(AXES)
    share = teacher_states.shape[0]
    masks = jnp.array(place_masks(), jnp.int32)
    order = ((masks ^ device)[:, None] * share + jnp.arange(share)[None, :]).reshape(-1)

    student_own = student_states.astype(jnp.float32)
    student_rows = gather_rows(scaled_rows(student_own, student_gain).astype(jnp.bfloat16))
    teacher_rows = gather_rows(
        scaled_rows(teacher_states.astype(jnp.float32), teacher_gain).astype(jnp.bfloat16)
    )

    vocab_local = student_head.shape[1]
    local_ids = jnp.take(token_ids, order) - device * vocab_local
    chosen = (local_ids[:, None] == jnp.arange(vocab_local)[None, :]).astype(jnp.bfloat16)
    embedded = scatter_sum(row_product(chosen, student_head), jnp.bfloat16)
    ffn_rows = gather_rows(scaled_rows(embedded, ffn_gain).astype(jnp.bfloat16))

    student_logits = jnp.dot(student_rows, student_head, preferred_element_type=jnp.float32)
    teacher_logits = jnp.dot(teacher_rows, teacher_head, preferred_element_type=jnp.float32)
    teacher_peak = jnp.max(teacher_logits, axis=1)
    student_peak = jnp.max(student_logits, axis=1)
    teacher_exp = jnp.exp(teacher_logits - teacher_peak[:, None])
    student_exp = jnp.exp(student_logits - student_peak[:, None])
    stats = jnp.stack(
        [
            teacher_peak,
            student_peak,
            jnp.sum(teacher_exp, axis=1),
            jnp.sum(student_exp, axis=1),
            jnp.sum(teacher_exp * (teacher_logits - student_logits), axis=1),
        ]
    )
    back = jnp.argsort(order)
    stats = jnp.take(stats, back, axis=1)
    for stage in STAGES:
        stats = combined([stats] + [swap(stats, m) for m in stage])
    teacher_peak, student_peak, teacher_total, student_total, cross = stats
    divergence = (
        cross / teacher_total
        - teacher_peak
        - jnp.log(teacher_total)
        + student_peak
        + jnp.log(student_total)
    )
    local = jnp.take(jnp.concatenate([stats, token_weight[None]]), order, axis=1)
    teacher_peak, student_peak, teacher_total, student_total, _, weight = local
    teacher_prob = jnp.exp(teacher_logits - teacher_peak[:, None]) / teacher_total[:, None]
    student_prob = jnp.exp(student_logits - student_peak[:, None]) / student_total[:, None]
    logit_grad = (weight[:, None] * (student_prob - teacher_prob)).astype(jnp.bfloat16)
    row_grad = scatter_sum(row_product(logit_grad, student_head), jnp.bfloat16)
    final_grad = norm_back(row_grad, student_own, student_gain)
    final_half = gather_rows(final_grad.astype(jnp.bfloat16))

    gate = jnp.dot(ffn_rows, gate_weight, preferred_element_type=jnp.float32)
    upper = jnp.dot(ffn_rows, up_weight, preferred_element_type=jnp.float32)
    act_grad = row_product(final_half, down_weight)
    sigmoid_gate = jax.nn.sigmoid(gate)
    gate_grad = (act_grad * upper * sigmoid_gate * (1.0 + gate * (1.0 - sigmoid_gate))).astype(
        jnp.bfloat16
    )
    upper_grad = (act_grad * gate * sigmoid_gate).astype(jnp.bfloat16)
    ffn_grad = scatter_sum(
        row_product(gate_grad, gate_weight) + row_product(upper_grad, up_weight), jnp.bfloat16
    )
    state_grad = final_grad + norm_back(ffn_grad, embedded, ffn_gain)
    return (divergence, state_grad)


def solution(mesh):
    in_specs = (
        P(AXES, None),
        P(),
        P(None, AXES),
        P(AXES, None),
        P(),
        P(None, AXES),
        P(),
        P(),
        P(None, AXES),
        P(None, AXES),
        P(AXES, None),
        P(),
    )
    out_specs = (P(), P(AXES, None))
    return jax.shard_map(shards, mesh=mesh, in_specs=in_specs, out_specs=out_specs, check_vma=False)
```

```python
import functools

import jax
import jax.numpy as jnp
from jax import lax
from jax.experimental import pallas as pl
from jax.experimental.pallas import tpu as pltpu
from jax.sharding import Mesh
from jax.sharding import PartitionSpec as P

eps = 1e-05
SHAPE = (2, 4, 2, 4, 2)
AXES = ("core", "x", "yh", "z", "yl")
CHIPS = AXES[1:]
CORES = 2
LIMIT = 40 * 1024 * 1024


def scaled_rows(values, gain):
    inverse = lax.rsqrt(jnp.mean(values * values, axis=-1, keepdims=True) + eps)
    return values * inverse * gain.astype(jnp.float32)


def norm_back(upstream, values, gain):
    inverse = lax.rsqrt(jnp.mean(values * values, axis=-1, keepdims=True) + eps)
    gained = upstream * gain.astype(jnp.float32)
    return inverse * gained - values * inverse**3 * jnp.mean(
        gained * values, axis=-1, keepdims=True
    )


def row_product(left, right):
    return lax.dot_general(
        left, right, (((1,), (1,)), ((), ())), preferred_element_type=jnp.float32
    )


def swap_cores(values):
    return lax.ppermute(values, "core", [(0, 1), (1, 0)])


def exchange(blocks, axes):
    return lax.all_to_all(blocks, axes, split_axis=0, concat_axis=0, tiled=True)


def rows_kernel(
    core_ref, teacher_ref, teacher_gain, student_ref, student_gain, keep_ref, send_ref
):
    column = 0
    for values, gain in ((student_ref, student_gain), (teacher_ref, teacher_gain)):
        half = values.shape[1] // 2
        every = values[...].astype(jnp.float32)
        inverse = lax.rsqrt(jnp.mean(every * every, axis=-1, keepdims=True) + eps)
        for part, out in ((core_ref[0], keep_ref), (1 - core_ref[0], send_ref)):
            place = pl.ds(pl.multiple_of(part * half, half), half)
            rows = values[:, place].astype(jnp.float32) * inverse
            rows = rows * gain[:, place].astype(jnp.float32)
            out[:, column : column + half] = rows.astype(jnp.bfloat16)
        column = column + half


def spread_kernel(core_ref, keep_ref, came_ref, *out_refs):
    keep, came = keep_ref[...].astype(jnp.float32), came_ref[...].astype(jnp.float32)
    first = core_ref[0] == 0
    rows = jnp.concatenate([jnp.where(first, keep, came), jnp.where(first, came, keep)], axis=0)
    rows = rows.astype(jnp.bfloat16)
    column = 0
    for out in out_refs:
        width = out.shape[2]
        out[...] = jnp.broadcast_to(rows[None, :, column : column + width], out.shape)
        column = column + width


GROUPS = (
    ((0, 0, 2048), (1, 0, 1408)),
    ((1, 1408, 1152), (1, 2560, 1152), (1, 3712, 1152)),
    ((1, 4864, 1664), (1, 6528, 1664)),
)
WIDTHS = tuple(sum(p[2] for p in group) for group in GROUPS)


def group_order(group):
    place = lax.broadcasted_iota(jnp.int32, (256, 256), 1)
    source = lax.broadcasted_iota(jnp.int32, (256, 256), 0)
    x, yh, z, yl = (place >> 6) & 3, (place >> 5) & 1, (place >> 3) & 3, (place >> 2) & 1
    if group == 1:
        wanted = (z << 6) | (x << 4) | (yh << 3) | (yl << 2) | (place & 3)
    else:
        wanted = (yh << 7) | (yl << 6) | (x << 4) | (z << 2) | (place & 3)
    return (source == wanted).astype(jnp.bfloat16)


def reordered(values, group):
    moves = group_order(group)
    high = values.astype(jnp.bfloat16)
    rest = values - high.astype(jnp.float32)
    middle = rest.astype(jnp.bfloat16)
    low = (rest - middle.astype(jnp.float32)).astype(jnp.bfloat16)
    high, middle, low = (
        jnp.dot(part, moves, preferred_element_type=jnp.float32) for part in (high, middle, low)
    )
    return (high + middle) + low


def softmax_stats(teacher, student, stats_out):
    teacher_peak = jnp.max(teacher, axis=0, keepdims=True)
    student_peak = jnp.max(student, axis=0, keepdims=True)
    teacher_exp = jnp.exp(teacher - teacher_peak)
    teacher_total = jnp.sum(teacher_exp, axis=0, keepdims=True)
    student_total = jnp.sum(jnp.exp(student - student_peak), axis=0, keepdims=True)
    cross = jnp.sum(teacher_exp * (teacher - student), axis=0, keepdims=True)
    stats = (
        teacher_peak + jnp.log(teacher_total),
        student_peak + jnp.log(student_total),
        cross / teacher_total,
    )
    stats_out[...] = jnp.zeros_like(stats_out)
    for i, row in enumerate(stats):
        stats_out[i : i + 1, :] = row[:, :128]
        stats_out[i + 3 : i + 4, :] = row[:, 128:]


def logits_kernel(group, pieces, sums, stats, place_ref, *refs):
    piece_refs, refs = refs[:pieces], refs[pieces:]
    heads, refs = refs[:2], refs[2:]
    sum_refs, refs = refs[:sums], refs[sums:]
    student_out = None
    if group == 0:
        student_out, refs = refs[0], refs[1:]
    teacher_out, refs = refs[0], refs[1:]
    if stats:
        stats_out, refs = refs[0], refs[1:]
    rows, head, row_sems, head_sems = refs
    copies = []
    column = 0
    for i, (kind, start, width) in enumerate(GROUPS[group]):
        columns = slice(column, column + width)
        size = heads[kind].shape[1] // 2
        start = pl.multiple_of(place_ref[0] * size + start, 128)
        copy = pltpu.make_async_copy(
            heads[kind].at[:, pl.ds(start, width)], head.at[:, columns], head_sems.at[i]
        )
        copy.start()
        needed = [copy]
        for m, piece in enumerate(piece_refs):
            tokens = piece.shape[0]
            at = pl.multiple_of((place_ref[1] ^ m) * tokens, tokens)
            copy = pltpu.make_async_copy(
                piece.at[:, columns], rows.at[pl.ds(at, tokens), columns], row_sems.at[i, m]
            )
            copy.start()
            needed.append(copy)
        copies.append((kind, columns, needed))
        column = column + width
    teacher = None
    for kind, columns, needed in copies:
        for copy in needed:
            copy.wait()
        term = row_product(head[:, columns], rows[:, columns])
        if kind == 0:
            student_out[...] = sum_refs[1][...] + term if sums else term
        else:
            teacher = term if teacher is None else teacher + term
    if group > 0:
        teacher = reordered(teacher, group)
    if sums:
        teacher = sum_refs[0][...] + teacher
    teacher_out[...] = teacher
    if stats:
        softmax_stats(teacher, sum_refs[1][...], stats_out)


def logits_part(group, place, pieces, student_head_t, teacher_head_t, sums=(), stats=False):
    vocab, tokens, width = teacher_head_t.shape[0], 256, WIDTHS[group]
    shape = jax.ShapeDtypeStruct((vocab, tokens), jnp.float32)
    count = 2 if group == 0 else 1
    out_shape = [shape] * count
    if stats:
        out_shape = out_shape + [jax.ShapeDtypeStruct((8, 128), jnp.float32)]
    vmem, anywhere = pl.BlockSpec(memory_space=pltpu.VMEM), pl.BlockSpec(memory_space=pl.ANY)
    rows_shape = (tokens, width)
    scratch = [
        pltpu.VMEM((vocab, width), jnp.bfloat16),
        pltpu.SemaphoreType.DMA((len(GROUPS[group]), 4)),
        pltpu.SemaphoreType.DMA((len(GROUPS[group]),)),
    ]
    if len(pieces) > 1:
        out_shape = out_shape + [jax.ShapeDtypeStruct(rows_shape, jnp.bfloat16)]
    else:
        scratch = [pltpu.VMEM(rows_shape, jnp.bfloat16)] + scratch
    return pl.pallas_call(
        functools.partial(logits_kernel, group, len(pieces), len(sums), stats),
        in_specs=[pl.BlockSpec(memory_space=pltpu.SMEM)]
        + [anywhere] * (len(pieces) + 2)
        + [vmem] * len(sums),
        out_specs=[vmem] * len(out_shape),
        out_shape=out_shape,
        scratch_shapes=scratch,
        compiler_params=pltpu.CompilerParams(vmem_limit_bytes=LIMIT),
        cost_estimate=pl.CostEstimate(
            flops=2 * vocab * tokens * width,
            bytes_accessed=(vocab + tokens) * width * 2,
            transcendentals=0,
        ),
        name="logits",
    )(place, *pieces, student_head_t, teacher_head_t, *sums)


def one_hot_rows(core):
    place = lax.broadcasted_iota(jnp.int32, (256, 256), 0)
    column = lax.broadcasted_iota(jnp.int32, (256, 256), 1)
    source = (((place >> 1) & 63) << 2) | (((place >> 7) ^ core) << 1) | (place & 1)
    return (column == source).astype(jnp.bfloat16)


def row_grad_kernel(
    core_ref, every_ref, weight_ref, teacher_ref, student_ref, head_ref,
    own_ref, send_ref, divergence_ref, grad,
):
    @pl.when(pl.program_id(0) == 0)
    def _():
        every = every_ref[...]
        peak = jnp.max(every, axis=0)
        scaled = jnp.exp(every - peak[None])
        total = jnp.sum(scaled, axis=0)
        lse = peak + jnp.log(total)
        cross = jnp.sum(scaled * pltpu.roll(every, 6, 1), axis=0) / total
        teacher_lse = jnp.concatenate([lse[0:1], lse[3:4]], axis=1)
        student_lse = jnp.concatenate([lse[1:2], lse[4:5]], axis=1)
        divergence_ref[...] = (
            jnp.concatenate([cross[0:1], cross[3:4]], axis=1) - teacher_lse + student_lse
        )
        logit_grad = weight_ref[...] * (
            jnp.exp(student_ref[...] - student_lse) - jnp.exp(teacher_ref[...] - teacher_lse)
        )
        grad[...] = row_product(
            one_hot_rows(core_ref[0]), logit_grad.astype(jnp.bfloat16)
        ).astype(jnp.bfloat16)

    out = jnp.dot(grad[...], head_ref[...], preferred_element_type=jnp.float32)
    own_ref[...] = out[:128]
    send_ref[...] = out[128:].astype(jnp.bfloat16)


def row_grad_part(core, every, weight, teacher, student, student_head_t):
    vocab, width = student_head_t.shape
    tokens = weight.shape[1]
    columns = 1024
    return pl.pallas_call(
        row_grad_kernel,
        grid_spec=pltpu.PrefetchScalarGridSpec(
            num_scalar_prefetch=1,
            grid=(width // columns,),
            in_specs=[
                pl.BlockSpec(every.shape, lambda i, c: (0, 0, 0)),
                pl.BlockSpec(weight.shape, lambda i, c: (0, 0)),
                pl.BlockSpec(teacher.shape, lambda i, c: (0, 0)),
                pl.BlockSpec(student.shape, lambda i, c: (0, 0)),
                pl.BlockSpec((vocab, columns), lambda i, c: (0, i)),
            ],
            out_specs=[
                pl.BlockSpec((tokens // 2, columns), lambda i, c: (0, i)),
                pl.BlockSpec((tokens // 2, columns), lambda i, c: (0, i)),
                pl.BlockSpec((1, tokens), lambda i, c: (0, 0)),
            ],
            scratch_shapes=[pltpu.VMEM((tokens, vocab), jnp.bfloat16)],
        ),
        out_shape=[
            jax.ShapeDtypeStruct((tokens // 2, width), jnp.float32),
            jax.ShapeDtypeStruct((tokens // 2, width), jnp.bfloat16),
            jax.ShapeDtypeStruct((1, tokens), jnp.float32),
        ],
        compiler_params=pltpu.CompilerParams(vmem_limit_bytes=LIMIT),
        cost_estimate=pl.CostEstimate(
            flops=2 * vocab * tokens * width,
            bytes_accessed=vocab * width * 2 + tokens * width * 3,
            transcendentals=2 * vocab * tokens,
        ),
        name="row_grad",
    )(core, every, weight, teacher, student, student_head_t)


def gate_kernel(own_ref, other_ref, weight_ref, out_ref):
    out_ref[:, :128] = row_product(weight_ref[...], own_ref[...])
    out_ref[:, 128:] = row_product(weight_ref[...], other_ref[...])


def gate_part(own, other, weights_t):
    hidden, tokens = weights_t.shape[0], 2 * own.shape[0]
    return pl.pallas_call(
        gate_kernel,
        out_shape=jax.ShapeDtypeStruct((hidden, tokens), jnp.float32),
        compiler_params=pltpu.CompilerParams(vmem_limit_bytes=LIMIT),
        cost_estimate=pl.CostEstimate(
            flops=2 * hidden * tokens * own.shape[1],
            bytes_accessed=(hidden + tokens) * own.shape[1] * 2,
            transcendentals=0,
        ),
        name="gate_upper",
    )(own, other, weights_t)


def ffn_grad_kernel(own_ref, other_ref, down_ref, hidden_ref, weight_ref, own_out, send_out):
    units = down_ref.shape[0]
    act_grad = jnp.concatenate(
        [row_product(down_ref[...], own_ref[...]), row_product(down_ref[...], other_ref[...])],
        axis=1,
    )
    gate, upper = hidden_ref[:units, :], hidden_ref[units:, :]
    sigmoid_gate = jax.nn.sigmoid(gate)
    gate_grad = act_grad * upper * sigmoid_gate * (1.0 + gate * (1.0 - sigmoid_gate))
    upper_grad = act_grad * gate * sigmoid_gate
    grads = jnp.concatenate([gate_grad, upper_grad], axis=0).astype(jnp.bfloat16)
    tokens = grads.shape[1]
    same = lax.broadcasted_iota(jnp.int32, (tokens, tokens), 0) == lax.broadcasted_iota(
        jnp.int32, (tokens, tokens), 1
    )
    grads = row_product(same.astype(jnp.bfloat16), grads).astype(jnp.bfloat16)
    out = jnp.dot(grads, weight_ref[...], preferred_element_type=jnp.float32)
    own_out[...] = out[: tokens // 2]
    send_out[...] = out[tokens // 2 :].astype(jnp.bfloat16)


def ffn_grad_part(own, other, down, hidden, weights_t):
    rows, width = own.shape
    return pl.pallas_call(
        ffn_grad_kernel,
        out_shape=[
            jax.ShapeDtypeStruct((rows, width), jnp.float32),
            jax.ShapeDtypeStruct((rows, width), jnp.bfloat16),
        ],
        compiler_params=pltpu.CompilerParams(vmem_limit_bytes=LIMIT),
        cost_estimate=pl.CostEstimate(
            flops=12 * down.shape[0] * rows * width,
            bytes_accessed=(3 * down.shape[0] + 5 * rows) * width * 2,
            transcendentals=0,
        ),
        name="ffn_grad",
    )(own, other, down, hidden, weights_t)


def owned_sum(own, send):
    half = (own.astype(jnp.float32) + swap_cores(send).astype(jnp.float32)).astype(jnp.bfloat16)
    blocks = half.reshape(half.shape[0] // 2, 2, half.shape[1])
    return jnp.sum(exchange(blocks, CHIPS).astype(jnp.float32), axis=0)


def every_row(rows):
    chips = 64
    own = exchange(jnp.broadcast_to(rows[None], (chips,) + rows.shape), CHIPS)
    own = own.reshape(chips * rows.shape[0], rows.shape[1])
    return own, swap_cores(own)


def shards(
    teacher_states,
    teacher_gain,
    teacher_head,
    student_states,
    student_gain,
    student_head,
    token_ids,
    ffn_gain,
    gate_weight,
    up_weight,
    down_weight,
    token_weight,
):
    core = lax.axis_index("core")
    device = lax.axis_index(AXES)
    own_half = jnp.full((1,), core, jnp.int32)

    student_own = student_states.astype(jnp.float32)
    smem = pl.BlockSpec(memory_space=pltpu.SMEM)
    vmem = pl.BlockSpec(memory_space=pltpu.VMEM)
    width = sum(WIDTHS)
    half_shape = jax.ShapeDtypeStruct((2, width), jnp.bfloat16)
    keep, send = pl.pallas_call(
        rows_kernel,
        in_specs=[smem] + [vmem] * 4,
        out_shape=[half_shape, half_shape],
        name="rows",
    )(
        own_half,
        teacher_states,
        teacher_gain.reshape(1, -1),
        student_states,
        student_gain.reshape(1, -1),
    )
    came = swap_cores(send)
    spread = pl.pallas_call(
        spread_kernel,
        in_specs=[smem] + [vmem] * 2,
        out_shape=[jax.ShapeDtypeStruct((16, 4, w), jnp.bfloat16) for w in WIDTHS],
        name="spread",
    )(own_half, keep, came)
    planes = (("yh", "z", "yl"), ("x", "yh", "yl"), ("x", "z"))
    lines = ("x", "z", ("yh", "yl"))
    places = [lax.axis_index(line) for line in lines]
    pieces = []
    for blocks, plane, line in zip(spread, planes, lines):
        block = exchange(blocks, plane)
        block = block.reshape(block.shape[0] * block.shape[1], block.shape[2])
        pieces.append(
            [block]
            + [lax.ppermute(block, line, [(i, i ^ m) for i in range(4)]) for m in (1, 2, 3)]
        )

    vocab_local = student_head.shape[1]
    ids = token_ids.reshape(2, 128)
    ids = jnp.where(core == 0, ids, ids[::-1]).reshape(256) - device * vocab_local
    chosen = (ids[:, None] == jnp.arange(vocab_local)[None, :]).astype(jnp.bfloat16)
    picked = row_product(chosen, student_head).astype(jnp.bfloat16)
    embedded = owned_sum(picked[:128], picked[128:])
    ffn_rows = every_row(scaled_rows(embedded, ffn_gain).astype(jnp.bfloat16))
    weights_t = jnp.concatenate([gate_weight.T, up_weight.T], axis=0)
    hidden = gate_part(*ffn_rows, weights_t)

    heads = (student_head.T, teacher_head.T)
    place = [jnp.stack([core, p]).astype(jnp.int32) for p in places]
    student, teacher, assembled = logits_part(0, place[0], pieces[0], *heads)
    others = [swap_cores(assembled)]
    for g in (1, 2):
        teacher, assembled = logits_part(g, place[g], pieces[g], *heads, (teacher,))
        others.append(swap_cores(assembled))
    place = jnp.stack([1 - core, 0 * core]).astype(jnp.int32)
    student, teacher = logits_part(0, place, others[:1], *heads, (teacher, student))
    (teacher,) = logits_part(1, place, others[1:2], *heads, (teacher,))
    teacher, stats = logits_part(2, place, others[2:], *heads, (teacher, student), True)
    every = exchange(jnp.broadcast_to(stats[None], (128,) + stats.shape), AXES)
    weight = token_weight.reshape(2, 64, 2).transpose(1, 0, 2).reshape(1, 256)
    own, send, divergence = row_grad_part(
        own_half, every, weight, teacher, student, heads[0]
    )
    divergence = divergence.reshape(64, 2, 2).transpose(1, 0, 2).reshape(256)

    row_grad = owned_sum(own, send)
    final_grad = norm_back(row_grad, student_own, student_gain)
    final_half = every_row(final_grad.astype(jnp.bfloat16))
    ffn_grad = owned_sum(*ffn_grad_part(*final_half, down_weight, hidden, weights_t))
    state_grad = final_grad + norm_back(ffn_grad, embedded, ffn_gain)
    return (divergence, state_grad)


def solution(mesh):
    fine = Mesh(mesh.devices.reshape(SHAPE), AXES)
    in_specs = (
        P(AXES, None),
        P(),
        P(None, AXES),
        P(AXES, None),
        P(),
        P(None, AXES),
        P(),
        P(),
        P(None, AXES),
        P(None, AXES),
        P(AXES, None),
        P(),
    )
    out_specs = (P(), P(AXES, None))
    return jax.shard_map(shards, mesh=fine, in_specs=in_specs, out_specs=out_specs, check_vma=False)
```

```python
import functools

import jax
import jax.numpy as jnp
from jax import lax
from jax.experimental import pallas as pl
from jax.experimental.pallas import tpu as pltpu
from jax.sharding import Mesh
from jax.sharding import PartitionSpec as P

eps = 1e-05
SHAPE = (2, 4, 2, 4, 2)
AXES = ("core", "x", "yh", "z", "yl")
CHIPS = AXES[1:]
MIB = 1024 * 1024

VMEM = pl.BlockSpec(memory_space=pltpu.VMEM)
SMEM = pl.BlockSpec(memory_space=pltpu.SMEM)
HBM = pl.BlockSpec(memory_space=pltpu.HBM)
ANY = pl.BlockSpec(memory_space=pl.ANY)
SEGMENTS = 8
SEGMENT = 512


def kernel_call(body, name, out_shape, limit=8, flops=0, moved=0, **options):
    return pl.pallas_call(
        body,
        name=name,
        out_shape=out_shape,
        compiler_params=pltpu.CompilerParams(vmem_limit_bytes=limit * MIB),
        cost_estimate=pl.CostEstimate(flops=flops, bytes_accessed=moved, transcendentals=0),
        **options,
    )


def shape_of(shape, dtype=jnp.bfloat16):
    return jax.ShapeDtypeStruct(shape, dtype)


def row_product(left, right):
    return lax.dot_general(
        left, right, (((1,), (1,)), ((), ())), preferred_element_type=jnp.float32
    )


def swap_cores(values):
    return lax.ppermute(values, "core", [(0, 1), (1, 0)])


def line_pieces(block, line):
    return [block] + [lax.ppermute(block, line, [(i, i ^ m) for i in range(4)]) for m in (1, 2, 3)]


def exchange(blocks, axes):
    return lax.all_to_all(blocks, axes, split_axis=0, concat_axis=0, tiled=True)


def rows_kernel(
    core_ref, teacher_ref, teacher_gain, student_ref, student_gain, keep_ref, send_ref, gains
):
    first = student_gain.shape[0]
    gains[:first, :] = student_gain[...].astype(jnp.float32)
    gains[first:, :] = teacher_gain[...].astype(jnp.float32)
    column = 0
    for values, base in ((student_ref, 0), (teacher_ref, first)):
        half = values.shape[1] // 2
        every = values[...].astype(jnp.float32)
        inverse = lax.rsqrt(jnp.mean(every * every, axis=-1, keepdims=True) + eps)
        for part, out in ((core_ref[0], keep_ref), (1 - core_ref[0], send_ref)):
            for k in range(half // 128):
                place = pl.ds(pl.multiple_of(part * half + k * 128, 128), 128)
                rows = values[:, place].astype(jnp.float32) * inverse
                rows = rows * gains[pl.ds(base + part * (half // 128) + k, 1), :]
                out[:, column + k * 128 : column + (k + 1) * 128] = rows.astype(jnp.bfloat16)
        column = column + half


def chip_kernel(core_ref, keep_ref, came_ref, out_ref):
    keep, came = keep_ref[...].astype(jnp.float32), came_ref[...].astype(jnp.float32)
    first = core_ref[0] == 0
    rows = jnp.concatenate([jnp.where(first, keep, came), jnp.where(first, came, keep)], axis=0)
    out_ref[...] = rows.astype(jnp.bfloat16)


def line_kernel(place_ref, *refs):
    pieces = [ref[...].astype(jnp.float32) for ref in refs[:4]]
    rows = []
    for j in range(4):
        m = place_ref[0] ^ j
        low = jnp.where(m == 0, pieces[0], pieces[1])
        high = jnp.where(m == 2, pieces[2], pieces[3])
        rows.append(jnp.where(m < 2, low, high))
    rows = jnp.concatenate(rows, axis=0).astype(jnp.bfloat16)
    column = 0
    for out in refs[4:]:
        out[...] = rows[:, column : column + out.shape[1]]
        column = column + out.shape[1]


def plane_kernel(place_ref, *refs):
    pieces, out, sems = refs[:4], refs[4], refs[5]
    copies = []
    for m, piece in enumerate(pieces):
        tokens = piece.shape[0]
        at = pl.multiple_of((place_ref[0] ^ m) * tokens, tokens)
        copy = pltpu.make_async_copy(piece, out.at[pl.ds(at, tokens), :], sems.at[m])
        copy.start()
        copies.append(copy)
    for copy in copies:
        copy.wait()


def in_line_order(place, pieces):
    tokens, width = pieces[0].shape
    return kernel_call(
        plane_kernel,
        "plane",
        shape_of((4 * tokens, width)),
        limit=2,
        moved=16 * tokens * width,
        in_specs=[SMEM] + [ANY] * 4,
        out_specs=ANY,
        scratch_shapes=[pltpu.SemaphoreType.DMA((4,))],
    )(place, *pieces)


GROUPS = (
    ((0, 0, 2048), (1, 0, 1536), (1, 1536, 1536)),
    ((1, 3072, 1280), (1, 4352, 1280), (1, 5632, 1280), (1, 6912, 1280)),
)
WIDTHS = tuple(sum(p[2] for p in group) for group in GROUPS)


def reordered(values):
    source = lax.broadcasted_iota(jnp.int32, (256, 256), 0)
    place = lax.broadcasted_iota(jnp.int32, (256, 256), 1)
    wanted = (((place >> 4) & 3) << 6) | (((place >> 6) & 3) << 4) | (place & 15)
    moves = (source == wanted).astype(jnp.bfloat16)
    high = values.astype(jnp.bfloat16)
    rest = values - high.astype(jnp.float32)
    middle = rest.astype(jnp.bfloat16)
    low = (rest - middle.astype(jnp.float32)).astype(jnp.bfloat16)
    high, middle, low = (
        jnp.dot(part, moves, preferred_element_type=jnp.float32) for part in (high, middle, low)
    )
    return (high + middle) + low


def softmax_stats(teacher, student, stats_out):
    teacher_peak = jnp.max(teacher, axis=0, keepdims=True)
    student_peak = jnp.max(student, axis=0, keepdims=True)
    teacher_exp = jnp.exp(teacher - teacher_peak)
    teacher_total = jnp.sum(teacher_exp, axis=0, keepdims=True)
    student_total = jnp.sum(jnp.exp(student - student_peak), axis=0, keepdims=True)
    cross = jnp.sum(teacher_exp * (teacher - student), axis=0, keepdims=True)
    stats = (
        teacher_peak + jnp.log(teacher_total),
        student_peak + jnp.log(student_total),
        cross / teacher_total,
    )
    stats_out[...] = jnp.zeros_like(stats_out)
    for i, row in enumerate(stats):
        stats_out[i : i + 1, :] = row[:, :128]
        stats_out[i + 3 : i + 4, :] = row[:, 128:]


def logits_kernel(group, own, place_ref, *refs):
    count = 4 if own else 1
    pieces, heads, refs = refs[:count], refs[count : count + 2], refs[count + 2 :]
    rows, head, row_sems, head_sems = refs[-4:]
    refs = refs[:-4]
    copies = []
    column = 0
    for i, (kind, start, width) in enumerate(GROUPS[group]):
        columns = slice(column, column + width)
        size = heads[kind].shape[1] // 2
        start = pl.multiple_of(place_ref[0] * size + start, 128)
        copy = pltpu.make_async_copy(
            heads[kind].at[:, pl.ds(start, width)], head.at[:, columns], head_sems.at[i]
        )
        copy.start()
        needed = [copy]
        for m, piece in enumerate(pieces):
            tokens = piece.shape[0]
            at = pl.multiple_of((place_ref[1] ^ m) * tokens, tokens)
            copy = pltpu.make_async_copy(
                piece.at[:, columns], rows.at[pl.ds(at, tokens), columns], row_sems.at[i, m]
            )
            copy.start()
            needed.append(copy)
        copies.append((kind, columns, needed))
        column = column + width
    sums = [None, None]
    for kind, columns, needed in copies:
        for copy in needed:
            copy.wait()
        term = row_product(head[:, columns], rows[:, columns])
        sums[kind] = term if sums[kind] is None else sums[kind] + term
    if group == 0:
        student, teacher = sums
        if own:
            student_out, teacher_out = refs
        else:
            student_in, teacher_in, student_out, teacher_out = refs
            student, teacher = student + student_in[...], teacher + teacher_in[...]
        student_out[...] = student
        teacher_out[...] = teacher
    elif own:
        refs[0][...] = sums[1]
    else:
        second_in, student_in, teacher_in, teacher_out, stats_out = refs
        teacher = teacher_in[...] + reordered(sums[1] + second_in[...])
        teacher_out[...] = teacher
        softmax_stats(teacher, student_in[...], stats_out)


def logits_part(group, place, pieces, heads, sums=()):
    vocab, tokens, width = heads[1].shape[0], 256, WIDTHS[group]
    own = len(pieces) > 1
    shape = shape_of((vocab, tokens), jnp.float32)
    out_shape = [shape, shape] if group == 0 else [shape]
    scratch = [
        pltpu.VMEM((vocab, width), jnp.bfloat16),
        pltpu.SemaphoreType.DMA((len(GROUPS[group]), 4)),
        pltpu.SemaphoreType.DMA((len(GROUPS[group]),)),
    ]
    if own:
        out_shape = out_shape + [shape_of((tokens, width))]
    else:
        scratch = [pltpu.VMEM((tokens, width), jnp.bfloat16)] + scratch
        if group == 1:
            out_shape = out_shape + [shape_of((8, 128), jnp.float32)]
    return kernel_call(
        functools.partial(logits_kernel, group, own),
        "logits",
        out_shape,
        limit=20,
        flops=2 * vocab * tokens * width,
        moved=(vocab + tokens) * width * 2,
        in_specs=[SMEM] + [ANY] * len(pieces) + [HBM] * 2 + [VMEM] * len(sums),
        out_specs=[VMEM] * len(out_shape),
        scratch_shapes=scratch,
    )(place, *pieces, *heads, *sums)


def one_hot_rows(core):
    place = lax.broadcasted_iota(jnp.int32, (256, 256), 0)
    column = lax.broadcasted_iota(jnp.int32, (256, 256), 1)
    x, yh, z, yl = (place >> 4) & 3, (place >> 3) & 1, (place >> 1) & 3, place & 1
    source = (x << 6) | (z << 4) | (yh << 3) | (yl << 2)
    source = source | (((place >> 7) ^ core) << 1) | ((place >> 6) & 1)
    return (column == source).astype(jnp.bfloat16)


def row_grad_kernel(
    core_ref, every_ref, weight_ref, teacher_ref, student_ref, head_ref,
    own_ref, send_ref, divergence_ref, grad,
):
    @pl.when(pl.program_id(0) == 0)
    def _():
        every = every_ref[...]
        peak = jnp.max(every, axis=0)
        scaled = jnp.exp(every - peak[None])
        total = jnp.sum(scaled, axis=0)
        lse = peak + jnp.log(total)
        cross = jnp.sum(scaled * pltpu.roll(every, 6, 1), axis=0) / total
        teacher_lse = jnp.concatenate([lse[0:1], lse[3:4]], axis=1)
        student_lse = jnp.concatenate([lse[1:2], lse[4:5]], axis=1)
        divergence_ref[...] = (
            jnp.concatenate([cross[0:1], cross[3:4]], axis=1) - teacher_lse + student_lse
        )
        logit_grad = weight_ref[...] * (
            jnp.exp(student_ref[...] - student_lse) - jnp.exp(teacher_ref[...] - teacher_lse)
        )
        grad[...] = row_product(
            one_hot_rows(core_ref[0]), logit_grad.astype(jnp.bfloat16)
        ).astype(jnp.bfloat16)

    out = jnp.dot(grad[...], head_ref[...], preferred_element_type=jnp.float32)
    own_ref[...] = out[:128]
    send_ref[...] = out[128:].astype(jnp.bfloat16)


def row_grad_part(core, every, weight, teacher, student, student_head_t):
    vocab, width = student_head_t.shape
    tokens, columns = weight.shape[1], 1024
    half = pl.BlockSpec((tokens // 2, columns), lambda i, c: (0, i))
    return kernel_call(
        row_grad_kernel,
        "row_grad",
        [
            shape_of((tokens // 2, width), jnp.float32),
            shape_of((tokens // 2, width)),
            shape_of((1, tokens), jnp.float32),
        ],
        limit=14,
        flops=2 * vocab * tokens * width,
        moved=vocab * width * 2 + tokens * width * 3,
        grid_spec=pltpu.PrefetchScalarGridSpec(
            num_scalar_prefetch=1,
            grid=(width // columns,),
            in_specs=[
                pl.BlockSpec(every.shape, lambda i, c: (0, 0, 0)),
                pl.BlockSpec(weight.shape, lambda i, c: (0, 0)),
                pl.BlockSpec(teacher.shape, lambda i, c: (0, 0)),
                pl.BlockSpec(student.shape, lambda i, c: (0, 0)),
                pl.BlockSpec((vocab, columns), lambda i, c: (0, i)),
            ],
            out_specs=[half, half, pl.BlockSpec((1, tokens), lambda i, c: (0, 0))],
            scratch_shapes=[pltpu.VMEM((tokens, vocab), jnp.bfloat16)],
        ),
    )(core, every, weight, teacher, student, student_head_t)


def pick_kernel(ids_ref, head_ref, own_ref, send_ref):
    tokens, vocab = ids_ref.shape[0], head_ref.shape[0]
    entry = lax.broadcasted_iota(jnp.int32, (tokens, vocab), 1)
    chosen = (ids_ref[...] == entry).astype(jnp.bfloat16)
    out = jnp.dot(chosen, head_ref[...], preferred_element_type=jnp.float32)
    own_ref[...] = out[: tokens // 2].astype(jnp.bfloat16)
    send_ref[...] = out[tokens // 2 :].astype(jnp.bfloat16)


def pick_part(ids, student_head_t):
    vocab, width = student_head_t.shape
    tokens, columns = ids.shape[0], 1024
    half = pl.BlockSpec((tokens // 2, columns), lambda i: (0, i))
    shape = shape_of((tokens // 2, width))
    return kernel_call(
        pick_kernel,
        "pick",
        [shape, shape],
        flops=2 * vocab * tokens * width,
        moved=(vocab + tokens) * width * 2,
        grid=(width // columns,),
        in_specs=[
            pl.BlockSpec(ids.shape, lambda i: (0, 0)),
            pl.BlockSpec((vocab, columns), lambda i: (0, i)),
        ],
        out_specs=[half, half],
    )(ids, student_head_t)


def join_kernel(own_ref, came_ref, out_ref, rows):
    chips = out_ref.shape[0]
    for t in range(2):
        for i in range(SEGMENTS):
            for k in range(SEGMENT // 128):
                part = slice(t * chips, (t + 1) * chips)
                lanes = slice(i * SEGMENT + k * 128, i * SEGMENT + (k + 1) * 128)
                total = own_ref[part, lanes].astype(jnp.float32)
                total = total + came_ref[part, lanes].astype(jnp.float32)
                at = pl.ds(t * SEGMENTS + i, chips, stride=2 * SEGMENTS)
                rows[k, at, :] = total
    for k in range(SEGMENT // 128):
        out_ref[:, :, k * 128 : (k + 1) * 128] = (
            rows[k].reshape(chips, 2 * SEGMENTS, 128).astype(jnp.bfloat16)
        )


def join_part(own, send):
    chips = own.shape[0] // 2
    block = (chips, 2 * SEGMENTS, SEGMENT)
    return kernel_call(
        join_kernel,
        "join",
        shape_of(block),
        limit=10,
        moved=own.size * 8,
        in_specs=[VMEM] * 2,
        out_specs=VMEM,
        scratch_shapes=[pltpu.VMEM((SEGMENT // 128, chips * 2 * SEGMENTS, 128), jnp.float32)],
    )(own, swap_cores(send))


def block_gain(gain_ref):
    gain = gain_ref[...].astype(jnp.float32)
    lanes = SEGMENT // 128
    token = jnp.concatenate(
        [
            jnp.concatenate([gain[lanes * i + k : lanes * i + k + 1] for k in range(lanes)], axis=1)
            for i in range(SEGMENTS)
        ],
        axis=0,
    )
    return jnp.concatenate([token, token], axis=0)


def block_mean(values):
    means = []
    for t in range(2):
        part = values[t * SEGMENTS : (t + 1) * SEGMENTS]
        total = jnp.sum(jnp.sum(part, axis=0, keepdims=True), axis=1, keepdims=True)
        means.append(jnp.broadcast_to(total / (SEGMENTS * SEGMENT), (SEGMENTS, 1)))
    return jnp.concatenate(means, axis=0)


def block_inverse(values):
    return lax.rsqrt(block_mean(values * values) + eps)


def block_back(upstream, values, gain):
    inverse = block_inverse(values)
    gained = upstream * gain
    return inverse * gained - values * inverse**3 * block_mean(gained * values)


def block_sum(blocks_ref):
    return jnp.sum(blocks_ref[...].astype(jnp.float32), axis=0)


def embed_kernel(blocks_ref, gain_ref, embedded_ref, out_ref):
    values = block_sum(blocks_ref)
    embedded_ref[...] = values
    rows = (values * block_inverse(values) * block_gain(gain_ref)).astype(jnp.bfloat16)
    out_ref[...] = jnp.broadcast_to(rows[None], out_ref.shape)


def final_kernel(blocks_ref, states_ref, gain_ref, grad_ref, out_ref, states):
    for i in range(SEGMENTS):
        part = states_ref[:, i * SEGMENT : (i + 1) * SEGMENT].astype(jnp.float32)
        for t in range(2):
            states[t * SEGMENTS + i : t * SEGMENTS + i + 1, :] = part[t : t + 1]
    grad = block_back(block_sum(blocks_ref), states[...], block_gain(gain_ref))
    grad_ref[...] = grad
    out_ref[...] = jnp.broadcast_to(grad.astype(jnp.bfloat16)[None], out_ref.shape)


def state_kernel(blocks_ref, grad_ref, embedded_ref, gain_ref, out_ref):
    back = block_back(block_sum(blocks_ref), embedded_ref[...], block_gain(gain_ref))
    grad = grad_ref[...] + back
    for t in range(2):
        for i in range(SEGMENTS):
            out_ref[t : t + 1, i * SEGMENT : (i + 1) * SEGMENT] = grad[
                t * SEGMENTS + i : t * SEGMENTS + i + 1
            ]


BLOCK = (2 * SEGMENTS, SEGMENT)


def owner_part(body, name, blocks, *others, scratch=()):
    return kernel_call(
        body,
        name,
        [shape_of(BLOCK, jnp.float32), shape_of(blocks.shape)],
        moved=blocks.size * 4,
        in_specs=[VMEM] * (1 + len(others)),
        out_specs=[VMEM] * 2,
        scratch_shapes=list(scratch),
    )(blocks, *others)


def spread_rows(refs, scratches):
    for ref, rows in zip(refs, scratches):
        values = ref[...].astype(jnp.float32)
        values = values.reshape(values.shape[0] * values.shape[1], values.shape[2])
        for k in range(SEGMENT // 128):
            rows[k] = values[:, k * 128 : (k + 1) * 128]


def segment_rows(scratches, segment):
    parts = []
    for rows in scratches:
        chips = rows.shape[1] // (2 * SEGMENTS)
        for t in range(2):
            at = pl.ds(t * SEGMENTS + segment, chips, stride=2 * SEGMENTS)
            parts.append(
                jnp.concatenate([rows[k, at, :] for k in range(SEGMENT // 128)], axis=1)
            )
    return jnp.concatenate(parts, axis=0).astype(jnp.bfloat16)


def gate_kernel(own_ref, other_ref, gate_ref, up_ref, out_ref, *scratches):
    spread_rows((own_ref, other_ref), scratches)
    total = None
    for i in range(SEGMENTS):
        columns = slice(i * SEGMENT, (i + 1) * SEGMENT)
        weight = jnp.concatenate([gate_ref[:, columns], up_ref[:, columns]], axis=0)
        term = row_product(weight, segment_rows(scratches, i))
        total = term if total is None else total + term
    out_ref[...] = total


def ffn_grad_kernel(
    own_ref, other_ref, down_ref, hidden_ref, gate_ref, up_ref, own_out, send_out, *scratches
):
    spread_rows((own_ref, other_ref), scratches)
    units = down_ref.shape[0]
    act_grad = None
    for i in range(SEGMENTS):
        term = row_product(
            down_ref[:, i * SEGMENT : (i + 1) * SEGMENT], segment_rows(scratches, i)
        )
        act_grad = term if act_grad is None else act_grad + term
    gate, upper = hidden_ref[:units, :], hidden_ref[units:, :]
    sigmoid_gate = jax.nn.sigmoid(gate)
    gate_grad = act_grad * upper * sigmoid_gate * (1.0 + gate * (1.0 - sigmoid_gate))
    upper_grad = act_grad * gate * sigmoid_gate
    grads = jnp.concatenate([gate_grad, upper_grad], axis=0).astype(jnp.bfloat16)
    tokens = grads.shape[1]
    same = lax.broadcasted_iota(jnp.int32, (tokens, tokens), 0) == lax.broadcasted_iota(
        jnp.int32, (tokens, tokens), 1
    )
    grads = row_product(same.astype(jnp.bfloat16), grads).astype(jnp.bfloat16)
    for i in range(SEGMENTS):
        columns = slice(i * SEGMENT, (i + 1) * SEGMENT)
        weight = jnp.concatenate([gate_ref[:, columns], up_ref[:, columns]], axis=0)
        out = jnp.dot(grads, weight, preferred_element_type=jnp.float32)
        own_out[:, columns] = out[: tokens // 2]
        send_out[:, columns] = out[tokens // 2 :].astype(jnp.bfloat16)


def ffn_part(body, name, out_shape, blocks, *others):
    rows = blocks.shape[0] * blocks.shape[1]
    scratch = pltpu.VMEM((SEGMENT // 128, rows, 128), jnp.float32)
    return kernel_call(
        body,
        name,
        out_shape,
        limit=18,
        flops=16 * 112 * 256 * 4096 // 2,
        moved=blocks.size * 8,
        in_specs=[VMEM] * (2 + len(others)),
        out_specs=[VMEM] * len(out_shape),
        scratch_shapes=[scratch, scratch],
    )(blocks, swap_cores(blocks), *others)


def shards(
    teacher_states,
    teacher_gain,
    teacher_head,
    student_states,
    student_gain,
    student_head,
    token_ids,
    ffn_gain,
    gate_weight,
    up_weight,
    down_weight,
    token_weight,
):
    core = lax.axis_index("core")
    device = lax.axis_index(AXES)
    own_core = jnp.full((1,), core, jnp.int32)
    x, z, y = (
        jnp.full((1,), lax.axis_index(line), jnp.int32) for line in ("x", "z", ("yh", "yl"))
    )
    teacher_gain, student_gain, ffn_gain = (
        gain.reshape(-1, 128) for gain in (teacher_gain, student_gain, ffn_gain)
    )
    student_head_t, teacher_head_t = student_head.T, teacher_head.T
    heads = (student_head_t, teacher_head_t)
    gate_t, up_t = gate_weight.T, up_weight.T

    width = sum(WIDTHS)
    half_shape = shape_of((2, width))
    keep, send = kernel_call(
        rows_kernel,
        "rows",
        [half_shape, half_shape],
        in_specs=[SMEM] + [VMEM] * 4,
        out_specs=[VMEM] * 2,
        scratch_shapes=[pltpu.VMEM((160, 128), jnp.float32)],
    )(own_core, teacher_states, teacher_gain, student_states, student_gain)
    rows = kernel_call(
        chip_kernel,
        "chip",
        shape_of((4, width)),
        in_specs=[SMEM] + [VMEM] * 2,
        out_specs=VMEM,
    )(own_core, keep, swap_cores(send))
    first, second = kernel_call(
        line_kernel,
        "line",
        [shape_of((16, w)) for w in WIDTHS],
        in_specs=[SMEM] + [VMEM] * 4,
        out_specs=[VMEM] * 2,
    )(y, *line_pieces(rows, ("yh", "yl")))
    first, second = line_pieces(first, "z"), line_pieces(second, "x")
    first, second = in_line_order(z, first), in_line_order(x, second)

    ids = token_ids.reshape(2, 64, 2).transpose(0, 2, 1).reshape(2, 128)
    ids = jnp.where(core == 0, ids, ids[::-1]).reshape(256, 1) - device * student_head.shape[1]
    ids, second = lax.optimization_barrier((ids, second))
    picked = join_part(*pick_part(ids, student_head_t))

    first, second = line_pieces(first, "x"), line_pieces(second, "z")
    first, picked = lax.optimization_barrier((first, picked))
    picked = exchange(picked, CHIPS)
    place = jnp.concatenate([own_core, x])
    student, teacher, first = logits_part(0, place, first, heads)
    place = jnp.concatenate([own_core, z])
    teacher_second, second = logits_part(1, place, second, heads)
    first, second = swap_cores(first), swap_cores(second)
    first, picked = lax.optimization_barrier((first, picked))
    place = jnp.concatenate([1 - own_core, 0 * x])
    student, teacher = logits_part(0, place, [first], heads, (student, teacher))
    teacher, stats = logits_part(
        1, place, [second], heads, (teacher_second, student, teacher)
    )
    every = exchange(jnp.broadcast_to(stats[None], (128,) + stats.shape), AXES)
    embedded, ffn_rows = owner_part(embed_kernel, "embed", picked, ffn_gain)
    ffn_rows = exchange(ffn_rows, CHIPS)

    weight = token_weight.reshape(2, 4, 2, 4, 2, 2).transpose(1, 3, 2, 4, 0, 5).reshape(1, 256)
    own, send, divergence = row_grad_part(
        own_core, every, weight, teacher, student, student_head_t
    )
    divergence = divergence.reshape(4, 4, 2, 2, 2, 2).transpose(4, 0, 2, 1, 3, 5).reshape(256)
    row_grad = join_part(own, send)
    row_grad, ffn_rows = lax.optimization_barrier((row_grad, ffn_rows))
    row_grad = exchange(row_grad, CHIPS)
    (hidden,) = ffn_part(
        gate_kernel, "gate_upper", [shape_of((224, 256), jnp.float32)], ffn_rows, gate_t, up_t
    )
    final_grad, final_half = owner_part(
        final_kernel,
        "final",
        row_grad,
        student_states,
        student_gain,
        scratch=[pltpu.VMEM(BLOCK, jnp.float32)],
    )
    final_half, hidden = lax.optimization_barrier((final_half, hidden))
    final_half = exchange(final_half, CHIPS)
    shape = (128, 4096)
    own, send = ffn_part(
        ffn_grad_kernel,
        "ffn_grad",
        [shape_of(shape, jnp.float32), shape_of(shape)],
        final_half,
        down_weight,
        hidden,
        gate_t,
        up_t,
    )
    ffn_grad = exchange(join_part(own, send), CHIPS)
    state_grad = kernel_call(
        state_kernel,
        "state",
        shape_of((2, 4096), jnp.float32),
        in_specs=[VMEM] * 4,
        out_specs=VMEM,
    )(ffn_grad, final_grad, embedded, ffn_gain)
    return (divergence, state_grad)


def solution(mesh):
    fine = Mesh(mesh.devices.reshape(SHAPE), AXES)
    in_specs = (
        P(AXES, None),
        P(),
        P(None, AXES),
        P(AXES, None),
        P(),
        P(None, AXES),
        P(),
        P(),
        P(None, AXES),
        P(None, AXES),
        P(AXES, None),
        P(),
    )
    out_specs = (P(), P(AXES, None))
    return jax.shard_map(shards, mesh=fine, in_specs=in_specs, out_specs=out_specs, check_vma=False)
```

```python
import functools

import jax
import jax.numpy as jnp
from jax import lax
from jax.experimental import pallas as pl
from jax.experimental.pallas import tpu as pltpu
from jax.sharding import Mesh
from jax.sharding import PartitionSpec as P

eps = 1e-05
SHAPE = (2, 4, 2, 4, 2)
AXES = ("core", "x", "yh", "z", "yl")
CHIPS = AXES[1:]
MIB = 1024 * 1024

VMEM = pl.BlockSpec(memory_space=pltpu.VMEM)
SMEM = pl.BlockSpec(memory_space=pltpu.SMEM)
ANY = pl.BlockSpec(memory_space=pl.ANY)
SEGMENTS = 8
SEGMENT = 512


def kernel_call(body, name, out_shape, limit=8, **options):
    return pl.pallas_call(
        body,
        name=name,
        out_shape=out_shape,
        compiler_params=pltpu.CompilerParams(vmem_limit_bytes=limit * MIB),
        cost_estimate=pl.CostEstimate(flops=1, bytes_accessed=1, transcendentals=0),
        **options,
    )


def shape_of(shape, dtype=jnp.bfloat16):
    return jax.ShapeDtypeStruct(shape, dtype)


def row_product(left, right):
    return lax.dot_general(
        left, right, (((1,), (1,)), ((), ())), preferred_element_type=jnp.float32
    )


def swap_cores(values):
    return lax.ppermute(values, "core", [(0, 1), (1, 0)])


def line_pieces(block, line):
    return [block] + [lax.ppermute(block, line, [(i, i ^ m) for i in range(4)]) for m in (1, 2, 3)]


def exchange(blocks, axes):
    return lax.all_to_all(blocks, axes, split_axis=0, concat_axis=0, tiled=True)


def rows_kernel(
    core_ref, teacher_from, teacher_gain, student_from, student_gain, keep_ref, send_ref,
    teacher_ref, student_ref, teacher_gains, student_gains, gains, sems,
):
    copies = [
        pltpu.make_async_copy(source, target, sems.at[i])
        for i, (source, target) in enumerate(
            (
                (student_gain, student_gains),
                (student_from, student_ref),
                (teacher_gain, teacher_gains),
                (teacher_from, teacher_ref),
            )
        )
    ]
    for copy in copies:
        copy.start()
    for copy in copies:
        copy.wait()
    first = student_gain.shape[0]
    gains[:first, :] = student_gains[...].astype(jnp.float32)
    gains[first:, :] = teacher_gains[...].astype(jnp.float32)
    column = 0
    for values, base in ((student_ref, 0), (teacher_ref, first)):
        half = values.shape[1] // 2
        every = values[...].astype(jnp.float32)
        inverse = lax.rsqrt(jnp.mean(every * every, axis=-1, keepdims=True) + eps)
        for part, out in ((core_ref[0], keep_ref), (1 - core_ref[0], send_ref)):
            for k in range(half // 128):
                place = pl.ds(pl.multiple_of(part * half + k * 128, 128), 128)
                rows = values[:, place].astype(jnp.float32) * inverse
                rows = rows * gains[pl.ds(base + part * (half // 128) + k, 1), :]
                out[:, column + k * 128 : column + (k + 1) * 128] = rows.astype(jnp.bfloat16)
        column = column + half


def chip_kernel(core_ref, keep_ref, came_ref, out_ref):
    keep, came = keep_ref[...].astype(jnp.float32), came_ref[...].astype(jnp.float32)
    first = core_ref[0] == 0
    rows = jnp.concatenate([jnp.where(first, keep, came), jnp.where(first, came, keep)], axis=0)
    out_ref[...] = rows.astype(jnp.bfloat16)


def line_kernel(place_ref, *refs):
    pieces = [ref[...].astype(jnp.float32) for ref in refs[:4]]
    rows = []
    for j in range(4):
        m = place_ref[0] ^ j
        low = jnp.where(m == 0, pieces[0], pieces[1])
        high = jnp.where(m == 2, pieces[2], pieces[3])
        rows.append(jnp.where(m < 2, low, high))
    rows = jnp.concatenate(rows, axis=0).astype(jnp.bfloat16)
    column = 0
    for out in refs[4:]:
        out[...] = rows[:, column : column + out.shape[1]]
        column = column + out.shape[1]


def plane_kernel(place_ref, *refs):
    pieces, out, sems = refs[:4], refs[4], refs[5]
    copies = []
    for m, piece in enumerate(pieces):
        tokens = piece.shape[0]
        at = pl.multiple_of((place_ref[0] ^ m) * tokens, tokens)
        copy = pltpu.make_async_copy(piece, out.at[pl.ds(at, tokens), :], sems.at[m])
        copy.start()
        copies.append(copy)
    for copy in copies:
        copy.wait()


def in_line_order(place, pieces):
    tokens, width = pieces[0].shape
    return kernel_call(
        plane_kernel,
        "plane",
        shape_of((4 * tokens, width)),
        limit=2,
        in_specs=[SMEM] + [ANY] * 4,
        out_specs=ANY,
        scratch_shapes=[pltpu.SemaphoreType.DMA((4,))],
    )(place, *pieces)


GROUPS = (
    ((0, 0, 2048), (1, 0, 1536), (1, 1536, 1536)),
    ((1, 3072, 1280), (1, 4352, 1280), (1, 5632, 1280), (1, 6912, 1280)),
)
WIDTHS = tuple(sum(p[2] for p in group) for group in GROUPS)


def reordered(values):
    source = lax.broadcasted_iota(jnp.int32, (256, 256), 0)
    place = lax.broadcasted_iota(jnp.int32, (256, 256), 1)
    wanted = (((place >> 4) & 3) << 6) | (((place >> 6) & 3) << 4) | (place & 15)
    moves = (source == wanted).astype(jnp.bfloat16)
    high = values.astype(jnp.bfloat16)
    rest = values - high.astype(jnp.float32)
    middle = rest.astype(jnp.bfloat16)
    low = (rest - middle.astype(jnp.float32)).astype(jnp.bfloat16)
    high, middle, low = (
        jnp.dot(part, moves, preferred_element_type=jnp.float32) for part in (high, middle, low)
    )
    return (high + middle) + low


def softmax_stats(teacher, student, stats_out):
    teacher_peak = jnp.max(teacher, axis=0, keepdims=True)
    student_peak = jnp.max(student, axis=0, keepdims=True)
    teacher_exp = jnp.exp(teacher - teacher_peak)
    teacher_total = jnp.sum(teacher_exp, axis=0, keepdims=True)
    student_total = jnp.sum(jnp.exp(student - student_peak), axis=0, keepdims=True)
    cross = jnp.sum(teacher_exp * (teacher - student), axis=0, keepdims=True)
    stats = (
        teacher_peak + jnp.log(teacher_total),
        student_peak + jnp.log(student_total),
        cross / teacher_total,
    )
    stats_out[...] = jnp.zeros_like(stats_out)
    for i, row in enumerate(stats):
        stats_out[i : i + 1, :] = row[:, :128]
        stats_out[i + 3 : i + 4, :] = row[:, 128:]


def logits_kernel(last, place_ref, *refs):
    rows_from, heads, refs = refs[:2], refs[2:4], refs[4:]
    rows, head, row_sems, head_sems = refs[-4:]
    refs = refs[:-4]
    copies = []
    column = 0
    for group, source in zip(GROUPS, rows_from):
        base = column
        for kind, start, width in group:
            i = len(copies)
            columns = slice(column, column + width)
            size = heads[kind].shape[1] // 2
            start = pl.multiple_of(place_ref[0] * size + start, 128)
            pair = (
                pltpu.make_async_copy(
                    source.at[:, column - base : column - base + width],
                    rows.at[:, columns],
                    row_sems.at[i],
                ),
                pltpu.make_async_copy(
                    heads[kind].at[:, pl.ds(start, width)], head.at[:, columns], head_sems.at[i]
                ),
            )
            for copy in pair:
                copy.start()
            copies.append((kind + (base > 0), columns, pair))
            column = column + width
    sums = [None, None, None]
    for kind, columns, pair in copies:
        for copy in pair:
            copy.wait()
        term = row_product(head[:, columns], rows[:, columns])
        sums[kind] = term if sums[kind] is None else sums[kind] + term
    if last:
        came, (student_out, teacher_out, stats_out) = refs[:3], refs[3:]
        student, teacher, second = (total + ref[...] for total, ref in zip(sums, came))
        teacher = teacher + reordered(second)
        student_out[...] = student
        teacher_out[...] = teacher
        softmax_stats(teacher, student, stats_out)
    else:
        for total, out in zip(sums, refs):
            out[...] = total


def logits_part(place, rows, heads, sums=()):
    vocab, tokens = heads[1].shape[0], rows[0].shape[0]
    shape = shape_of((vocab, tokens), jnp.float32)
    last = len(sums) > 0
    pieces = sum(len(group) for group in GROUPS)
    out_shape = [shape, shape, shape_of((8, 128), jnp.float32) if last else shape]
    return kernel_call(
        functools.partial(logits_kernel, last),
        "logits",
        out_shape,
        limit=56,
        in_specs=[SMEM] + [ANY] * 4 + [VMEM] * len(sums),
        out_specs=[VMEM] * 3,
        scratch_shapes=[
            pltpu.VMEM((tokens, sum(WIDTHS)), jnp.bfloat16),
            pltpu.VMEM((vocab, sum(WIDTHS)), jnp.bfloat16),
            pltpu.SemaphoreType.DMA((pieces,)),
            pltpu.SemaphoreType.DMA((pieces,)),
        ],
    )(place, *rows, *heads, *sums)


def one_hot_rows(core):
    place = lax.broadcasted_iota(jnp.int32, (256, 256), 0)
    column = lax.broadcasted_iota(jnp.int32, (256, 256), 1)
    x, yh, z, yl = (place >> 4) & 3, (place >> 3) & 1, (place >> 1) & 3, place & 1
    source = (x << 6) | (z << 4) | (yh << 3) | (yl << 2)
    source = source | (((place >> 7) ^ core) << 1) | ((place >> 6) & 1)
    return (column == source).astype(jnp.bfloat16)


def row_grad_kernel(
    core_ref, every_ref, weight_ref, teacher_ref, student_ref, head_ref,
    own_ref, send_ref, divergence_ref, grad,
):
    @pl.when(pl.program_id(0) == 0)
    def _():
        every = every_ref[...]
        peak = jnp.max(every, axis=0)
        scaled = jnp.exp(every - peak[None])
        total = jnp.sum(scaled, axis=0)
        lse = peak + jnp.log(total)
        cross = jnp.sum(scaled * pltpu.roll(every, 6, 1), axis=0) / total
        teacher_lse = jnp.concatenate([lse[0:1], lse[3:4]], axis=1)
        student_lse = jnp.concatenate([lse[1:2], lse[4:5]], axis=1)
        divergence_ref[...] = (
            jnp.concatenate([cross[0:1], cross[3:4]], axis=1) - teacher_lse + student_lse
        )
        logit_grad = weight_ref[...] * (
            jnp.exp(student_ref[...] - student_lse) - jnp.exp(teacher_ref[...] - teacher_lse)
        )
        grad[...] = row_product(
            one_hot_rows(core_ref[0]), logit_grad.astype(jnp.bfloat16)
        ).astype(jnp.bfloat16)

    out = jnp.dot(grad[...], head_ref[...], preferred_element_type=jnp.float32)
    own_ref[...] = out[:128]
    send_ref[...] = out[128:].astype(jnp.bfloat16)


def row_grad_part(core, every, weight, teacher, student, student_head_t):
    vocab, width = student_head_t.shape
    tokens, columns = weight.shape[1], 1024
    half = pl.BlockSpec((tokens // 2, columns), lambda i, c: (0, i))
    return kernel_call(
        row_grad_kernel,
        "row_grad",
        [
            shape_of((tokens // 2, width), jnp.float32),
            shape_of((tokens // 2, width)),
            shape_of((1, tokens), jnp.float32),
        ],
        limit=56,
        grid_spec=pltpu.PrefetchScalarGridSpec(
            num_scalar_prefetch=1,
            grid=(width // columns,),
            in_specs=[
                pl.BlockSpec(every.shape, lambda i, c: (0, 0, 0)),
                pl.BlockSpec(weight.shape, lambda i, c: (0, 0)),
                pl.BlockSpec(teacher.shape, lambda i, c: (0, 0)),
                pl.BlockSpec(student.shape, lambda i, c: (0, 0)),
                pl.BlockSpec((vocab, columns), lambda i, c: (0, i)),
            ],
            out_specs=[half, half, pl.BlockSpec((1, tokens), lambda i, c: (0, 0))],
            scratch_shapes=[pltpu.VMEM((tokens, vocab), jnp.bfloat16)],
        ),
    )(core, every, weight, teacher, student, student_head_t)


def pick_kernel(place_ref, ids_ref, head_ref, own_ref, send_ref, chosen):
    @pl.when(pl.program_id(0) == 0)
    def _():
        vocab, tokens = head_ref.shape[0], ids_ref.shape[1]
        entry = lax.broadcasted_iota(jnp.int32, (vocab, tokens), 0) + place_ref[1] * vocab
        place = lax.broadcasted_iota(jnp.int32, (tokens, tokens), 0)
        column = lax.broadcasted_iota(jnp.int32, (tokens, tokens), 1)
        source = (((place >> 7) ^ place_ref[0]) << 7) | ((place & 63) << 1) | ((place >> 6) & 1)
        chosen[...] = row_product(
            (column == source).astype(jnp.bfloat16), (ids_ref[...] == entry).astype(jnp.bfloat16)
        ).astype(jnp.bfloat16)

    half = own_ref.shape[0]
    out = jnp.dot(chosen[...], head_ref[...], preferred_element_type=jnp.float32)
    own_ref[...] = out[:half].astype(jnp.bfloat16)
    send_ref[...] = out[half:].astype(jnp.bfloat16)


def pick_part(place, ids, student_head_t):
    vocab, width = student_head_t.shape
    tokens, columns = ids.shape[1], 1024
    half = pl.BlockSpec((tokens // 2, columns), lambda i, p: (0, i))
    shape = shape_of((tokens // 2, width))
    return kernel_call(
        pick_kernel,
        "pick",
        [shape, shape],
        limit=56,
        grid_spec=pltpu.PrefetchScalarGridSpec(
            num_scalar_prefetch=1,
            grid=(width // columns,),
            in_specs=[
                pl.BlockSpec(ids.shape, lambda i, p: (0, 0)),
                pl.BlockSpec((vocab, columns), lambda i, p: (0, i)),
            ],
            out_specs=[half, half],
            scratch_shapes=[pltpu.VMEM((tokens, vocab), jnp.bfloat16)],
        ),
    )(place, ids, student_head_t)


def join_kernel(own_ref, came_ref, out_ref, rows):
    chips = out_ref.shape[0]
    for t in range(2):
        for i in range(SEGMENTS):
            for k in range(SEGMENT // 128):
                part = slice(t * chips, (t + 1) * chips)
                lanes = slice(i * SEGMENT + k * 128, i * SEGMENT + (k + 1) * 128)
                total = own_ref[part, lanes].astype(jnp.float32)
                total = total + came_ref[part, lanes].astype(jnp.float32)
                at = pl.ds(t * SEGMENTS + i, chips, stride=2 * SEGMENTS)
                rows[k, at, :] = total
    for k in range(SEGMENT // 128):
        out_ref[:, :, k * 128 : (k + 1) * 128] = (
            rows[k].reshape(chips, 2 * SEGMENTS, 128).astype(jnp.bfloat16)
        )


def join_part(own, send):
    chips = own.shape[0] // 2
    block = (chips, 2 * SEGMENTS, SEGMENT)
    return kernel_call(
        join_kernel,
        "join",
        shape_of(block),
        limit=10,
        in_specs=[VMEM] * 2,
        out_specs=VMEM,
        scratch_shapes=[pltpu.VMEM((SEGMENT // 128, chips * 2 * SEGMENTS, 128), jnp.float32)],
    )(own, swap_cores(send))


def block_gain(gain_ref):
    gain = gain_ref[...].astype(jnp.float32)
    lanes = SEGMENT // 128
    token = jnp.concatenate(
        [
            jnp.concatenate([gain[lanes * i + k : lanes * i + k + 1] for k in range(lanes)], axis=1)
            for i in range(SEGMENTS)
        ],
        axis=0,
    )
    return jnp.concatenate([token, token], axis=0)


def block_mean(values):
    means = []
    for t in range(2):
        part = values[t * SEGMENTS : (t + 1) * SEGMENTS]
        total = jnp.sum(jnp.sum(part, axis=0, keepdims=True), axis=1, keepdims=True)
        means.append(jnp.broadcast_to(total / (SEGMENTS * SEGMENT), (SEGMENTS, 1)))
    return jnp.concatenate(means, axis=0)


def block_inverse(values):
    return lax.rsqrt(block_mean(values * values) + eps)


def block_back(upstream, values, gain):
    inverse = block_inverse(values)
    gained = upstream * gain
    return inverse * gained - values * inverse**3 * block_mean(gained * values)


def block_sum(blocks_ref):
    return jnp.sum(blocks_ref[...].astype(jnp.float32), axis=0)


def embed_kernel(blocks_ref, gain_ref, embedded_ref, out_ref):
    values = block_sum(blocks_ref)
    embedded_ref[...] = values
    rows = (values * block_inverse(values) * block_gain(gain_ref)).astype(jnp.bfloat16)
    out_ref[...] = jnp.broadcast_to(rows[None], out_ref.shape)


def final_kernel(blocks_ref, states_ref, gain_ref, grad_ref, out_ref, states):
    for i in range(SEGMENTS):
        part = states_ref[:, i * SEGMENT : (i + 1) * SEGMENT].astype(jnp.float32)
        for t in range(2):
            states[t * SEGMENTS + i : t * SEGMENTS + i + 1, :] = part[t : t + 1]
    grad = block_back(block_sum(blocks_ref), states[...], block_gain(gain_ref))
    grad_ref[...] = grad
    out_ref[...] = jnp.broadcast_to(grad.astype(jnp.bfloat16)[None], out_ref.shape)


def state_kernel(blocks_ref, grad_ref, embedded_ref, gain_ref, out_ref):
    back = block_back(block_sum(blocks_ref), embedded_ref[...], block_gain(gain_ref))
    grad = grad_ref[...] + back
    for t in range(2):
        for i in range(SEGMENTS):
            out_ref[t : t + 1, i * SEGMENT : (i + 1) * SEGMENT] = grad[
                t * SEGMENTS + i : t * SEGMENTS + i + 1
            ]


BLOCK = (2 * SEGMENTS, SEGMENT)


def owner_part(body, name, blocks, *others, scratch=()):
    return kernel_call(
        body,
        name,
        [shape_of(BLOCK, jnp.float32), shape_of(blocks.shape)],
        in_specs=[VMEM] * (1 + len(others)),
        out_specs=[VMEM] * 2,
        scratch_shapes=list(scratch),
    )(blocks, *others)


def spread_rows(refs, scratches):
    for ref, rows in zip(refs, scratches):
        values = ref[...].astype(jnp.float32)
        values = values.reshape(values.shape[0] * values.shape[1], values.shape[2])
        for k in range(SEGMENT // 128):
            rows[k] = values[:, k * 128 : (k + 1) * 128]


def segment_rows(scratches, segment):
    parts = []
    for rows in scratches:
        chips = rows.shape[1] // (2 * SEGMENTS)
        for t in range(2):
            at = pl.ds(t * SEGMENTS + segment, chips, stride=2 * SEGMENTS)
            parts.append(
                jnp.concatenate([rows[k, at, :] for k in range(SEGMENT // 128)], axis=1)
            )
    return jnp.concatenate(parts, axis=0).astype(jnp.bfloat16)


def gate_kernel(own_ref, other_ref, gate_ref, up_ref, out_ref, *scratches):
    spread_rows((own_ref, other_ref), scratches)
    total = None
    for i in range(SEGMENTS):
        columns = slice(i * SEGMENT, (i + 1) * SEGMENT)
        weight = jnp.concatenate([gate_ref[:, columns], up_ref[:, columns]], axis=0)
        term = row_product(weight, segment_rows(scratches, i))
        total = term if total is None else total + term
    out_ref[...] = total


def ffn_grad_kernel(
    own_ref, other_ref, down_ref, hidden_ref, gate_ref, up_ref, own_out, send_out, *scratches
):
    spread_rows((own_ref, other_ref), scratches)
    units = down_ref.shape[0]
    act_grad = None
    for i in range(SEGMENTS):
        term = row_product(
            down_ref[:, i * SEGMENT : (i + 1) * SEGMENT], segment_rows(scratches, i)
        )
        act_grad = term if act_grad is None else act_grad + term
    gate, upper = hidden_ref[:units, :], hidden_ref[units:, :]
    sigmoid_gate = jax.nn.sigmoid(gate)
    gate_grad = act_grad * upper * sigmoid_gate * (1.0 + gate * (1.0 - sigmoid_gate))
    upper_grad = act_grad * gate * sigmoid_gate
    grads = jnp.concatenate([gate_grad, upper_grad], axis=0).astype(jnp.bfloat16)
    tokens = grads.shape[1]
    same = lax.broadcasted_iota(jnp.int32, (tokens, tokens), 0) == lax.broadcasted_iota(
        jnp.int32, (tokens, tokens), 1
    )
    grads = row_product(same.astype(jnp.bfloat16), grads).astype(jnp.bfloat16)
    for i in range(SEGMENTS):
        columns = slice(i * SEGMENT, (i + 1) * SEGMENT)
        weight = jnp.concatenate([gate_ref[:, columns], up_ref[:, columns]], axis=0)
        out = jnp.dot(grads, weight, preferred_element_type=jnp.float32)
        own_out[:, columns] = out[: tokens // 2]
        send_out[:, columns] = out[tokens // 2 :].astype(jnp.bfloat16)


def ffn_part(body, name, out_shape, blocks, *others):
    rows = blocks.shape[0] * blocks.shape[1]
    scratch = pltpu.VMEM((SEGMENT // 128, rows, 128), jnp.float32)
    return kernel_call(
        body,
        name,
        out_shape,
        limit=18,
        in_specs=[VMEM] * (2 + len(others)),
        out_specs=[VMEM] * len(out_shape),
        scratch_shapes=[scratch, scratch],
    )(blocks, swap_cores(blocks), *others)


def shards(
    teacher_states,
    teacher_gain,
    teacher_head,
    student_states,
    student_gain,
    student_head,
    token_ids,
    ffn_gain,
    gate_weight,
    up_weight,
    down_weight,
    token_weight,
):
    core = lax.axis_index("core")
    device = lax.axis_index(AXES)
    own_core = jnp.full((1,), core, jnp.int32)
    x, z, y = (
        jnp.full((1,), lax.axis_index(line), jnp.int32) for line in ("x", "z", ("yh", "yl"))
    )
    teacher_gain, student_gain, ffn_gain = (
        gain.reshape(-1, 128) for gain in (teacher_gain, student_gain, ffn_gain)
    )
    student_head_t, teacher_head_t = student_head.T, teacher_head.T
    heads = (student_head_t, teacher_head_t)
    gate_t, up_t = gate_weight.T, up_weight.T

    width = sum(WIDTHS)
    half_shape = shape_of((2, width))
    keep, send = kernel_call(
        rows_kernel,
        "rows",
        [half_shape, half_shape],
        limit=56,
        in_specs=[SMEM] + [ANY] * 4,
        out_specs=[VMEM] * 2,
        scratch_shapes=[
            pltpu.VMEM(teacher_states.shape, jnp.bfloat16),
            pltpu.VMEM(student_states.shape, jnp.bfloat16),
            pltpu.VMEM(teacher_gain.shape, jnp.bfloat16),
            pltpu.VMEM(student_gain.shape, jnp.bfloat16),
            pltpu.VMEM((160, 128), jnp.float32),
            pltpu.SemaphoreType.DMA((4,)),
        ],
    )(own_core, teacher_states, teacher_gain, student_states, student_gain)
    rows = kernel_call(
        chip_kernel,
        "chip",
        shape_of((4, width)),
        in_specs=[SMEM] + [VMEM] * 2,
        out_specs=VMEM,
    )(own_core, keep, swap_cores(send))
    pieces = line_pieces(rows, ("yh", "yl"))

    place = jnp.stack([core, device]).astype(jnp.int32)
    picked = join_part(*pick_part(place, token_ids.reshape(1, 256), student_head_t))
    pieces, picked = lax.optimization_barrier((pieces, picked))
    picked = exchange(picked, CHIPS)

    first, second = kernel_call(
        line_kernel,
        "line",
        [shape_of((16, w)) for w in WIDTHS],
        in_specs=[SMEM] + [VMEM] * 4,
        out_specs=[VMEM] * 2,
    )(y, *pieces)
    first, second = line_pieces(first, "z"), line_pieces(second, "x")
    first, second, picked = lax.optimization_barrier((first, second, picked))
    embedded, ffn_rows = owner_part(embed_kernel, "embed", picked, ffn_gain)
    ffn_rows = exchange(ffn_rows, CHIPS)
    first, second = in_line_order(z, first), in_line_order(x, second)
    first, second = line_pieces(first, "x"), line_pieces(second, "z")
    first, second, ffn_rows = lax.optimization_barrier((first, second, ffn_rows))
    rows = (in_line_order(x, first), in_line_order(z, second))
    others = tuple(swap_cores(part) for part in rows)
    sums = logits_part(own_core, rows, heads)
    student, teacher, stats = logits_part(1 - own_core, others, heads, sums)
    every = exchange(jnp.broadcast_to(stats[None], (128,) + stats.shape), AXES)

    weight = token_weight.reshape(2, 4, 2, 4, 2, 2).transpose(1, 3, 2, 4, 0, 5).reshape(1, 256)
    own, send, divergence = row_grad_part(
        own_core, every, weight, teacher, student, student_head_t
    )
    divergence = divergence.reshape(4, 4, 2, 2, 2, 2).transpose(4, 0, 2, 1, 3, 5).reshape(256)
    row_grad = join_part(own, send)
    (hidden,) = ffn_part(
        gate_kernel, "gate_upper", [shape_of((224, 256), jnp.float32)], ffn_rows, gate_t, up_t
    )
    row_grad, hidden = lax.optimization_barrier((row_grad, hidden))
    row_grad = exchange(row_grad, CHIPS)
    final_grad, final_half = owner_part(
        final_kernel,
        "final",
        row_grad,
        student_states,
        student_gain,
        scratch=[pltpu.VMEM(BLOCK, jnp.float32)],
    )
    final_half = exchange(final_half, CHIPS)
    shape = (128, 4096)
    own, send = ffn_part(
        ffn_grad_kernel,
        "ffn_grad",
        [shape_of(shape, jnp.float32), shape_of(shape)],
        final_half,
        down_weight,
        hidden,
        gate_t,
        up_t,
    )
    ffn_grad = exchange(join_part(own, send), CHIPS)
    state_grad = kernel_call(
        state_kernel,
        "state",
        shape_of((2, 4096), jnp.float32),
        in_specs=[VMEM] * 4,
        out_specs=VMEM,
    )(ffn_grad, final_grad, embedded, ffn_gain)
    return (divergence, state_grad)


def solution(mesh):
    fine = Mesh(mesh.devices.reshape(SHAPE), AXES)
    in_specs = (
        P(AXES, None),
        P(),
        P(None, AXES),
        P(AXES, None),
        P(),
        P(None, AXES),
        P(),
        P(),
        P(None, AXES),
        P(None, AXES),
        P(AXES, None),
        P(),
    )
    out_specs = (P(), P(AXES, None))
    return jax.shard_map(shards, mesh=fine, in_specs=in_specs, out_specs=out_specs, check_vma=False)
```

```python
import functools

import jax
import jax.numpy as jnp
from jax import lax
from jax.experimental import pallas as pl
from jax.experimental.pallas import tpu as pltpu
from jax.sharding import Mesh
from jax.sharding import PartitionSpec as P

eps = 1e-05
SHAPE = (2, 4, 2, 4, 2)
AXES = ("core", "x", "yh", "z", "yl")
CHIPS = AXES[1:]
MIB = 1024 * 1024

VMEM = pl.BlockSpec(memory_space=pltpu.VMEM)
SMEM = pl.BlockSpec(memory_space=pltpu.SMEM)
ANY = pl.BlockSpec(memory_space=pl.ANY)
SEGMENTS = 8
SEGMENT = 512


def kernel_call(body, name, out_shape, limit=8, **options):
    return pl.pallas_call(
        body,
        name=name,
        out_shape=out_shape,
        compiler_params=pltpu.CompilerParams(vmem_limit_bytes=limit * MIB),
        cost_estimate=pl.CostEstimate(flops=1, bytes_accessed=1, transcendentals=0),
        **options,
    )


def shape_of(shape, dtype=jnp.bfloat16):
    return jax.ShapeDtypeStruct(shape, dtype)


def row_product(left, right):
    return lax.dot_general(
        left, right, (((1,), (1,)), ((), ())), preferred_element_type=jnp.float32
    )


def swap_cores(values):
    return lax.ppermute(values, "core", [(0, 1), (1, 0)])


def line_pieces(block, line):
    return [block] + [lax.ppermute(block, line, [(i, i ^ m) for i in range(4)]) for m in (1, 2, 3)]


def exchange(blocks, axes):
    return lax.all_to_all(blocks, axes, split_axis=0, concat_axis=0, tiled=True)


def rows_kernel(
    core_ref, teacher_from, teacher_gain, student_from, student_gain, keep_ref, send_ref,
    teacher_ref, student_ref, teacher_gains, student_gains, gains, sems,
):
    copies = [
        pltpu.make_async_copy(source, target, sems.at[i])
        for i, (source, target) in enumerate(
            (
                (student_gain, student_gains),
                (student_from, student_ref),
                (teacher_gain, teacher_gains),
                (teacher_from, teacher_ref),
            )
        )
    ]
    for copy in copies:
        copy.start()
    for copy in copies:
        copy.wait()
    first = student_gain.shape[0]
    gains[:first, :] = student_gains[...].astype(jnp.float32)
    gains[first:, :] = teacher_gains[...].astype(jnp.float32)
    column = 0
    for values, base in ((student_ref, 0), (teacher_ref, first)):
        half = values.shape[1] // 2
        every = values[...].astype(jnp.float32)
        inverse = lax.rsqrt(jnp.mean(every * every, axis=-1, keepdims=True) + eps)
        for part, out in ((core_ref[0], keep_ref), (1 - core_ref[0], send_ref)):
            for k in range(half // 128):
                place = pl.ds(pl.multiple_of(part * half + k * 128, 128), 128)
                rows = values[:, place].astype(jnp.float32) * inverse
                rows = rows * gains[pl.ds(base + part * (half // 128) + k, 1), :]
                out[:, column + k * 128 : column + (k + 1) * 128] = rows.astype(jnp.bfloat16)
        column = column + half


def chip_kernel(core_ref, keep_ref, came_ref, out_ref):
    keep, came = keep_ref[...].astype(jnp.float32), came_ref[...].astype(jnp.float32)
    first = core_ref[0] == 0
    rows = jnp.concatenate([jnp.where(first, keep, came), jnp.where(first, came, keep)], axis=0)
    out_ref[...] = rows.astype(jnp.bfloat16)


def line_kernel(place_ref, *refs):
    pieces = [ref[...].astype(jnp.float32) for ref in refs[:4]]
    rows = []
    for j in range(4):
        m = place_ref[0] ^ j
        low = jnp.where(m == 0, pieces[0], pieces[1])
        high = jnp.where(m == 2, pieces[2], pieces[3])
        rows.append(jnp.where(m < 2, low, high))
    rows = jnp.concatenate(rows, axis=0).astype(jnp.bfloat16)
    column = 0
    for out in refs[4:]:
        out[...] = rows[:, column : column + out.shape[1]]
        column = column + out.shape[1]


def plane_kernel(place_ref, *refs):
    pieces, out, sems = refs[:4], refs[4], refs[5]
    copies = []
    for m, piece in enumerate(pieces):
        tokens = piece.shape[0]
        at = pl.multiple_of((place_ref[0] ^ m) * tokens, tokens)
        copy = pltpu.make_async_copy(piece, out.at[pl.ds(at, tokens), :], sems.at[m])
        copy.start()
        copies.append(copy)
    for copy in copies:
        copy.wait()


def in_line_order(place, pieces):
    tokens, width = pieces[0].shape
    return kernel_call(
        plane_kernel,
        "plane",
        shape_of((4 * tokens, width)),
        limit=2,
        in_specs=[SMEM] + [ANY] * 4,
        out_specs=ANY,
        scratch_shapes=[pltpu.SemaphoreType.DMA((4,))],
    )(place, *pieces)


def halves_kernel(*refs):
    count = (len(refs) - 1) // 2
    copies = []
    for i, (piece, out) in enumerate(zip(refs[:count], refs[count:])):
        rows = out.shape[0]
        copy = pltpu.make_async_copy(piece.at[pl.ds((i % 2) * rows, rows), :], out, refs[-1].at[i])
        copy.start()
        copies.append(copy)
    for copy in copies:
        copy.wait()


def halves_of(pieces):
    return kernel_call(
        halves_kernel,
        "halves",
        [shape_of((p.shape[0] // 2, p.shape[1])) for p in pieces],
        limit=2,
        in_specs=[ANY] * len(pieces),
        out_specs=[ANY] * len(pieces),
        scratch_shapes=[pltpu.SemaphoreType.DMA((len(pieces),))],
    )(*pieces)


def along(block, line, mask):
    return lax.ppermute(block, line, [(i, i ^ mask) for i in range(4)])


def whole_kernel(place_ref, *refs):
    pieces, out, sems = refs[:5], refs[5], refs[6]
    tokens = pieces[0].shape[0]
    copies = []
    for i, (mask, half) in enumerate(((0, 0), (1, 0), (3, 0), (2, 0), (2, 1))):
        at = (place_ref[0] ^ mask) * tokens + half * (tokens // 2)
        at = pl.multiple_of(at, tokens // 2)
        rows = pieces[i].shape[0]
        copy = pltpu.make_async_copy(pieces[i], out.at[pl.ds(at, rows), :], sems.at[i])
        copy.start()
        copies.append(copy)
    for copy in copies:
        copy.wait()


def whole_rows(place, pieces):
    tokens, width = pieces[0].shape
    return kernel_call(
        whole_kernel,
        "whole",
        shape_of((4 * tokens, width)),
        limit=2,
        in_specs=[SMEM] + [ANY] * 5,
        out_specs=ANY,
        scratch_shapes=[pltpu.SemaphoreType.DMA((5,))],
    )(place, *pieces)


GROUPS = (
    tuple((0, i * 1024, 1024) for i in range(2)) + tuple((1, i * 1024, 1024) for i in range(3)),
    tuple((1, i * 1024, 1024) for i in range(3, 8)),
)
WIDTHS = tuple(sum(p[2] for p in group) for group in GROUPS)


def reordered(values):
    source = lax.broadcasted_iota(jnp.int32, (256, 256), 0)
    place = lax.broadcasted_iota(jnp.int32, (256, 256), 1)
    wanted = (((place >> 4) & 3) << 6) | (((place >> 6) & 3) << 4) | (place & 15)
    moves = (source == wanted).astype(jnp.bfloat16)
    high = values.astype(jnp.bfloat16)
    rest = values - high.astype(jnp.float32)
    middle = rest.astype(jnp.bfloat16)
    low = (rest - middle.astype(jnp.float32)).astype(jnp.bfloat16)
    high, middle, low = (
        jnp.dot(part, moves, preferred_element_type=jnp.float32) for part in (high, middle, low)
    )
    return (high + middle) + low


def softmax_stats(teacher, student, stats_out):
    teacher_peak = jnp.max(teacher, axis=0, keepdims=True)
    student_peak = jnp.max(student, axis=0, keepdims=True)
    teacher_exp = jnp.exp(teacher - teacher_peak)
    teacher_total = jnp.sum(teacher_exp, axis=0, keepdims=True)
    student_total = jnp.sum(jnp.exp(student - student_peak), axis=0, keepdims=True)
    cross = jnp.sum(teacher_exp * (teacher - student), axis=0, keepdims=True)
    stats = (
        teacher_peak + jnp.log(teacher_total),
        student_peak + jnp.log(student_total),
        cross / teacher_total,
    )
    rows = [row[:, :128] for row in stats] + [row[:, 128:] for row in stats]
    rows = jnp.concatenate(rows + [jnp.zeros((2, 128), jnp.float32)], axis=0)
    stats_out[...] = jnp.broadcast_to(rows[None], stats_out.shape)


def logits_kernel(last, place_ref, *refs):
    rows_from, heads, refs = refs[:2], refs[2:4], refs[4:]
    rows, head, row_sems, head_sems = refs[-4:]
    refs = refs[:-4]
    copies = []
    column = 0
    for group, source in zip(GROUPS, rows_from):
        base = column
        for kind, start, width in group:
            i = len(copies)
            columns = slice(column, column + width)
            size = heads[kind].shape[1] // 2
            start = pl.multiple_of(place_ref[0] * size + start, 128)
            pair = (
                pltpu.make_async_copy(
                    source.at[:, column - base : column - base + width],
                    rows.at[:, columns],
                    row_sems.at[i],
                ),
                pltpu.make_async_copy(
                    heads[kind].at[:, pl.ds(start, width)], head.at[:, columns], head_sems.at[i]
                ),
            )
            copies.append((kind + (base > 0), columns, pair))
            column = column + width
    ahead = 3
    for _, _, pair in copies[:ahead]:
        for copy in pair:
            copy.start()
    sums = [None, None, None]
    for i, (kind, columns, pair) in enumerate(copies):
        for copy in pair:
            copy.wait()
        if i + ahead < len(copies):
            for copy in copies[i + ahead][2]:
                copy.start()
        term = row_product(head[:, columns], rows[:, columns])
        sums[kind] = term if sums[kind] is None else sums[kind] + term
    if last:
        came, (student_out, teacher_out, stats_out) = refs[:3], refs[3:]
        student, teacher, second = (total + ref[...] for total, ref in zip(sums, came))
        teacher = teacher + reordered(second)
        student_out[...] = student
        teacher_out[...] = teacher
        softmax_stats(teacher, student, stats_out)
    else:
        for total, out in zip(sums, refs):
            out[...] = total


def logits_part(place, rows, heads, sums=()):
    vocab, tokens = heads[1].shape[0], rows[0].shape[0]
    shape = shape_of((vocab, tokens), jnp.float32)
    last = len(sums) > 0
    pieces = sum(len(group) for group in GROUPS)
    out_shape = [shape, shape, shape_of((128, 8, 128), jnp.float32) if last else shape]
    return kernel_call(
        functools.partial(logits_kernel, last),
        "logits",
        out_shape,
        limit=48,
        in_specs=[SMEM] + [ANY] * 4 + [VMEM] * len(sums),
        out_specs=[VMEM] * 3,
        scratch_shapes=[
            pltpu.VMEM((tokens, sum(WIDTHS)), jnp.bfloat16),
            pltpu.VMEM((vocab, sum(WIDTHS)), jnp.bfloat16),
            pltpu.SemaphoreType.DMA((pieces,)),
            pltpu.SemaphoreType.DMA((pieces,)),
        ],
    )(place, *rows, *heads, *sums)


def one_hot_rows(core):
    place = lax.broadcasted_iota(jnp.int32, (256, 256), 0)
    column = lax.broadcasted_iota(jnp.int32, (256, 256), 1)
    x, yh, z, yl = (place >> 4) & 3, (place >> 3) & 1, (place >> 1) & 3, place & 1
    source = (x << 6) | (z << 4) | (yh << 3) | (yl << 2)
    source = source | (((place >> 7) ^ core) << 1) | ((place >> 6) & 1)
    return (column == source).astype(jnp.bfloat16)


def head_copies(source, head, sems):
    columns = head.shape[1] // sems.shape[0]
    parts = [slice(i * columns, (i + 1) * columns) for i in range(sems.shape[0])]
    copies = [
        pltpu.make_async_copy(source.at[:, part], head.at[:, part], sems.at[i])
        for i, part in enumerate(parts)
    ]
    for copy in copies:
        copy.start()
    return list(zip(parts, copies))


def row_grad_kernel(
    core_ref, every_ref, weight_ref, teacher_ref, student_ref, head_from,
    own_ref, send_ref, divergence_ref, head, sems,
):
    copies = head_copies(head_from, head, sems)
    every = every_ref[...]
    peak = jnp.max(every, axis=0)
    scaled = jnp.exp(every - peak[None])
    total = jnp.sum(scaled, axis=0)
    lse = peak + jnp.log(total)
    cross = jnp.sum(scaled * pltpu.roll(every, 6, 1), axis=0) / total
    teacher_lse = jnp.concatenate([lse[0:1], lse[3:4]], axis=1)
    student_lse = jnp.concatenate([lse[1:2], lse[4:5]], axis=1)
    divergence_ref[...] = (
        jnp.concatenate([cross[0:1], cross[3:4]], axis=1) - teacher_lse + student_lse
    )
    logit_grad = weight_ref[...] * (
        jnp.exp(student_ref[...] - student_lse) - jnp.exp(teacher_ref[...] - teacher_lse)
    )
    grad = row_product(one_hot_rows(core_ref[0]), logit_grad.astype(jnp.bfloat16))
    grad = grad.astype(jnp.bfloat16)
    half = own_ref.shape[0]
    for columns, copy in copies:
        copy.wait()
        out = jnp.dot(grad, head[:, columns], preferred_element_type=jnp.float32)
        own_ref[:, columns] = out[:half]
        send_ref[:, columns] = out[half:].astype(jnp.bfloat16)


def row_grad_part(core, every, weight, teacher, student, student_head_t):
    vocab, width = student_head_t.shape
    tokens = weight.shape[1]
    return kernel_call(
        row_grad_kernel,
        "row_grad",
        [
            shape_of((tokens // 2, width), jnp.float32),
            shape_of((tokens // 2, width)),
            shape_of((1, tokens), jnp.float32),
        ],
        limit=48,
        in_specs=[SMEM] + [VMEM] * 4 + [ANY],
        out_specs=[VMEM] * 3,
        scratch_shapes=[
            pltpu.VMEM((vocab, width), jnp.bfloat16),
            pltpu.SemaphoreType.DMA((4,)),
        ],
    )(core, every, weight, teacher, student, student_head_t)


def pick_kernel(place_ref, ids_ref, head_from, own_ref, send_ref, head, sems):
    copies = head_copies(head_from, head, sems)
    vocab, tokens = head.shape[0], ids_ref.shape[1]
    entry = lax.broadcasted_iota(jnp.int32, (vocab, tokens), 0) + place_ref[1] * vocab
    place = lax.broadcasted_iota(jnp.int32, (tokens, tokens), 0)
    column = lax.broadcasted_iota(jnp.int32, (tokens, tokens), 1)
    source = (((place >> 7) ^ place_ref[0]) << 7) | ((place & 63) << 1) | ((place >> 6) & 1)
    chosen = row_product(
        (column == source).astype(jnp.bfloat16), (ids_ref[...] == entry).astype(jnp.bfloat16)
    ).astype(jnp.bfloat16)
    half = own_ref.shape[0]
    for columns, copy in copies:
        copy.wait()
        out = jnp.dot(chosen, head[:, columns], preferred_element_type=jnp.float32)
        own_ref[:, columns] = out[:half].astype(jnp.bfloat16)
        send_ref[:, columns] = out[half:].astype(jnp.bfloat16)


def pick_part(place, ids, student_head_t):
    vocab, width = student_head_t.shape
    shape = shape_of((ids.shape[1] // 2, width))
    return kernel_call(
        pick_kernel,
        "pick",
        [shape, shape],
        limit=48,
        in_specs=[SMEM, VMEM, ANY],
        out_specs=[VMEM] * 2,
        scratch_shapes=[
            pltpu.VMEM((vocab, width), jnp.bfloat16),
            pltpu.SemaphoreType.DMA((4,)),
        ],
    )(place, ids, student_head_t)


def join_kernel(*refs):
    pairs, out_ref, rows = refs[:-2], refs[-2], refs[-1]
    chips, height = out_ref.shape[0], 2 * SEGMENTS
    for base, (own_ref, came_ref) in enumerate(zip(pairs[::2], pairs[1::2])):
        for t in range(2):
            for i in range(SEGMENTS):
                for k in range(SEGMENT // 128):
                    part = slice(t * chips, (t + 1) * chips)
                    lanes = slice(i * SEGMENT + k * 128, i * SEGMENT + (k + 1) * 128)
                    total = own_ref[part, lanes].astype(jnp.float32)
                    total = total + came_ref[part, lanes].astype(jnp.float32)
                    at = pl.ds(t * SEGMENTS + i, chips, stride=height)
                    rows[k, at, :] = total
        for k in range(SEGMENT // 128):
            out_ref[:, base * height : (base + 1) * height, k * 128 : (k + 1) * 128] = (
                rows[k].reshape(chips, height, 128).astype(jnp.bfloat16)
            )


def join_part(*pairs):
    chips = pairs[0].shape[0] // 2
    height = 2 * SEGMENTS
    return kernel_call(
        join_kernel,
        "join",
        shape_of((chips, height * len(pairs) // 2, SEGMENT)),
        limit=14,
        in_specs=[VMEM] * len(pairs),
        out_specs=VMEM,
        scratch_shapes=[pltpu.VMEM((SEGMENT // 128, chips * height, 128), jnp.float32)],
    )(*pairs)


def block_gain(gain_ref):
    gain = gain_ref[...].astype(jnp.float32)
    lanes = SEGMENT // 128
    token = jnp.concatenate(
        [
            jnp.concatenate([gain[lanes * i + k : lanes * i + k + 1] for k in range(lanes)], axis=1)
            for i in range(SEGMENTS)
        ],
        axis=0,
    )
    return jnp.concatenate([token, token], axis=0)


def block_mean(values):
    means = []
    for t in range(2):
        part = values[t * SEGMENTS : (t + 1) * SEGMENTS]
        total = jnp.sum(jnp.sum(part, axis=0, keepdims=True), axis=1, keepdims=True)
        means.append(jnp.broadcast_to(total / (SEGMENTS * SEGMENT), (SEGMENTS, 1)))
    return jnp.concatenate(means, axis=0)


def block_inverse(values):
    return lax.rsqrt(block_mean(values * values) + eps)


def block_back(upstream, values, gain):
    inverse = block_inverse(values)
    gained = upstream * gain
    return inverse * gained - values * inverse**3 * block_mean(gained * values)


def block_sum(blocks_ref):
    return jnp.sum(blocks_ref[...].astype(jnp.float32), axis=0)


def final_kernel(
    blocks_ref, states_ref, student_gain, ffn_gain, grad_ref, embedded_ref, out_ref, states
):
    height = 2 * SEGMENTS
    total = block_sum(blocks_ref)
    embedded = total[height:]
    embedded_ref[...] = embedded
    rows = embedded * block_inverse(embedded) * block_gain(ffn_gain)
    for i in range(SEGMENTS):
        part = states_ref[:, i * SEGMENT : (i + 1) * SEGMENT].astype(jnp.float32)
        for t in range(2):
            states[t * SEGMENTS + i : t * SEGMENTS + i + 1, :] = part[t : t + 1]
    grad = block_back(total[:height], states[...], block_gain(student_gain))
    grad_ref[...] = grad
    rows = jnp.concatenate([grad, rows], axis=0).astype(jnp.bfloat16)
    out_ref[...] = jnp.broadcast_to(rows[None], out_ref.shape)


def state_kernel(blocks_ref, grad_ref, embedded_ref, gain_ref, out_ref):
    back = block_back(block_sum(blocks_ref), embedded_ref[...], block_gain(gain_ref))
    grad = grad_ref[...] + back
    for t in range(2):
        for i in range(SEGMENTS):
            out_ref[t : t + 1, i * SEGMENT : (i + 1) * SEGMENT] = grad[
                t * SEGMENTS + i : t * SEGMENTS + i + 1
            ]


BLOCK = (2 * SEGMENTS, SEGMENT)


def spread_rows(refs, scratches):
    for ref, rows in zip(refs, scratches):
        values = ref[...].astype(jnp.float32)
        values = values.reshape(values.shape[0] * values.shape[1], values.shape[2])
        for k in range(SEGMENT // 128):
            rows[k] = values[:, k * 128 : (k + 1) * 128]


def segment_rows(scratches, first):
    parts = []
    for rows in scratches:
        height = 4 * SEGMENTS
        for t in range(2):
            at = pl.ds(first + t * SEGMENTS, rows.shape[1] // height, stride=height)
            parts.append(
                jnp.concatenate([rows[k, at, :] for k in range(SEGMENT // 128)], axis=1)
            )
    return jnp.concatenate(parts, axis=0).astype(jnp.bfloat16)


def ffn_grad_kernel(
    own_ref, other_ref, down_ref, gate_ref, up_ref, own_out, send_out, *scratches
):
    spread_rows((own_ref, other_ref), scratches)
    units = down_ref.shape[0]
    hidden, act_grad = None, None
    for i in range(SEGMENTS):
        columns = slice(i * SEGMENT, (i + 1) * SEGMENT)
        weight = jnp.concatenate([gate_ref[:, columns], up_ref[:, columns]], axis=0)
        term = row_product(weight, segment_rows(scratches, 2 * SEGMENTS + i))
        hidden = term if hidden is None else hidden + term
        term = row_product(down_ref[:, columns], segment_rows(scratches, i))
        act_grad = term if act_grad is None else act_grad + term
    gate, upper = hidden[:units, :], hidden[units:, :]
    sigmoid_gate = jax.nn.sigmoid(gate)
    gate_grad = act_grad * upper * sigmoid_gate * (1.0 + gate * (1.0 - sigmoid_gate))
    upper_grad = act_grad * gate * sigmoid_gate
    grads = jnp.concatenate([gate_grad, upper_grad], axis=0).astype(jnp.bfloat16)
    tokens = grads.shape[1]
    same = lax.broadcasted_iota(jnp.int32, (tokens, tokens), 0) == lax.broadcasted_iota(
        jnp.int32, (tokens, tokens), 1
    )
    grads = row_product(same.astype(jnp.bfloat16), grads).astype(jnp.bfloat16)
    for i in range(SEGMENTS):
        columns = slice(i * SEGMENT, (i + 1) * SEGMENT)
        weight = jnp.concatenate([gate_ref[:, columns], up_ref[:, columns]], axis=0)
        out = jnp.dot(grads, weight, preferred_element_type=jnp.float32)
        own_out[:, columns] = out[: tokens // 2]
        send_out[:, columns] = out[tokens // 2 :].astype(jnp.bfloat16)


def ffn_part(body, name, out_shape, blocks, *others):
    rows = blocks.shape[0] * blocks.shape[1]
    scratch = pltpu.VMEM((SEGMENT // 128, rows, 128), jnp.float32)
    return kernel_call(
        body,
        name,
        out_shape,
        limit=30,
        in_specs=[VMEM] * (2 + len(others)),
        out_specs=[VMEM] * len(out_shape),
        scratch_shapes=[scratch, scratch],
    )(blocks, swap_cores(blocks), *others)


def shards(
    teacher_states,
    teacher_gain,
    teacher_head,
    student_states,
    student_gain,
    student_head,
    token_ids,
    ffn_gain,
    gate_weight,
    up_weight,
    down_weight,
    token_weight,
):
    core = lax.axis_index("core")
    device = lax.axis_index(AXES)
    own_core = jnp.full((1,), core, jnp.int32)
    x, z, y = (
        jnp.full((1,), lax.axis_index(line), jnp.int32) for line in ("x", "z", ("yh", "yl"))
    )
    teacher_gain, student_gain, ffn_gain = (
        gain.reshape(-1, 128) for gain in (teacher_gain, student_gain, ffn_gain)
    )
    student_head_t, teacher_head_t = student_head.T, teacher_head.T
    heads = (student_head_t, teacher_head_t)
    gate_t, up_t = gate_weight.T, up_weight.T

    width = sum(WIDTHS)
    half_shape = shape_of((2, width))
    keep, send = kernel_call(
        rows_kernel,
        "rows",
        [half_shape, half_shape],
        limit=56,
        in_specs=[SMEM] + [ANY] * 4,
        out_specs=[VMEM] * 2,
        scratch_shapes=[
            pltpu.VMEM(teacher_states.shape, jnp.bfloat16),
            pltpu.VMEM(student_states.shape, jnp.bfloat16),
            pltpu.VMEM(teacher_gain.shape, jnp.bfloat16),
            pltpu.VMEM(student_gain.shape, jnp.bfloat16),
            pltpu.VMEM((160, 128), jnp.float32),
            pltpu.SemaphoreType.DMA((4,)),
        ],
    )(own_core, teacher_states, teacher_gain, student_states, student_gain)
    rows = kernel_call(
        chip_kernel,
        "chip",
        shape_of((4, width)),
        in_specs=[SMEM] + [VMEM] * 2,
        out_specs=VMEM,
    )(own_core, keep, swap_cores(send))
    pieces = line_pieces(rows, ("yh", "yl"))
    place = jnp.stack([core, device]).astype(jnp.int32)
    picked = pick_part(place, token_ids.reshape(1, 256), student_head_t)
    pieces, picked = lax.optimization_barrier((pieces, picked))
    picked = (picked[0], swap_cores(picked[1]))
    first, second = kernel_call(
        line_kernel,
        "line",
        [shape_of((16, w)) for w in WIDTHS],
        in_specs=[SMEM] + [VMEM] * 4,
        out_specs=[VMEM] * 2,
    )(y, *pieces)
    first, second = line_pieces(first, "z"), line_pieces(second, "x")
    first, second, picked = lax.optimization_barrier((first, second, picked))
    first, second = in_line_order(z, first), in_line_order(x, second)
    came = [along(first, "x", 1), along(first, "x", 3), along(second, "z", 1), along(second, "z", 3)]
    came = lax.optimization_barrier(came)
    halves = halves_of(came)
    far = [
        along(half, line, mask)
        for half, line, mask in zip(halves, ("x", "x", "z", "z"), (3, 1, 3, 1))
    ]
    far = lax.optimization_barrier(far)
    rows = (
        whole_rows(x, [first] + came[:2] + far[:2]),
        whole_rows(z, [second] + came[2:] + far[2:]),
    )
    others = tuple(swap_cores(part) for part in rows)
    sums = logits_part(own_core, rows, heads)
    student, teacher, stats = logits_part(1 - own_core, others, heads, sums)
    every = exchange(stats, AXES)

    weight = token_weight.reshape(2, 4, 2, 4, 2, 2).transpose(1, 3, 2, 4, 0, 5).reshape(1, 256)
    own, send, divergence = row_grad_part(
        own_core, every, weight, teacher, student, student_head_t
    )
    divergence = divergence.reshape(4, 4, 2, 2, 2, 2).transpose(4, 0, 2, 1, 3, 5).reshape(256)
    blocks = exchange(join_part(own, swap_cores(send), *picked), CHIPS)
    final_grad, embedded, blocks = kernel_call(
        final_kernel,
        "final",
        [shape_of(BLOCK, jnp.float32), shape_of(BLOCK, jnp.float32), shape_of(blocks.shape)],
        limit=14,
        in_specs=[VMEM] * 4,
        out_specs=[VMEM] * 3,
        scratch_shapes=[pltpu.VMEM(BLOCK, jnp.float32)],
    )(blocks, student_states, student_gain, ffn_gain)
    blocks = exchange(blocks, CHIPS)
    shape = (128, 4096)
    own, send = ffn_part(
        ffn_grad_kernel,
        "ffn_grad",
        [shape_of(shape, jnp.float32), shape_of(shape)],
        blocks,
        down_weight,
        gate_t,
        up_t,
    )
    ffn_grad = exchange(join_part(own, swap_cores(send)), CHIPS)
    state_grad = kernel_call(
        state_kernel,
        "state",
        shape_of((2, 4096), jnp.float32),
        in_specs=[VMEM] * 4,
        out_specs=VMEM,
    )(ffn_grad, final_grad, embedded, ffn_gain)
    return (divergence, state_grad)


def solution(mesh):
    fine = Mesh(mesh.devices.reshape(SHAPE), AXES)
    in_specs = (
        P(AXES, None),
        P(),
        P(None, AXES),
        P(AXES, None),
        P(),
        P(None, AXES),
        P(),
        P(),
        P(None, AXES),
        P(None, AXES),
        P(AXES, None),
        P(),
    )
    out_specs = (P(), P(AXES, None))
    return jax.shard_map(shards, mesh=fine, in_specs=in_specs, out_specs=out_specs, check_vma=False)
```

```python
import functools

import jax
import jax.numpy as jnp
from jax import lax
from jax.experimental import pallas as pl
from jax.experimental.pallas import tpu as pltpu
from jax.sharding import Mesh
from jax.sharding import PartitionSpec as P

eps = 1e-05
SHAPE = (2, 4, 2, 4, 2)
AXES = ("core", "x", "yh", "z", "yl")
CHIPS = AXES[1:]
MIB = 1024 * 1024

VMEM = pl.BlockSpec(memory_space=pltpu.VMEM)
SMEM = pl.BlockSpec(memory_space=pltpu.SMEM)
ANY = pl.BlockSpec(memory_space=pl.ANY)
SEGMENTS = 8
SEGMENT = 512


def kernel_call(body, name, out_shape, limit=8, **options):
    return pl.pallas_call(
        body,
        name=name,
        out_shape=out_shape,
        compiler_params=pltpu.CompilerParams(vmem_limit_bytes=limit * MIB),
        cost_estimate=pl.CostEstimate(flops=1, bytes_accessed=1, transcendentals=0),
        **options,
    )


def shape_of(shape, dtype=jnp.bfloat16):
    return jax.ShapeDtypeStruct(shape, dtype)


def row_product(left, right):
    return lax.dot_general(
        left, right, (((1,), (1,)), ((), ())), preferred_element_type=jnp.float32
    )


def swap_cores(values):
    return lax.ppermute(values, "core", [(0, 1), (1, 0)])


def exchange(blocks, axes):
    return lax.all_to_all(blocks, axes, split_axis=0, concat_axis=0, tiled=True)


def rows_kernel(
    core_ref, teacher_from, teacher_gain, student_from, student_gain, keep_ref, send_ref,
    teacher_ref, student_ref, teacher_gains, student_gains, gains, sems,
):
    copies = [
        pltpu.make_async_copy(source, target, sems.at[i])
        for i, (source, target) in enumerate(
            (
                (student_gain, student_gains),
                (student_from, student_ref),
                (teacher_gain, teacher_gains),
                (teacher_from, teacher_ref),
            )
        )
    ]
    for copy in copies:
        copy.start()
    for copy in copies:
        copy.wait()
    first = student_gain.shape[0]
    gains[:first, :] = student_gains[...].astype(jnp.float32)
    gains[first:, :] = teacher_gains[...].astype(jnp.float32)
    column = 0
    for values, base in ((student_ref, 0), (teacher_ref, first)):
        half = values.shape[1] // 2
        every = values[...].astype(jnp.float32)
        inverse = lax.rsqrt(jnp.mean(every * every, axis=-1, keepdims=True) + eps)
        for part, out in ((core_ref[0], keep_ref), (1 - core_ref[0], send_ref)):
            for k in range(half // 128):
                place = pl.ds(pl.multiple_of(part * half + k * 128, 128), 128)
                rows = values[:, place].astype(jnp.float32) * inverse
                rows = rows * gains[pl.ds(base + part * (half // 128) + k, 1), :]
                out[:, column + k * 128 : column + (k + 1) * 128] = rows.astype(jnp.bfloat16)
        column = column + half


def pair_kernel(place_ref, own_ref, came_ref, *out_refs):
    own, came = own_ref[...].astype(jnp.float32), came_ref[...].astype(jnp.float32)
    first = place_ref[0] == 0
    rows = jnp.concatenate([jnp.where(first, own, came), jnp.where(first, came, own)], axis=0)
    rows = rows.astype(jnp.bfloat16)
    column = 0
    for out in out_refs:
        out[...] = rows[:, column : column + out.shape[1]]
        column = column + out.shape[1]


def in_pair(bit, own, came, widths):
    tokens = 2 * own.shape[0]
    return kernel_call(
        pair_kernel,
        "pair",
        [shape_of((tokens, w)) for w in widths],
        in_specs=[SMEM] + [VMEM] * 2,
        out_specs=[VMEM] * len(widths),
    )(bit, own, came)


def groups_kernel(place_ref, *refs):
    count = (len(refs) - 1) // 3
    sources, outs, sems = refs[: 2 * count], refs[2 * count : -1], refs[-1]
    copies = []
    for g, out in enumerate(outs):
        for i in range(2):
            source = sources[2 * g + i]
            tokens = source.shape[0]
            at = pl.multiple_of((place_ref[g] ^ i) * tokens, tokens)
            copy = pltpu.make_async_copy(source, out.at[pl.ds(at, tokens), :], sems.at[2 * g + i])
            copy.start()
            copies.append(copy)
    for copy in copies:
        copy.wait()


def in_pairs(bits, parts):
    tokens = 2 * parts[0].shape[0]
    return kernel_call(
        groups_kernel,
        "pairs",
        [shape_of((tokens, part.shape[1])) for part in parts[::2]],
        limit=2,
        in_specs=[SMEM] + [ANY] * len(parts),
        out_specs=[ANY] * (len(parts) // 2),
        scratch_shapes=[pltpu.SemaphoreType.DMA((len(parts),))],
    )(bits, *parts)


def halves_kernel(*refs):
    count = (len(refs) - 1) // 2
    copies = []
    for i, (piece, out) in enumerate(zip(refs[:count], refs[count:])):
        rows = out.shape[0]
        copy = pltpu.make_async_copy(piece.at[pl.ds((i % 2) * rows, rows), :], out, refs[-1].at[i])
        copy.start()
        copies.append(copy)
    for copy in copies:
        copy.wait()


def halves_of(pieces):
    return kernel_call(
        halves_kernel,
        "halves",
        [shape_of((p.shape[0] // 2, p.shape[1])) for p in pieces],
        limit=2,
        in_specs=[ANY] * len(pieces),
        out_specs=[ANY] * len(pieces),
        scratch_shapes=[pltpu.SemaphoreType.DMA((len(pieces),))],
    )(*pieces)


def along(block, line, mask):
    return lax.ppermute(block, line, [(i, i ^ mask) for i in range(4)])


def whole_kernel(place_ref, *refs):
    pieces, out, sems = refs[:5], refs[5], refs[6]
    tokens = pieces[0].shape[0]
    copies = []
    for i, (mask, half) in enumerate(((0, 0), (1, 0), (3, 0), (2, 0), (2, 1))):
        at = (place_ref[0] ^ mask) * tokens + half * (tokens // 2)
        at = pl.multiple_of(at, tokens // 2)
        rows = pieces[i].shape[0]
        copy = pltpu.make_async_copy(pieces[i], out.at[pl.ds(at, rows), :], sems.at[i])
        copy.start()
        copies.append(copy)
    for copy in copies:
        copy.wait()


def whole_rows(place, pieces):
    tokens, width = pieces[0].shape
    return kernel_call(
        whole_kernel,
        "whole",
        shape_of((4 * tokens, width)),
        limit=2,
        in_specs=[SMEM] + [ANY] * 5,
        out_specs=ANY,
        scratch_shapes=[pltpu.SemaphoreType.DMA((5,))],
    )(place, *pieces)


GROUPS = (
    ((0, 0, 2048), (1, 0, 3072)),
    ((1, 3072, 2560), (1, 5632, 2560)),
)
WIDTHS = tuple(sum(p[2] for p in group) for group in GROUPS)


def reordered(values):
    source = lax.broadcasted_iota(jnp.int32, (256, 256), 0)
    place = lax.broadcasted_iota(jnp.int32, (256, 256), 1)
    wanted = (((place >> 4) & 3) << 6) | (((place >> 6) & 3) << 4) | (place & 15)
    moves = (source == wanted).astype(jnp.bfloat16)
    high = values.astype(jnp.bfloat16)
    rest = values - high.astype(jnp.float32)
    middle = rest.astype(jnp.bfloat16)
    low = (rest - middle.astype(jnp.float32)).astype(jnp.bfloat16)
    high, middle, low = (
        jnp.dot(part, moves, preferred_element_type=jnp.float32) for part in (high, middle, low)
    )
    return (high + middle) + low


def softmax_stats(teacher, student, stats_out):
    teacher_peak = jnp.max(teacher, axis=0, keepdims=True)
    student_peak = jnp.max(student, axis=0, keepdims=True)
    teacher_exp = jnp.exp(teacher - teacher_peak)
    teacher_total = jnp.sum(teacher_exp, axis=0, keepdims=True)
    student_total = jnp.sum(jnp.exp(student - student_peak), axis=0, keepdims=True)
    cross = jnp.sum(teacher_exp * (teacher - student), axis=0, keepdims=True)
    stats = (
        teacher_peak + jnp.log(teacher_total),
        student_peak + jnp.log(student_total),
        cross / teacher_total,
    )
    rows = [row[:, :128] for row in stats] + [row[:, 128:] for row in stats]
    stats_out[...] = jnp.concatenate(rows + [jnp.zeros((2, 128), jnp.float32)], axis=0)


def logits_kernel(last, place_ref, *refs):
    rows_from, heads, refs = refs[:2], refs[2:4], refs[4:]
    rows, head, row_sems, head_sems = refs[-4:]
    refs = refs[:-4]
    copies = []
    column = 0
    for group, source in zip(GROUPS, rows_from):
        base = column
        for kind, start, width in group:
            i = len(copies)
            columns = slice(column, column + width)
            size = heads[kind].shape[1] // 2
            start = pl.multiple_of(place_ref[0] * size + start, 128)
            pair = (
                pltpu.make_async_copy(
                    source.at[:, column - base : column - base + width],
                    rows.at[:, columns],
                    row_sems.at[i],
                ),
                pltpu.make_async_copy(
                    heads[kind].at[:, pl.ds(start, width)], head.at[:, columns], head_sems.at[i]
                ),
            )
            copies.append((kind + (base > 0), columns, pair))
            column = column + width
    ahead = 2
    for _, _, pair in copies[:ahead]:
        for copy in pair:
            copy.start()
    sums = [None, None, None]
    for i, (kind, columns, pair) in enumerate(copies):
        for copy in pair:
            copy.wait()
        if i + ahead < len(copies):
            for copy in copies[i + ahead][2]:
                copy.start()
        term = row_product(head[:, columns], rows[:, columns])
        sums[kind] = term if sums[kind] is None else sums[kind] + term
    if last:
        came, (student_out, teacher_out, stats_out) = refs[:3], refs[3:]
        student, teacher, second = (total + ref[...] for total, ref in zip(sums, came))
        teacher = teacher + reordered(second)
        student_out[...] = student
        teacher_out[...] = teacher
        softmax_stats(teacher, student, stats_out)
    else:
        for total, out in zip(sums, refs):
            out[...] = total


def logits_part(place, rows, heads, sums=()):
    vocab, tokens = heads[1].shape[0], rows[0].shape[0]
    shape = shape_of((vocab, tokens), jnp.float32)
    last = len(sums) > 0
    pieces = sum(len(group) for group in GROUPS)
    out_shape = [shape, shape, shape_of((8, 128), jnp.float32) if last else shape]
    return kernel_call(
        functools.partial(logits_kernel, last),
        "logits",
        out_shape,
        limit=48,
        in_specs=[SMEM] + [ANY] * 4 + [VMEM] * len(sums),
        out_specs=[VMEM] * 3,
        scratch_shapes=[
            pltpu.VMEM((tokens, sum(WIDTHS)), jnp.bfloat16),
            pltpu.VMEM((vocab, sum(WIDTHS)), jnp.bfloat16),
            pltpu.SemaphoreType.DMA((pieces,)),
            pltpu.SemaphoreType.DMA((pieces,)),
        ],
    )(place, *rows, *heads, *sums)


def one_hot_rows(core):
    place = lax.broadcasted_iota(jnp.int32, (256, 256), 0)
    column = lax.broadcasted_iota(jnp.int32, (256, 256), 1)
    x, yh, z, yl = (place >> 4) & 3, (place >> 3) & 1, (place >> 1) & 3, place & 1
    source = (x << 6) | (z << 4) | (yh << 3) | (yl << 2)
    source = source | (((place >> 7) ^ core) << 1) | ((place >> 6) & 1)
    return (column == source).astype(jnp.bfloat16)


def head_copies(source, head, sems):
    columns = head.shape[1] // sems.shape[0]
    parts = [slice(i * columns, (i + 1) * columns) for i in range(sems.shape[0])]
    copies = [
        pltpu.make_async_copy(source.at[:, part], head.at[:, part], sems.at[i])
        for i, part in enumerate(parts)
    ]
    for copy in copies:
        copy.start()
    return list(zip(parts, copies))


def merged_stats(every):
    peak = jnp.max(every, axis=0)
    scaled = jnp.exp(every - peak[None])
    total = jnp.sum(scaled, axis=0)
    cross = jnp.sum(scaled * pltpu.roll(every, 6, 1), axis=0) / total
    return peak + jnp.log(total), cross


def chip_stats_kernel(own_ref, came_ref, out_ref):
    lse, cross = merged_stats(jnp.concatenate([own_ref[...][None], came_ref[...][None]], axis=0))
    row = lax.broadcasted_iota(jnp.int32, lse.shape, 0)
    merged = jnp.where((row == 2) | (row == 5), pltpu.roll(cross, 2, 0), lse)
    out_ref[...] = jnp.broadcast_to(merged[None], out_ref.shape)


def row_grad_kernel(
    core_ref, every_ref, weight_ref, teacher_ref, student_ref, head_from,
    own_ref, send_ref, divergence_ref, head, sems,
):
    copies = head_copies(head_from, head, sems)
    lse, cross = merged_stats(every_ref[...])
    teacher_lse = jnp.concatenate([lse[0:1], lse[3:4]], axis=1)
    student_lse = jnp.concatenate([lse[1:2], lse[4:5]], axis=1)
    divergence_ref[...] = (
        jnp.concatenate([cross[0:1], cross[3:4]], axis=1) - teacher_lse + student_lse
    )
    logit_grad = weight_ref[...] * (
        jnp.exp(student_ref[...] - student_lse) - jnp.exp(teacher_ref[...] - teacher_lse)
    )
    grad = row_product(one_hot_rows(core_ref[0]), logit_grad.astype(jnp.bfloat16))
    grad = grad.astype(jnp.bfloat16)
    half = own_ref.shape[0]
    for columns, copy in copies:
        copy.wait()
        out = jnp.dot(grad, head[:, columns], preferred_element_type=jnp.float32)
        own_ref[:, columns] = out[:half]
        send_ref[:, columns] = out[half:].astype(jnp.bfloat16)


def row_grad_part(core, every, weight, teacher, student, student_head_t):
    vocab, width = student_head_t.shape
    tokens = weight.shape[1]
    return kernel_call(
        row_grad_kernel,
        "row_grad",
        [
            shape_of((tokens // 2, width), jnp.float32),
            shape_of((tokens // 2, width)),
            shape_of((1, tokens), jnp.float32),
        ],
        limit=48,
        in_specs=[SMEM] + [VMEM] * 4 + [ANY],
        out_specs=[VMEM] * 3,
        scratch_shapes=[
            pltpu.VMEM((vocab, width), jnp.bfloat16),
            pltpu.SemaphoreType.DMA((4,)),
        ],
    )(core, every, weight, teacher, student, student_head_t)


def pick_kernel(place_ref, ids_ref, head_from, own_ref, send_ref, head, sems):
    copies = head_copies(head_from, head, sems)
    vocab, tokens = head.shape[0], ids_ref.shape[1]
    entry = lax.broadcasted_iota(jnp.int32, (vocab, tokens), 0) + place_ref[1] * vocab
    place = lax.broadcasted_iota(jnp.int32, (tokens, tokens), 0)
    column = lax.broadcasted_iota(jnp.int32, (tokens, tokens), 1)
    source = (((place >> 7) ^ place_ref[0]) << 7) | ((place & 63) << 1) | ((place >> 6) & 1)
    chosen = row_product(
        (column == source).astype(jnp.bfloat16), (ids_ref[...] == entry).astype(jnp.bfloat16)
    ).astype(jnp.bfloat16)
    half = own_ref.shape[0]
    for columns, copy in copies:
        copy.wait()
        out = jnp.dot(chosen, head[:, columns], preferred_element_type=jnp.float32)
        own_ref[:, columns] = out[:half].astype(jnp.bfloat16)
        send_ref[:, columns] = out[half:].astype(jnp.bfloat16)


def pick_part(place, ids, student_head_t):
    vocab, width = student_head_t.shape
    shape = shape_of((ids.shape[1] // 2, width))
    return kernel_call(
        pick_kernel,
        "pick",
        [shape, shape],
        limit=48,
        in_specs=[SMEM, VMEM, ANY],
        out_specs=[VMEM] * 2,
        scratch_shapes=[
            pltpu.VMEM((vocab, width), jnp.bfloat16),
            pltpu.SemaphoreType.DMA((4,)),
        ],
    )(place, ids, student_head_t)


def join_kernel(*refs):
    pairs, out_ref, rows = refs[:-2], refs[-2], refs[-1]
    chips, height = out_ref.shape[0], 2 * SEGMENTS
    for base, (own_ref, came_ref) in enumerate(zip(pairs[::2], pairs[1::2])):
        for t in range(2):
            for i in range(SEGMENTS):
                for k in range(SEGMENT // 128):
                    part = slice(t * chips, (t + 1) * chips)
                    lanes = slice(i * SEGMENT + k * 128, i * SEGMENT + (k + 1) * 128)
                    total = own_ref[part, lanes].astype(jnp.float32)
                    total = total + came_ref[part, lanes].astype(jnp.float32)
                    at = pl.ds(t * SEGMENTS + i, chips, stride=height)
                    rows[k, at, :] = total
        for k in range(SEGMENT // 128):
            out_ref[:, base * height : (base + 1) * height, k * 128 : (k + 1) * 128] = (
                rows[k].reshape(chips, height, 128).astype(jnp.bfloat16)
            )


def join_part(*pairs):
    chips = pairs[0].shape[0] // 2
    height = 2 * SEGMENTS
    return kernel_call(
        join_kernel,
        "join",
        shape_of((chips, height * len(pairs) // 2, SEGMENT)),
        limit=14,
        in_specs=[VMEM] * len(pairs),
        out_specs=VMEM,
        scratch_shapes=[pltpu.VMEM((SEGMENT // 128, chips * height, 128), jnp.float32)],
    )(*pairs)


def block_gain(gain_ref):
    gain = gain_ref[...].astype(jnp.float32)
    lanes = SEGMENT // 128
    token = jnp.concatenate(
        [
            jnp.concatenate([gain[lanes * i + k : lanes * i + k + 1] for k in range(lanes)], axis=1)
            for i in range(SEGMENTS)
        ],
        axis=0,
    )
    return jnp.concatenate([token, token], axis=0)


def block_mean(values):
    means = []
    for t in range(2):
        part = values[t * SEGMENTS : (t + 1) * SEGMENTS]
        total = jnp.sum(jnp.sum(part, axis=0, keepdims=True), axis=1, keepdims=True)
        means.append(jnp.broadcast_to(total / (SEGMENTS * SEGMENT), (SEGMENTS, 1)))
    return jnp.concatenate(means, axis=0)


def block_inverse(values):
    return lax.rsqrt(block_mean(values * values) + eps)


def block_back(upstream, values, gain):
    inverse = block_inverse(values)
    gained = upstream * gain
    return inverse * gained - values * inverse**3 * block_mean(gained * values)


def block_sum(blocks_ref):
    return jnp.sum(blocks_ref[...].astype(jnp.float32), axis=0)


def embed_kernel(blocks_ref, gain_ref, embedded_ref, out_ref):
    values = block_sum(blocks_ref)
    embedded_ref[...] = values
    rows = (values * block_inverse(values) * block_gain(gain_ref)).astype(jnp.bfloat16)
    out_ref[...] = jnp.broadcast_to(rows[None], out_ref.shape)


def final_kernel(blocks_ref, states_ref, gain_ref, grad_ref, out_ref, states):
    for i in range(SEGMENTS):
        part = states_ref[:, i * SEGMENT : (i + 1) * SEGMENT].astype(jnp.float32)
        for t in range(2):
            states[t * SEGMENTS + i : t * SEGMENTS + i + 1, :] = part[t : t + 1]
    grad = block_back(block_sum(blocks_ref), states[...], block_gain(gain_ref))
    grad_ref[...] = grad
    out_ref[...] = jnp.broadcast_to(grad.astype(jnp.bfloat16)[None], out_ref.shape)


def state_kernel(blocks_ref, grad_ref, embedded_ref, gain_ref, out_ref):
    back = block_back(block_sum(blocks_ref), embedded_ref[...], block_gain(gain_ref))
    grad = grad_ref[...] + back
    for t in range(2):
        for i in range(SEGMENTS):
            out_ref[t : t + 1, i * SEGMENT : (i + 1) * SEGMENT] = grad[
                t * SEGMENTS + i : t * SEGMENTS + i + 1
            ]


BLOCK = (2 * SEGMENTS, SEGMENT)


def spread_rows(refs, scratches):
    for ref, rows in zip(refs, scratches):
        values = ref[...].astype(jnp.float32)
        values = values.reshape(values.shape[0] * values.shape[1], values.shape[2])
        for k in range(SEGMENT // 128):
            rows[k] = values[:, k * 128 : (k + 1) * 128]


def segment_rows(scratches, segment):
    parts = []
    for rows in scratches:
        height = 2 * SEGMENTS
        for t in range(2):
            at = pl.ds(t * SEGMENTS + segment, rows.shape[1] // height, stride=height)
            parts.append(
                jnp.concatenate([rows[k, at, :] for k in range(SEGMENT // 128)], axis=1)
            )
    return jnp.concatenate(parts, axis=0).astype(jnp.bfloat16)


def gate_kernel(own_ref, other_ref, gate_ref, up_ref, out_ref, *scratches):
    spread_rows((own_ref, other_ref), scratches)
    total = None
    for i in range(SEGMENTS):
        columns = slice(i * SEGMENT, (i + 1) * SEGMENT)
        weight = jnp.concatenate([gate_ref[:, columns], up_ref[:, columns]], axis=0)
        term = row_product(weight, segment_rows(scratches, i))
        total = term if total is None else total + term
    out_ref[...] = total


def ffn_grad_kernel(
    own_ref, other_ref, down_ref, hidden_ref, gate_ref, up_ref, own_out, send_out, *scratches
):
    spread_rows((own_ref, other_ref), scratches)
    units = down_ref.shape[0]
    hidden, act_grad = hidden_ref[...], None
    for i in range(SEGMENTS):
        columns = slice(i * SEGMENT, (i + 1) * SEGMENT)
        term = row_product(down_ref[:, columns], segment_rows(scratches, i))
        act_grad = term if act_grad is None else act_grad + term
    gate, upper = hidden[:units, :], hidden[units:, :]
    sigmoid_gate = jax.nn.sigmoid(gate)
    gate_grad = act_grad * upper * sigmoid_gate * (1.0 + gate * (1.0 - sigmoid_gate))
    upper_grad = act_grad * gate * sigmoid_gate
    grads = jnp.concatenate([gate_grad, upper_grad], axis=0).astype(jnp.bfloat16)
    tokens = grads.shape[1]
    same = lax.broadcasted_iota(jnp.int32, (tokens, tokens), 0) == lax.broadcasted_iota(
        jnp.int32, (tokens, tokens), 1
    )
    grads = row_product(same.astype(jnp.bfloat16), grads).astype(jnp.bfloat16)
    for i in range(SEGMENTS):
        columns = slice(i * SEGMENT, (i + 1) * SEGMENT)
        weight = jnp.concatenate([gate_ref[:, columns], up_ref[:, columns]], axis=0)
        out = jnp.dot(grads, weight, preferred_element_type=jnp.float32)
        own_out[:, columns] = out[: tokens // 2]
        send_out[:, columns] = out[tokens // 2 :].astype(jnp.bfloat16)


def ffn_part(body, name, out_shape, blocks, *others):
    rows = blocks.shape[0] * blocks.shape[1]
    scratch = pltpu.VMEM((SEGMENT // 128, rows, 128), jnp.float32)
    return kernel_call(
        body,
        name,
        out_shape,
        limit=20,
        in_specs=[VMEM] * (2 + len(others)),
        out_specs=[VMEM] * len(out_shape),
        scratch_shapes=[scratch, scratch],
    )(blocks, swap_cores(blocks), *others)


def shards(
    teacher_states,
    teacher_gain,
    teacher_head,
    student_states,
    student_gain,
    student_head,
    token_ids,
    ffn_gain,
    gate_weight,
    up_weight,
    down_weight,
    token_weight,
):
    core = lax.axis_index("core")
    device = lax.axis_index(AXES)
    own_core = jnp.full((1,), core, jnp.int32)
    x, z, y = (lax.axis_index(line).astype(jnp.int32) for line in ("x", "z", ("yh", "yl")))
    teacher_gain, student_gain, ffn_gain = (
        gain.reshape(-1, 128) for gain in (teacher_gain, student_gain, ffn_gain)
    )
    student_head_t, teacher_head_t = student_head.T, teacher_head.T
    heads = (student_head_t, teacher_head_t)
    gate_t, up_t = gate_weight.T, up_weight.T

    width = sum(WIDTHS)
    half_shape = shape_of((2, width))
    keep, send = kernel_call(
        rows_kernel,
        "rows",
        [half_shape, half_shape],
        limit=56,
        in_specs=[SMEM] + [ANY] * 4,
        out_specs=[VMEM] * 2,
        scratch_shapes=[
            pltpu.VMEM(teacher_states.shape, jnp.bfloat16),
            pltpu.VMEM(student_states.shape, jnp.bfloat16),
            pltpu.VMEM(teacher_gain.shape, jnp.bfloat16),
            pltpu.VMEM(student_gain.shape, jnp.bfloat16),
            pltpu.VMEM((160, 128), jnp.float32),
            pltpu.SemaphoreType.DMA((4,)),
        ],
    )(own_core, teacher_states, teacher_gain, student_states, student_gain)
    (rows,) = in_pair(own_core, keep, swap_cores(send), (width,))

    (rows,) = in_pair((y & 1).reshape(1), rows, along(rows, ("yh", "yl"), 1), (width,))
    first, second = in_pair((y >> 1).reshape(1), rows, along(rows, ("yh", "yl"), 3), WIDTHS)
    for bit, mask in ((0, 1), (1, 3)):
        came = (along(first, "z", mask), along(second, "x", mask))
        bits = (jnp.stack([z, x]) >> bit) & 1
        first, second = in_pairs(bits, (first, came[0], second, came[1]))
    came = [along(first, "x", 1), along(first, "x", 3), along(second, "z", 1), along(second, "z", 3)]
    place = jnp.stack([core, device]).astype(jnp.int32)
    own, send = pick_part(place, token_ids.reshape(1, 256), student_head_t)
    came, picked = lax.optimization_barrier((came, join_part(own, swap_cores(send))))
    halves = halves_of(came)
    far = [
        along(half, line, mask)
        for half, line, mask in zip(halves, ("x", "x", "z", "z"), (3, 1, 3, 1))
    ]
    far = lax.optimization_barrier(far)
    rows = (
        whole_rows(x.reshape(1), [first] + came[:2] + far[:2]),
        whole_rows(z.reshape(1), [second] + came[2:] + far[2:]),
    )
    others = tuple(swap_cores(part) for part in rows)
    sums = logits_part(own_core, rows, heads)
    student, teacher, stats = logits_part(1 - own_core, others, heads, sums)
    stats = kernel_call(
        chip_stats_kernel,
        "chip_stats",
        shape_of((64, 8, 128), jnp.float32),
        limit=2,
        in_specs=[VMEM] * 2,
        out_specs=VMEM,
    )(stats, swap_cores(stats))
    stats, picked = lax.optimization_barrier((stats, picked))
    every = exchange(stats, CHIPS)
    picked = exchange(picked, CHIPS)

    weight = token_weight.reshape(2, 4, 2, 4, 2, 2).transpose(1, 3, 2, 4, 0, 5).reshape(1, 256)
    own, send, divergence = row_grad_part(
        own_core, every, weight, teacher, student, student_head_t
    )
    divergence = divergence.reshape(4, 4, 2, 2, 2, 2).transpose(4, 0, 2, 1, 3, 5).reshape(256)
    embedded, ffn_rows = kernel_call(
        embed_kernel,
        "embed",
        [shape_of(BLOCK, jnp.float32), shape_of(picked.shape)],
        in_specs=[VMEM] * 2,
        out_specs=[VMEM] * 2,
    )(picked, ffn_gain)
    blocks = join_part(own, swap_cores(send))
    blocks, ffn_rows = lax.optimization_barrier((blocks, ffn_rows))
    blocks = exchange(blocks, CHIPS)
    ffn_rows = exchange(ffn_rows, CHIPS)
    final_grad, blocks = kernel_call(
        final_kernel,
        "final",
        [shape_of(BLOCK, jnp.float32), shape_of(blocks.shape)],
        in_specs=[VMEM] * 3,
        out_specs=[VMEM] * 2,
        scratch_shapes=[pltpu.VMEM(BLOCK, jnp.float32)],
    )(blocks, student_states, student_gain)
    blocks = exchange(blocks, CHIPS)
    (hidden,) = ffn_part(
        gate_kernel, "gate_upper", [shape_of((224, 256), jnp.float32)], ffn_rows, gate_t, up_t
    )
    shape = (128, 4096)
    own, send = ffn_part(
        ffn_grad_kernel,
        "ffn_grad",
        [shape_of(shape, jnp.float32), shape_of(shape)],
        blocks,
        down_weight,
        hidden,
        gate_t,
        up_t,
    )
    ffn_grad = exchange(join_part(own, swap_cores(send)), CHIPS)
    state_grad = kernel_call(
        state_kernel,
        "state",
        shape_of((2, 4096), jnp.float32),
        in_specs=[VMEM] * 4,
        out_specs=VMEM,
    )(ffn_grad, final_grad, embedded, ffn_gain)
    return (divergence, state_grad)


def solution(mesh):
    fine = Mesh(mesh.devices.reshape(SHAPE), AXES)
    in_specs = (
        P(AXES, None),
        P(),
        P(None, AXES),
        P(AXES, None),
        P(),
        P(None, AXES),
        P(),
        P(),
        P(None, AXES),
        P(None, AXES),
        P(AXES, None),
        P(),
    )
    out_specs = (P(), P(AXES, None))
    return jax.shard_map(shards, mesh=fine, in_specs=in_specs, out_specs=out_specs, check_vma=False)
```

```python
import functools

import jax
import jax.numpy as jnp
from jax import lax
from jax.experimental import pallas as pl
from jax.experimental.pallas import tpu as pltpu
from jax.sharding import Mesh
from jax.sharding import PartitionSpec as P

eps = 1e-05
SHAPE = (2, 4, 2, 4, 2)
AXES = ("core", "x", "yh", "z", "yl")
CHIPS = AXES[1:]
MIB = 1024 * 1024

VMEM = pl.BlockSpec(memory_space=pltpu.VMEM)
SMEM = pl.BlockSpec(memory_space=pltpu.SMEM)
ANY = pl.BlockSpec(memory_space=pl.ANY)
SEGMENTS = 8
SEGMENT = 512


def kernel_call(body, name, out_shape, limit=8, **options):
    return pl.pallas_call(
        body,
        name=name,
        out_shape=out_shape,
        compiler_params=pltpu.CompilerParams(vmem_limit_bytes=limit * MIB),
        cost_estimate=pl.CostEstimate(flops=1, bytes_accessed=1, transcendentals=0),
        **options,
    )


def shape_of(shape, dtype=jnp.bfloat16):
    return jax.ShapeDtypeStruct(shape, dtype)


def row_product(left, right):
    return lax.dot_general(
        left, right, (((1,), (1,)), ((), ())), preferred_element_type=jnp.float32
    )


def swap_cores(values):
    return lax.ppermute(values, "core", [(0, 1), (1, 0)])


def exchange(blocks, axes):
    return lax.all_to_all(blocks, axes, split_axis=0, concat_axis=0, tiled=True)


def rows_kernel(
    core_ref, teacher_from, teacher_gain, student_from, student_gain, keep_ref, send_ref,
    teacher_ref, student_ref, teacher_gains, student_gains, gains, sems,
):
    copies = [
        pltpu.make_async_copy(source, target, sems.at[i])
        for i, (source, target) in enumerate(
            (
                (student_gain, student_gains),
                (student_from, student_ref),
                (teacher_gain, teacher_gains),
                (teacher_from, teacher_ref),
            )
        )
    ]
    for copy in copies:
        copy.start()
    for copy in copies:
        copy.wait()
    first = student_gain.shape[0]
    gains[:first, :] = student_gains[...].astype(jnp.float32)
    gains[first:, :] = teacher_gains[...].astype(jnp.float32)
    column = 0
    for values, base in ((student_ref, 0), (teacher_ref, first)):
        half = values.shape[1] // 2
        every = values[...].astype(jnp.float32)
        inverse = lax.rsqrt(jnp.mean(every * every, axis=-1, keepdims=True) + eps)
        for part, out in ((core_ref[0], keep_ref), (1 - core_ref[0], send_ref)):
            for k in range(half // 128):
                place = pl.ds(pl.multiple_of(part * half + k * 128, 128), 128)
                rows = values[:, place].astype(jnp.float32) * inverse
                rows = rows * gains[pl.ds(base + part * (half // 128) + k, 1), :]
                out[:, column + k * 128 : column + (k + 1) * 128] = rows.astype(jnp.bfloat16)
        column = column + half


def pair_kernel(place_ref, own_ref, came_ref, *out_refs):
    own, came = own_ref[...].astype(jnp.float32), came_ref[...].astype(jnp.float32)
    first = place_ref[0] == 0
    rows = jnp.concatenate([jnp.where(first, own, came), jnp.where(first, came, own)], axis=0)
    rows = rows.astype(jnp.bfloat16)
    column = 0
    for out in out_refs:
        out[...] = rows[:, column : column + out.shape[1]]
        column = column + out.shape[1]


def in_pair(bit, own, came, widths):
    tokens = 2 * own.shape[0]
    return kernel_call(
        pair_kernel,
        "pair",
        [shape_of((tokens, w)) for w in widths],
        in_specs=[SMEM] + [VMEM] * 2,
        out_specs=[VMEM] * len(widths),
    )(bit, own, came)


def groups_kernel(place_ref, *refs):
    count = (len(refs) - 1) // 3
    sources, outs, sems = refs[: 2 * count], refs[2 * count : -1], refs[-1]
    copies = []
    for g, out in enumerate(outs):
        for i in range(2):
            source = sources[2 * g + i]
            tokens = source.shape[0]
            at = pl.multiple_of((place_ref[g] ^ i) * tokens, tokens)
            copy = pltpu.make_async_copy(source, out.at[pl.ds(at, tokens), :], sems.at[2 * g + i])
            copy.start()
            copies.append(copy)
    for copy in copies:
        copy.wait()


def in_pairs(bits, parts):
    tokens = 2 * parts[0].shape[0]
    return kernel_call(
        groups_kernel,
        "pairs",
        [shape_of((tokens, part.shape[1])) for part in parts[::2]],
        limit=2,
        in_specs=[SMEM] + [ANY] * len(parts),
        out_specs=[ANY] * (len(parts) // 2),
        scratch_shapes=[pltpu.SemaphoreType.DMA((len(parts),))],
    )(bits, *parts)


def halves_kernel(*refs):
    count = (len(refs) - 1) // 2
    copies = []
    for i, (piece, out) in enumerate(zip(refs[:count], refs[count:])):
        rows = out.shape[0]
        copy = pltpu.make_async_copy(piece.at[pl.ds((i % 2) * rows, rows), :], out, refs[-1].at[i])
        copy.start()
        copies.append(copy)
    for copy in copies:
        copy.wait()


def halves_of(pieces):
    return kernel_call(
        halves_kernel,
        "halves",
        [shape_of((p.shape[0] // 2, p.shape[1])) for p in pieces],
        limit=2,
        in_specs=[ANY] * len(pieces),
        out_specs=[ANY] * len(pieces),
        scratch_shapes=[pltpu.SemaphoreType.DMA((len(pieces),))],
    )(*pieces)


def along(block, line, mask):
    return lax.ppermute(block, line, [(i, i ^ mask) for i in range(4)])


def whole_kernel(place_ref, *refs):
    pieces, out, sems = refs[:5], refs[5], refs[6]
    tokens = pieces[0].shape[0]
    copies = []
    for i, (mask, half) in enumerate(((0, 0), (1, 0), (3, 0), (2, 0), (2, 1))):
        at = (place_ref[0] ^ mask) * tokens + half * (tokens // 2)
        at = pl.multiple_of(at, tokens // 2)
        rows = pieces[i].shape[0]
        copy = pltpu.make_async_copy(pieces[i], out.at[pl.ds(at, rows), :], sems.at[i])
        copy.start()
        copies.append(copy)
    for copy in copies:
        copy.wait()


def whole_rows(place, pieces):
    tokens, width = pieces[0].shape
    return kernel_call(
        whole_kernel,
        "whole",
        shape_of((4 * tokens, width)),
        limit=2,
        in_specs=[SMEM] + [ANY] * 5,
        out_specs=ANY,
        scratch_shapes=[pltpu.SemaphoreType.DMA((5,))],
    )(place, *pieces)


GROUPS = (
    ((0, 0, 2048), (1, 0, 3072)),
    ((1, 3072, 2560), (1, 5632, 2560)),
)
WIDTHS = tuple(sum(p[2] for p in group) for group in GROUPS)


def reordered(values):
    source = lax.broadcasted_iota(jnp.int32, (256, 256), 0)
    place = lax.broadcasted_iota(jnp.int32, (256, 256), 1)
    wanted = (((place >> 4) & 3) << 6) | (((place >> 6) & 3) << 4) | (place & 15)
    moves = (source == wanted).astype(jnp.bfloat16)
    high = values.astype(jnp.bfloat16)
    rest = values - high.astype(jnp.float32)
    middle = rest.astype(jnp.bfloat16)
    low = (rest - middle.astype(jnp.float32)).astype(jnp.bfloat16)
    high, middle, low = (
        jnp.dot(part, moves, preferred_element_type=jnp.float32) for part in (high, middle, low)
    )
    return (high + middle) + low


def softmax_stats(teacher, student, stats_out):
    teacher_peak = jnp.max(teacher, axis=0, keepdims=True)
    student_peak = jnp.max(student, axis=0, keepdims=True)
    teacher_exp = jnp.exp(teacher - teacher_peak)
    teacher_total = jnp.sum(teacher_exp, axis=0, keepdims=True)
    student_total = jnp.sum(jnp.exp(student - student_peak), axis=0, keepdims=True)
    cross = jnp.sum(teacher_exp * (teacher - student), axis=0, keepdims=True)
    stats = (
        teacher_peak + jnp.log(teacher_total),
        student_peak + jnp.log(student_total),
        cross / teacher_total,
    )
    rows = [row[:, :128] for row in stats] + [row[:, 128:] for row in stats]
    stats_out[...] = jnp.concatenate(rows + [jnp.zeros((2, 128), jnp.float32)], axis=0)


def logits_kernel(last, place_ref, *refs):
    rows_from, heads, refs = refs[:2], refs[2:4], refs[4:]
    rows, head, row_sems, head_sems = refs[-4:]
    refs = refs[:-4]
    copies = []
    column = 0
    for group, source in zip(GROUPS, rows_from):
        base = column
        for kind, start, width in group:
            i = len(copies)
            columns = slice(column, column + width)
            size = heads[kind].shape[1] // 2
            start = pl.multiple_of(place_ref[0] * size + start, 128)
            pair = (
                pltpu.make_async_copy(
                    source.at[:, column - base : column - base + width],
                    rows.at[:, columns],
                    row_sems.at[i],
                ),
                pltpu.make_async_copy(
                    heads[kind].at[:, pl.ds(start, width)], head.at[:, columns], head_sems.at[i]
                ),
            )
            copies.append((kind + (base > 0), columns, pair))
            column = column + width
    ahead = 2
    for _, _, pair in copies[:ahead]:
        for copy in pair:
            copy.start()
    sums = [None, None, None]
    for i, (kind, columns, pair) in enumerate(copies):
        for copy in pair:
            copy.wait()
        if i + ahead < len(copies):
            for copy in copies[i + ahead][2]:
                copy.start()
        term = row_product(head[:, columns], rows[:, columns])
        sums[kind] = term if sums[kind] is None else sums[kind] + term
    if last:
        came, (student_out, teacher_out, stats_out) = refs[:3], refs[3:]
        student, teacher, second = (total + ref[...] for total, ref in zip(sums, came))
        teacher = teacher + reordered(second)
        student_out[...] = student
        teacher_out[...] = teacher
        softmax_stats(teacher, student, stats_out)
    else:
        for total, out in zip(sums, refs):
            out[...] = total


def logits_part(place, rows, heads, sums=()):
    vocab, tokens = heads[1].shape[0], rows[0].shape[0]
    shape = shape_of((vocab, tokens), jnp.float32)
    last = len(sums) > 0
    pieces = sum(len(group) for group in GROUPS)
    out_shape = [shape, shape, shape_of((8, 128), jnp.float32) if last else shape]
    return kernel_call(
        functools.partial(logits_kernel, last),
        "logits",
        out_shape,
        limit=48,
        in_specs=[SMEM] + [ANY] * 4 + [VMEM] * len(sums),
        out_specs=[VMEM] * 3,
        scratch_shapes=[
            pltpu.VMEM((tokens, sum(WIDTHS)), jnp.bfloat16),
            pltpu.VMEM((vocab, sum(WIDTHS)), jnp.bfloat16),
            pltpu.SemaphoreType.DMA((pieces,)),
            pltpu.SemaphoreType.DMA((pieces,)),
        ],
    )(place, *rows, *heads, *sums)


def one_hot_rows(core):
    place = lax.broadcasted_iota(jnp.int32, (256, 256), 0)
    column = lax.broadcasted_iota(jnp.int32, (256, 256), 1)
    x, yh, z, yl = (place >> 4) & 3, (place >> 3) & 1, (place >> 1) & 3, place & 1
    source = (x << 6) | (z << 4) | (yh << 3) | (yl << 2)
    source = source | (((place >> 7) ^ core) << 1) | ((place >> 6) & 1)
    return (column == source).astype(jnp.bfloat16)


def head_copies(source, head, sems):
    columns = head.shape[1] // sems.shape[0]
    parts = [slice(i * columns, (i + 1) * columns) for i in range(sems.shape[0])]
    copies = [
        pltpu.make_async_copy(source.at[:, part], head.at[:, part], sems.at[i])
        for i, part in enumerate(parts)
    ]
    for copy in copies:
        copy.start()
    return list(zip(parts, copies))


def merged_stats(every):
    peak = jnp.max(every, axis=0)
    scaled = jnp.exp(every - peak[None])
    total = jnp.sum(scaled, axis=0)
    cross = jnp.sum(scaled * pltpu.roll(every, 6, 1), axis=0) / total
    return peak + jnp.log(total), cross


def chip_stats_kernel(own_ref, came_ref, out_ref):
    lse, cross = merged_stats(jnp.concatenate([own_ref[...][None], came_ref[...][None]], axis=0))
    row = lax.broadcasted_iota(jnp.int32, lse.shape, 0)
    merged = jnp.where((row == 2) | (row == 5), pltpu.roll(cross, 2, 0), lse)
    out_ref[...] = jnp.broadcast_to(merged[None], out_ref.shape)


def row_grad_kernel(
    core_ref, every_ref, weight_ref, teacher_ref, student_ref, head_from,
    own_ref, send_ref, divergence_ref, head, sems,
):
    copies = head_copies(head_from, head, sems)
    lse, cross = merged_stats(every_ref[...])
    teacher_lse = jnp.concatenate([lse[0:1], lse[3:4]], axis=1)
    student_lse = jnp.concatenate([lse[1:2], lse[4:5]], axis=1)
    divergence_ref[...] = (
        jnp.concatenate([cross[0:1], cross[3:4]], axis=1) - teacher_lse + student_lse
    )
    logit_grad = weight_ref[...] * (
        jnp.exp(student_ref[...] - student_lse) - jnp.exp(teacher_ref[...] - teacher_lse)
    )
    grad = row_product(one_hot_rows(core_ref[0]), logit_grad.astype(jnp.bfloat16))
    grad = grad.astype(jnp.bfloat16)
    half = own_ref.shape[0]
    for columns, copy in copies:
        copy.wait()
        out = jnp.dot(grad, head[:, columns], preferred_element_type=jnp.float32)
        own_ref[:, columns] = out[:half]
        send_ref[:, columns] = out[half:].astype(jnp.bfloat16)


def row_grad_part(core, every, weight, teacher, student, student_head_t):
    vocab, width = student_head_t.shape
    tokens = weight.shape[1]
    return kernel_call(
        row_grad_kernel,
        "row_grad",
        [
            shape_of((tokens // 2, width), jnp.float32),
            shape_of((tokens // 2, width)),
            shape_of((1, tokens), jnp.float32),
        ],
        limit=48,
        in_specs=[SMEM] + [VMEM] * 4 + [ANY],
        out_specs=[VMEM] * 3,
        scratch_shapes=[
            pltpu.VMEM((vocab, width), jnp.bfloat16),
            pltpu.SemaphoreType.DMA((4,)),
        ],
    )(core, every, weight, teacher, student, student_head_t)


def pick_kernel(place_ref, ids_ref, head_from, own_ref, send_ref, head, sems):
    copies = head_copies(head_from, head, sems)
    vocab, tokens = head.shape[0], ids_ref.shape[1]
    entry = lax.broadcasted_iota(jnp.int32, (vocab, tokens), 0) + place_ref[1] * vocab
    place = lax.broadcasted_iota(jnp.int32, (tokens, tokens), 0)
    column = lax.broadcasted_iota(jnp.int32, (tokens, tokens), 1)
    source = (((place >> 7) ^ place_ref[0]) << 7) | ((place & 63) << 1) | ((place >> 6) & 1)
    chosen = row_product(
        (column == source).astype(jnp.bfloat16), (ids_ref[...] == entry).astype(jnp.bfloat16)
    ).astype(jnp.bfloat16)
    half = own_ref.shape[0]
    for columns, copy in copies:
        copy.wait()
        out = jnp.dot(chosen, head[:, columns], preferred_element_type=jnp.float32)
        own_ref[:, columns] = out[:half].astype(jnp.bfloat16)
        send_ref[:, columns] = out[half:].astype(jnp.bfloat16)


def pick_part(place, ids, student_head_t):
    vocab, width = student_head_t.shape
    shape = shape_of((ids.shape[1] // 2, width))
    return kernel_call(
        pick_kernel,
        "pick",
        [shape, shape],
        limit=48,
        in_specs=[SMEM, VMEM, ANY],
        out_specs=[VMEM] * 2,
        scratch_shapes=[
            pltpu.VMEM((vocab, width), jnp.bfloat16),
            pltpu.SemaphoreType.DMA((4,)),
        ],
    )(place, ids, student_head_t)


def join_kernel(*refs):
    pairs, out_ref, rows = refs[:-2], refs[-2], refs[-1]
    chips, height = out_ref.shape[0], 2 * SEGMENTS
    for base, (own_ref, came_ref) in enumerate(zip(pairs[::2], pairs[1::2])):
        for t in range(2):
            for i in range(SEGMENTS):
                for k in range(SEGMENT // 128):
                    part = slice(t * chips, (t + 1) * chips)
                    lanes = slice(i * SEGMENT + k * 128, i * SEGMENT + (k + 1) * 128)
                    total = own_ref[part, lanes].astype(jnp.float32)
                    total = total + came_ref[part, lanes].astype(jnp.float32)
                    at = pl.ds(t * SEGMENTS + i, chips, stride=height)
                    rows[k, at, :] = total
        for k in range(SEGMENT // 128):
            out_ref[:, base * height : (base + 1) * height, k * 128 : (k + 1) * 128] = (
                rows[k].reshape(chips, height, 128).astype(jnp.bfloat16)
            )


def join_part(*pairs):
    chips = pairs[0].shape[0] // 2
    height = 2 * SEGMENTS
    return kernel_call(
        join_kernel,
        "join",
        shape_of((chips, height * len(pairs) // 2, SEGMENT)),
        limit=14,
        in_specs=[VMEM] * len(pairs),
        out_specs=VMEM,
        scratch_shapes=[pltpu.VMEM((SEGMENT // 128, chips * height, 128), jnp.float32)],
    )(*pairs)


def block_gain(gain_ref):
    gain = gain_ref[...].astype(jnp.float32)
    lanes = SEGMENT // 128
    token = jnp.concatenate(
        [
            jnp.concatenate([gain[lanes * i + k : lanes * i + k + 1] for k in range(lanes)], axis=1)
            for i in range(SEGMENTS)
        ],
        axis=0,
    )
    return jnp.concatenate([token, token], axis=0)


def block_mean(values):
    means = []
    for t in range(2):
        part = values[t * SEGMENTS : (t + 1) * SEGMENTS]
        total = jnp.sum(jnp.sum(part, axis=0, keepdims=True), axis=1, keepdims=True)
        means.append(jnp.broadcast_to(total / (SEGMENTS * SEGMENT), (SEGMENTS, 1)))
    return jnp.concatenate(means, axis=0)


def block_inverse(values):
    return lax.rsqrt(block_mean(values * values) + eps)


def block_back(upstream, values, gain):
    inverse = block_inverse(values)
    gained = upstream * gain
    return inverse * gained - values * inverse**3 * block_mean(gained * values)


def block_sum(blocks_ref):
    return jnp.sum(blocks_ref[...].astype(jnp.float32), axis=0)


def embed_kernel(blocks_ref, gain_ref, embedded_ref, out_ref):
    values = block_sum(blocks_ref)
    embedded_ref[...] = values
    rows = (values * block_inverse(values) * block_gain(gain_ref)).astype(jnp.bfloat16)
    out_ref[...] = jnp.broadcast_to(rows[None], out_ref.shape)


def final_kernel(blocks_ref, states_ref, gain_ref, grad_ref, out_ref, states):
    for i in range(SEGMENTS):
        part = states_ref[:, i * SEGMENT : (i + 1) * SEGMENT].astype(jnp.float32)
        for t in range(2):
            states[t * SEGMENTS + i : t * SEGMENTS + i + 1, :] = part[t : t + 1]
    grad = block_back(block_sum(blocks_ref), states[...], block_gain(gain_ref))
    grad_ref[...] = grad
    out_ref[...] = jnp.broadcast_to(grad.astype(jnp.bfloat16)[None], out_ref.shape)


def state_kernel(blocks_ref, grad_ref, embedded_ref, gain_ref, out_ref):
    back = block_back(block_sum(blocks_ref), embedded_ref[...], block_gain(gain_ref))
    grad = grad_ref[...] + back
    for t in range(2):
        for i in range(SEGMENTS):
            out_ref[t : t + 1, i * SEGMENT : (i + 1) * SEGMENT] = grad[
                t * SEGMENTS + i : t * SEGMENTS + i + 1
            ]


BLOCK = (2 * SEGMENTS, SEGMENT)


def spread_rows(refs, scratches):
    for ref, rows in zip(refs, scratches):
        values = ref[...].astype(jnp.float32)
        values = values.reshape(values.shape[0] * values.shape[1], values.shape[2])
        for k in range(SEGMENT // 128):
            rows[k] = values[:, k * 128 : (k + 1) * 128]


def segment_rows(scratches, segment):
    parts = []
    for rows in scratches:
        height = 2 * SEGMENTS
        for t in range(2):
            at = pl.ds(t * SEGMENTS + segment, rows.shape[1] // height, stride=height)
            parts.append(
                jnp.concatenate([rows[k, at, :] for k in range(SEGMENT // 128)], axis=1)
            )
    return jnp.concatenate(parts, axis=0).astype(jnp.bfloat16)


def gate_kernel(own_ref, other_ref, gate_ref, up_ref, out_ref, *scratches):
    spread_rows((own_ref, other_ref), scratches)
    total = None
    for i in range(SEGMENTS):
        columns = slice(i * SEGMENT, (i + 1) * SEGMENT)
        weight = jnp.concatenate([gate_ref[:, columns], up_ref[:, columns]], axis=0)
        term = row_product(weight, segment_rows(scratches, i))
        total = term if total is None else total + term
    out_ref[...] = total


def ffn_grad_kernel(
    own_ref, other_ref, down_ref, hidden_ref, gate_ref, up_ref, own_out, send_out, *scratches
):
    spread_rows((own_ref, other_ref), scratches)
    units = down_ref.shape[0]
    hidden, act_grad = hidden_ref[...], None
    for i in range(SEGMENTS):
        columns = slice(i * SEGMENT, (i + 1) * SEGMENT)
        term = row_product(down_ref[:, columns], segment_rows(scratches, i))
        act_grad = term if act_grad is None else act_grad + term
    gate, upper = hidden[:units, :], hidden[units:, :]
    sigmoid_gate = jax.nn.sigmoid(gate)
    gate_grad = act_grad * upper * sigmoid_gate * (1.0 + gate * (1.0 - sigmoid_gate))
    upper_grad = act_grad * gate * sigmoid_gate
    grads = jnp.concatenate([gate_grad, upper_grad], axis=0).astype(jnp.bfloat16)
    tokens = grads.shape[1]
    same = lax.broadcasted_iota(jnp.int32, (tokens, tokens), 0) == lax.broadcasted_iota(
        jnp.int32, (tokens, tokens), 1
    )
    grads = row_product(same.astype(jnp.bfloat16), grads).astype(jnp.bfloat16)
    for i in range(SEGMENTS):
        columns = slice(i * SEGMENT, (i + 1) * SEGMENT)
        weight = jnp.concatenate([gate_ref[:, columns], up_ref[:, columns]], axis=0)
        out = jnp.dot(grads, weight, preferred_element_type=jnp.float32)
        own_out[:, columns] = out[: tokens // 2]
        send_out[:, columns] = out[tokens // 2 :].astype(jnp.bfloat16)


def ffn_part(body, name, out_shape, blocks, *others):
    rows = blocks.shape[0] * blocks.shape[1]
    scratch = pltpu.VMEM((SEGMENT // 128, rows, 128), jnp.float32)
    return kernel_call(
        body,
        name,
        out_shape,
        limit=20,
        in_specs=[VMEM] * (2 + len(others)),
        out_specs=[VMEM] * len(out_shape),
        scratch_shapes=[scratch, scratch],
    )(blocks, swap_cores(blocks), *others)


def shards(
    teacher_states,
    teacher_gain,
    teacher_head,
    student_states,
    student_gain,
    student_head,
    token_ids,
    ffn_gain,
    gate_weight,
    up_weight,
    down_weight,
    token_weight,
):
    core = lax.axis_index("core")
    device = lax.axis_index(AXES)
    own_core = jnp.full((1,), core, jnp.int32)
    x, z, y = (lax.axis_index(line).astype(jnp.int32) for line in ("x", "z", ("yh", "yl")))
    teacher_gain, student_gain, ffn_gain = (
        gain.reshape(-1, 128) for gain in (teacher_gain, student_gain, ffn_gain)
    )
    student_head_t, teacher_head_t = student_head.T, teacher_head.T
    heads = (student_head_t, teacher_head_t)
    gate_t, up_t = gate_weight.T, up_weight.T

    width = sum(WIDTHS)
    half_shape = shape_of((2, width))
    keep, send = kernel_call(
        rows_kernel,
        "rows",
        [half_shape, half_shape],
        limit=56,
        in_specs=[SMEM] + [ANY] * 4,
        out_specs=[VMEM] * 2,
        scratch_shapes=[
            pltpu.VMEM(teacher_states.shape, jnp.bfloat16),
            pltpu.VMEM(student_states.shape, jnp.bfloat16),
            pltpu.VMEM(teacher_gain.shape, jnp.bfloat16),
            pltpu.VMEM(student_gain.shape, jnp.bfloat16),
            pltpu.VMEM((160, 128), jnp.float32),
            pltpu.SemaphoreType.DMA((4,)),
        ],
    )(own_core, teacher_states, teacher_gain, student_states, student_gain)
    (rows,) = in_pair(own_core, keep, swap_cores(send), (width,))

    place = jnp.stack([core, device]).astype(jnp.int32)
    own, send = pick_part(place, token_ids.reshape(1, 256), student_head_t)
    (rows,) = in_pair((y & 1).reshape(1), rows, along(rows, ("yh", "yl"), 1), (width,))
    came = along(rows, ("yh", "yl"), 3)
    came, picked = lax.optimization_barrier((came, join_part(own, swap_cores(send))))
    picked = exchange(picked, CHIPS)
    first, second = in_pair((y >> 1).reshape(1), rows, came, WIDTHS)
    for bit, mask in ((0, 1), (1, 3)):
        came = (along(first, "z", mask), along(second, "x", mask))
        bits = (jnp.stack([z, x]) >> bit) & 1
        first, second = in_pairs(bits, (first, came[0], second, came[1]))
    came = [along(first, "x", 1), along(first, "x", 3), along(second, "z", 1), along(second, "z", 3)]
    came, picked = lax.optimization_barrier((came, picked))
    halves = halves_of(came)
    far = [
        along(half, line, mask)
        for half, line, mask in zip(halves, ("x", "x", "z", "z"), (3, 1, 3, 1))
    ]
    far = lax.optimization_barrier(far)
    rows = (
        whole_rows(x.reshape(1), [first] + came[:2] + far[:2]),
        whole_rows(z.reshape(1), [second] + came[2:] + far[2:]),
    )
    embedded, ffn_rows = kernel_call(
        embed_kernel,
        "embed",
        [shape_of(BLOCK, jnp.float32), shape_of(picked.shape)],
        in_specs=[VMEM] * 2,
        out_specs=[VMEM] * 2,
    )(picked, ffn_gain)
    rows, ffn_rows = lax.optimization_barrier((rows, ffn_rows))
    ffn_rows = exchange(ffn_rows, CHIPS)
    others = tuple(swap_cores(part) for part in rows)
    sums = logits_part(own_core, rows, heads)
    student, teacher, stats = logits_part(1 - own_core, others, heads, sums)
    stats = kernel_call(
        chip_stats_kernel,
        "chip_stats",
        shape_of((64, 8, 128), jnp.float32),
        limit=2,
        in_specs=[VMEM] * 2,
        out_specs=VMEM,
    )(stats, swap_cores(stats))
    every = exchange(stats, CHIPS)

    weight = token_weight.reshape(2, 4, 2, 4, 2, 2).transpose(1, 3, 2, 4, 0, 5).reshape(1, 256)
    own, send, divergence = row_grad_part(
        own_core, every, weight, teacher, student, student_head_t
    )
    divergence = divergence.reshape(4, 4, 2, 2, 2, 2).transpose(4, 0, 2, 1, 3, 5).reshape(256)
    blocks = join_part(own, swap_cores(send))
    (hidden,) = ffn_part(
        gate_kernel, "gate_upper", [shape_of((224, 256), jnp.float32)], ffn_rows, gate_t, up_t
    )
    blocks, hidden = lax.optimization_barrier((blocks, hidden))
    blocks = exchange(blocks, CHIPS)
    final_grad, blocks = kernel_call(
        final_kernel,
        "final",
        [shape_of(BLOCK, jnp.float32), shape_of(blocks.shape)],
        in_specs=[VMEM] * 3,
        out_specs=[VMEM] * 2,
        scratch_shapes=[pltpu.VMEM(BLOCK, jnp.float32)],
    )(blocks, student_states, student_gain)
    blocks = exchange(blocks, CHIPS)
    shape = (128, 4096)
    own, send = ffn_part(
        ffn_grad_kernel,
        "ffn_grad",
        [shape_of(shape, jnp.float32), shape_of(shape)],
        blocks,
        down_weight,
        hidden,
        gate_t,
        up_t,
    )
    ffn_grad = exchange(join_part(own, swap_cores(send)), CHIPS)
    state_grad = kernel_call(
        state_kernel,
        "state",
        shape_of((2, 4096), jnp.float32),
        in_specs=[VMEM] * 4,
        out_specs=VMEM,
    )(ffn_grad, final_grad, embedded, ffn_gain)
    return (divergence, state_grad)


def solution(mesh):
    fine = Mesh(mesh.devices.reshape(SHAPE), AXES)
    in_specs = (
        P(AXES, None),
        P(),
        P(None, AXES),
        P(AXES, None),
        P(),
        P(None, AXES),
        P(),
        P(),
        P(None, AXES),
        P(None, AXES),
        P(AXES, None),
        P(),
    )
    out_specs = (P(), P(AXES, None))
    return jax.shard_map(shards, mesh=fine, in_specs=in_specs, out_specs=out_specs, check_vma=False)
```

```python
import functools

import jax
import jax.numpy as jnp
from jax import lax
from jax.experimental import pallas as pl
from jax.experimental.pallas import tpu as pltpu
from jax.sharding import Mesh
from jax.sharding import PartitionSpec as P

eps = 1e-05
SHAPE = (2, 4, 2, 4, 2)
AXES = ("core", "x", "yh", "z", "yl")
CHIPS = AXES[1:]
MIB = 1024 * 1024

VMEM = pl.BlockSpec(memory_space=pltpu.VMEM)
SMEM = pl.BlockSpec(memory_space=pltpu.SMEM)
ANY = pl.BlockSpec(memory_space=pl.ANY)
SEGMENTS = 8
SEGMENT = 512


def kernel_call(body, name, out_shape, limit=8, **options):
    return pl.pallas_call(
        body,
        name=name,
        out_shape=out_shape,
        compiler_params=pltpu.CompilerParams(vmem_limit_bytes=limit * MIB),
        cost_estimate=pl.CostEstimate(flops=1, bytes_accessed=1, transcendentals=0),
        **options,
    )


def shape_of(shape, dtype=jnp.bfloat16):
    return jax.ShapeDtypeStruct(shape, dtype)


def row_product(left, right):
    return lax.dot_general(
        left, right, (((1,), (1,)), ((), ())), preferred_element_type=jnp.float32
    )


def swap_cores(values):
    return lax.ppermute(values, "core", [(0, 1), (1, 0)])


def exchange(blocks, axes):
    return lax.all_to_all(blocks, axes, split_axis=0, concat_axis=0, tiled=True)


def rows_kernel(
    core_ref, teacher_from, teacher_gain, student_from, student_gain, keep_ref, send_ref,
    teacher_ref, student_ref, teacher_gains, student_gains, gains, sems,
):
    copies = [
        pltpu.make_async_copy(source, target, sems.at[i])
        for i, (source, target) in enumerate(
            (
                (student_gain, student_gains),
                (student_from, student_ref),
                (teacher_gain, teacher_gains),
                (teacher_from, teacher_ref),
            )
        )
    ]
    for copy in copies:
        copy.start()
    for copy in copies:
        copy.wait()
    first = student_gain.shape[0]
    gains[:first, :] = student_gains[...].astype(jnp.float32)
    gains[first:, :] = teacher_gains[...].astype(jnp.float32)
    column = 0
    for values, base in ((student_ref, 0), (teacher_ref, first)):
        half = values.shape[1] // 2
        every = values[...].astype(jnp.float32)
        inverse = lax.rsqrt(jnp.mean(every * every, axis=-1, keepdims=True) + eps)
        for part, out in ((core_ref[0], keep_ref), (1 - core_ref[0], send_ref)):
            for k in range(half // 128):
                place = pl.ds(pl.multiple_of(part * half + k * 128, 128), 128)
                rows = values[:, place].astype(jnp.float32) * inverse
                rows = rows * gains[pl.ds(base + part * (half // 128) + k, 1), :]
                out[:, column + k * 128 : column + (k + 1) * 128] = rows.astype(jnp.bfloat16)
        column = column + half


def pair_kernel(place_ref, own_ref, came_ref, *out_refs):
    own, came = own_ref[...].astype(jnp.float32), came_ref[...].astype(jnp.float32)
    first = place_ref[0] == 0
    rows = jnp.concatenate([jnp.where(first, own, came), jnp.where(first, came, own)], axis=0)
    rows = rows.astype(jnp.bfloat16)
    column = 0
    for out in out_refs:
        out[...] = rows[:, column : column + out.shape[1]]
        column = column + out.shape[1]


def in_pair(bit, own, came, widths):
    tokens = 2 * own.shape[0]
    return kernel_call(
        pair_kernel,
        "pair",
        [shape_of((tokens, w)) for w in widths],
        in_specs=[SMEM] + [VMEM] * 2,
        out_specs=[VMEM] * len(widths),
    )(bit, own, came)


def groups_kernel(place_ref, *refs):
    count = (len(refs) - 1) // 3
    sources, outs, sems = refs[: 2 * count], refs[2 * count : -1], refs[-1]
    copies = []
    for g, out in enumerate(outs):
        for i in range(2):
            source = sources[2 * g + i]
            tokens = source.shape[0]
            at = pl.multiple_of((place_ref[g] ^ i) * tokens, tokens)
            copy = pltpu.make_async_copy(source, out.at[pl.ds(at, tokens), :], sems.at[2 * g + i])
            copy.start()
            copies.append(copy)
    for copy in copies:
        copy.wait()


def in_pairs(bits, parts):
    tokens = 2 * parts[0].shape[0]
    return kernel_call(
        groups_kernel,
        "pairs",
        [shape_of((tokens, part.shape[1])) for part in parts[::2]],
        limit=4,
        in_specs=[SMEM] + [ANY] * len(parts),
        out_specs=[VMEM] * (len(parts) // 2),
        scratch_shapes=[pltpu.SemaphoreType.DMA((len(parts),))],
    )(bits, *parts)


def halves_kernel(*refs):
    count = (len(refs) - 1) // 2
    copies = []
    for i, (piece, out) in enumerate(zip(refs[:count], refs[count:])):
        rows = out.shape[0]
        copy = pltpu.make_async_copy(piece.at[pl.ds((i % 2) * rows, rows), :], out, refs[-1].at[i])
        copy.start()
        copies.append(copy)
    for copy in copies:
        copy.wait()


def halves_of(pieces):
    return kernel_call(
        halves_kernel,
        "halves",
        [shape_of((p.shape[0] // 2, p.shape[1])) for p in pieces],
        limit=4,
        in_specs=[ANY] * len(pieces),
        out_specs=[VMEM] * len(pieces),
        scratch_shapes=[pltpu.SemaphoreType.DMA((len(pieces),))],
    )(*pieces)


def along(block, line, mask):
    return lax.ppermute(block, line, [(i, i ^ mask) for i in range(4)])


def whole_kernel(place_ref, *refs):
    pieces, out, sems = refs[:5], refs[5], refs[6]
    tokens = pieces[0].shape[0]
    copies = []
    for i, (mask, half) in enumerate(((0, 0), (1, 0), (3, 0), (2, 0), (2, 1))):
        at = (place_ref[0] ^ mask) * tokens + half * (tokens // 2)
        at = pl.multiple_of(at, tokens // 2)
        rows = pieces[i].shape[0]
        copy = pltpu.make_async_copy(pieces[i], out.at[pl.ds(at, rows), :], sems.at[i])
        copy.start()
        copies.append(copy)
    for copy in copies:
        copy.wait()


def whole_rows(place, pieces):
    tokens, width = pieces[0].shape
    return kernel_call(
        whole_kernel,
        "whole",
        shape_of((4 * tokens, width)),
        limit=6,
        in_specs=[SMEM] + [ANY] * 5,
        out_specs=VMEM,
        scratch_shapes=[pltpu.SemaphoreType.DMA((5,))],
    )(place, *pieces)


GROUPS = (
    ((0, 0, 2048), (1, 0, 3072)),
    ((1, 3072, 2560), (1, 5632, 2560)),
)
WIDTHS = tuple(sum(p[2] for p in group) for group in GROUPS)


def reordered(values):
    source = lax.broadcasted_iota(jnp.int32, (256, 256), 0)
    place = lax.broadcasted_iota(jnp.int32, (256, 256), 1)
    wanted = (((place >> 4) & 3) << 6) | (((place >> 6) & 3) << 4) | (place & 15)
    moves = (source == wanted).astype(jnp.bfloat16)
    high = values.astype(jnp.bfloat16)
    rest = values - high.astype(jnp.float32)
    middle = rest.astype(jnp.bfloat16)
    low = (rest - middle.astype(jnp.float32)).astype(jnp.bfloat16)
    high, middle, low = (
        jnp.dot(part, moves, preferred_element_type=jnp.float32) for part in (high, middle, low)
    )
    return (high + middle) + low


def softmax_stats(teacher, student, stats_out):
    teacher_peak = jnp.max(teacher, axis=0, keepdims=True)
    student_peak = jnp.max(student, axis=0, keepdims=True)
    teacher_exp = jnp.exp(teacher - teacher_peak)
    teacher_total = jnp.sum(teacher_exp, axis=0, keepdims=True)
    student_total = jnp.sum(jnp.exp(student - student_peak), axis=0, keepdims=True)
    cross = jnp.sum(teacher_exp * (teacher - student), axis=0, keepdims=True)
    stats = (
        teacher_peak + jnp.log(teacher_total),
        student_peak + jnp.log(student_total),
        cross / teacher_total,
    )
    rows = [row[:, :128] for row in stats] + [row[:, 128:] for row in stats]
    stats_out[...] = jnp.concatenate(rows + [jnp.zeros((2, 128), jnp.float32)], axis=0)


def logits_kernel(last, place_ref, *refs):
    rows_from, heads, refs = refs[:2], refs[2:4], refs[4:]
    rows, head, row_sems, head_sems = refs[-4:]
    refs = refs[:-4]
    copies = []
    column = 0
    for group, source in zip(GROUPS, rows_from):
        base = column
        for kind, start, width in group:
            i = len(copies)
            columns = slice(column, column + width)
            size = heads[kind].shape[1] // 2
            start = pl.multiple_of(place_ref[0] * size + start, 128)
            pair = (
                pltpu.make_async_copy(
                    source.at[:, column - base : column - base + width],
                    rows.at[:, columns],
                    row_sems.at[i],
                ),
                pltpu.make_async_copy(
                    heads[kind].at[:, pl.ds(start, width)], head.at[:, columns], head_sems.at[i]
                ),
            )
            copies.append((kind + (base > 0), columns, pair))
            column = column + width
    ahead = 2
    for _, _, pair in copies[:ahead]:
        for copy in pair:
            copy.start()
    sums = [None, None, None]
    for i, (kind, columns, pair) in enumerate(copies):
        for copy in pair:
            copy.wait()
        if i + ahead < len(copies):
            for copy in copies[i + ahead][2]:
                copy.start()
        term = row_product(head[:, columns], rows[:, columns])
        sums[kind] = term if sums[kind] is None else sums[kind] + term
    if last:
        came, (student_out, teacher_out, stats_out) = refs[:3], refs[3:]
        student, teacher, second = (total + ref[...] for total, ref in zip(sums, came))
        teacher = teacher + reordered(second)
        student_out[...] = student
        teacher_out[...] = teacher
        softmax_stats(teacher, student, stats_out)
    else:
        for total, out in zip(sums, refs):
            out[...] = total


def logits_part(place, rows, heads, sums=()):
    vocab, tokens = heads[1].shape[0], rows[0].shape[0]
    shape = shape_of((vocab, tokens), jnp.float32)
    last = len(sums) > 0
    pieces = sum(len(group) for group in GROUPS)
    out_shape = [shape, shape, shape_of((8, 128), jnp.float32) if last else shape]
    return kernel_call(
        functools.partial(logits_kernel, last),
        "logits",
        out_shape,
        limit=48,
        in_specs=[SMEM] + [ANY] * 4 + [VMEM] * len(sums),
        out_specs=[VMEM] * 3,
        scratch_shapes=[
            pltpu.VMEM((tokens, sum(WIDTHS)), jnp.bfloat16),
            pltpu.VMEM((vocab, sum(WIDTHS)), jnp.bfloat16),
            pltpu.SemaphoreType.DMA((pieces,)),
            pltpu.SemaphoreType.DMA((pieces,)),
        ],
    )(place, *rows, *heads, *sums)


def one_hot_rows(core):
    place = lax.broadcasted_iota(jnp.int32, (256, 256), 0)
    column = lax.broadcasted_iota(jnp.int32, (256, 256), 1)
    x, yh, z, yl = (place >> 4) & 3, (place >> 3) & 1, (place >> 1) & 3, place & 1
    source = (x << 6) | (z << 4) | (yh << 3) | (yl << 2)
    source = source | (((place >> 7) ^ core) << 1) | ((place >> 6) & 1)
    return (column == source).astype(jnp.bfloat16)


def head_copies(source, head, sems):
    columns = head.shape[1] // sems.shape[0]
    parts = [slice(i * columns, (i + 1) * columns) for i in range(sems.shape[0])]
    copies = [
        pltpu.make_async_copy(source.at[:, part], head.at[:, part], sems.at[i])
        for i, part in enumerate(parts)
    ]
    for copy in copies:
        copy.start()
    return list(zip(parts, copies))


def merged_stats(every):
    peak = jnp.max(every, axis=0)
    scaled = jnp.exp(every - peak[None])
    total = jnp.sum(scaled, axis=0)
    cross = jnp.sum(scaled * pltpu.roll(every, 6, 1), axis=0) / total
    return peak + jnp.log(total), cross


def chip_stats_kernel(own_ref, came_ref, out_ref):
    lse, cross = merged_stats(jnp.concatenate([own_ref[...][None], came_ref[...][None]], axis=0))
    row = lax.broadcasted_iota(jnp.int32, lse.shape, 0)
    merged = jnp.where((row == 2) | (row == 5), pltpu.roll(cross, 2, 0), lse)
    out_ref[...] = jnp.broadcast_to(merged[None], out_ref.shape)


def row_grad_kernel(
    core_ref, every_ref, weight_ref, teacher_ref, student_ref, head_from,
    own_ref, send_ref, divergence_ref, head, sems,
):
    copies = head_copies(head_from, head, sems)
    lse, cross = merged_stats(every_ref[...])
    teacher_lse = jnp.concatenate([lse[0:1], lse[3:4]], axis=1)
    student_lse = jnp.concatenate([lse[1:2], lse[4:5]], axis=1)
    divergence_ref[...] = (
        jnp.concatenate([cross[0:1], cross[3:4]], axis=1) - teacher_lse + student_lse
    )
    logit_grad = weight_ref[...] * (
        jnp.exp(student_ref[...] - student_lse) - jnp.exp(teacher_ref[...] - teacher_lse)
    )
    grad = row_product(one_hot_rows(core_ref[0]), logit_grad.astype(jnp.bfloat16))
    grad = grad.astype(jnp.bfloat16)
    half = own_ref.shape[0]
    for columns, copy in copies:
        copy.wait()
        out = jnp.dot(grad, head[:, columns], preferred_element_type=jnp.float32)
        own_ref[:, columns] = out[:half]
        send_ref[:, columns] = out[half:].astype(jnp.bfloat16)


def row_grad_part(core, every, weight, teacher, student, student_head_t):
    vocab, width = student_head_t.shape
    tokens = weight.shape[1]
    return kernel_call(
        row_grad_kernel,
        "row_grad",
        [
            shape_of((tokens // 2, width), jnp.float32),
            shape_of((tokens // 2, width)),
            shape_of((1, tokens), jnp.float32),
        ],
        limit=48,
        in_specs=[SMEM] + [VMEM] * 4 + [ANY],
        out_specs=[VMEM] * 3,
        scratch_shapes=[
            pltpu.VMEM((vocab, width), jnp.bfloat16),
            pltpu.SemaphoreType.DMA((4,)),
        ],
    )(core, every, weight, teacher, student, student_head_t)


def pick_kernel(device_ref, ids_ref, head_from, out_ref, head, sems):
    copies = head_copies(head_from, head, sems)
    vocab, tokens = head.shape[0], ids_ref.shape[1]
    entry = lax.broadcasted_iota(jnp.int32, (vocab, tokens), 0) + device_ref[0] * vocab
    place = lax.broadcasted_iota(jnp.int32, (tokens, tokens), 0)
    column = lax.broadcasted_iota(jnp.int32, (tokens, tokens), 1)
    source = (place & 128) | ((place & 63) << 1) | ((place >> 6) & 1)
    chosen = row_product(
        (column == source).astype(jnp.bfloat16), (ids_ref[...] == entry).astype(jnp.bfloat16)
    ).astype(jnp.bfloat16)
    for columns, copy in copies:
        copy.wait()
        out_ref[:, columns] = jnp.dot(
            chosen, head[:, columns], preferred_element_type=jnp.float32
        )


def pick_part(device, ids, student_head_t):
    vocab, width = student_head_t.shape
    return kernel_call(
        pick_kernel,
        "pick",
        shape_of((ids.shape[1], width), jnp.float32),
        limit=48,
        in_specs=[SMEM, VMEM, ANY],
        out_specs=VMEM,
        scratch_shapes=[
            pltpu.VMEM((vocab, width), jnp.bfloat16),
            pltpu.SemaphoreType.DMA((4,)),
        ],
    )(device, ids, student_head_t)


def join_kernel(*refs):
    pairs, out_ref, rows = refs[:-2], refs[-2], refs[-1]
    chips, height = out_ref.shape[0], 2 * SEGMENTS
    for base, (own_ref, came_ref) in enumerate(zip(pairs[::2], pairs[1::2])):
        for t in range(2):
            for i in range(SEGMENTS):
                for k in range(SEGMENT // 128):
                    part = slice(t * chips, (t + 1) * chips)
                    lanes = slice(i * SEGMENT + k * 128, i * SEGMENT + (k + 1) * 128)
                    total = own_ref[part, lanes].astype(jnp.float32)
                    total = total + came_ref[part, lanes].astype(jnp.float32)
                    at = pl.ds(t * SEGMENTS + i, chips, stride=height)
                    rows[k, at, :] = total
        for k in range(SEGMENT // 128):
            out_ref[:, base * height : (base + 1) * height, k * 128 : (k + 1) * 128] = (
                rows[k].reshape(chips, height, 128).astype(jnp.bfloat16)
            )


def join_part(*pairs):
    chips = pairs[0].shape[0] // 2
    height = 2 * SEGMENTS
    return kernel_call(
        join_kernel,
        "join",
        shape_of((chips, height * len(pairs) // 2, SEGMENT)),
        limit=14,
        in_specs=[VMEM] * len(pairs),
        out_specs=VMEM,
        scratch_shapes=[pltpu.VMEM((SEGMENT // 128, chips * height, 128), jnp.float32)],
    )(*pairs)


def block_gain(gain_ref):
    gain = gain_ref[...].astype(jnp.float32)
    lanes = SEGMENT // 128
    token = jnp.concatenate(
        [
            jnp.concatenate([gain[lanes * i + k : lanes * i + k + 1] for k in range(lanes)], axis=1)
            for i in range(SEGMENTS)
        ],
        axis=0,
    )
    return jnp.concatenate([token, token], axis=0)


def block_mean(values):
    means = []
    for t in range(2):
        part = values[t * SEGMENTS : (t + 1) * SEGMENTS]
        total = jnp.sum(jnp.sum(part, axis=0, keepdims=True), axis=1, keepdims=True)
        means.append(jnp.broadcast_to(total / (SEGMENTS * SEGMENT), (SEGMENTS, 1)))
    return jnp.concatenate(means, axis=0)


def block_inverse(values):
    return lax.rsqrt(block_mean(values * values) + eps)


def block_back(upstream, values, gain):
    inverse = block_inverse(values)
    gained = upstream * gain
    return inverse * gained - values * inverse**3 * block_mean(gained * values)


def block_sum(blocks_ref):
    return jnp.sum(blocks_ref[...].astype(jnp.float32), axis=0)


def final_kernel(blocks_ref, states_ref, gain_ref, grad_ref, out_ref, states):
    for i in range(SEGMENTS):
        part = states_ref[:, i * SEGMENT : (i + 1) * SEGMENT].astype(jnp.float32)
        for t in range(2):
            states[t * SEGMENTS + i : t * SEGMENTS + i + 1, :] = part[t : t + 1]
    grad = block_back(block_sum(blocks_ref), states[...], block_gain(gain_ref))
    grad_ref[...] = grad
    out_ref[...] = jnp.broadcast_to(grad.astype(jnp.bfloat16)[None], out_ref.shape)


def state_kernel(blocks_ref, grad_ref, embedded_ref, gain_ref, out_ref):
    back = block_back(block_sum(blocks_ref), embedded_ref[...], block_gain(gain_ref))
    grad = grad_ref[...] + back
    for t in range(2):
        for i in range(SEGMENTS):
            out_ref[t : t + 1, i * SEGMENT : (i + 1) * SEGMENT] = grad[
                t * SEGMENTS + i : t * SEGMENTS + i + 1
            ]


BLOCK = (2 * SEGMENTS, SEGMENT)


def spread_rows(refs, scratches):
    for ref, rows in zip(refs, scratches):
        values = ref[...].astype(jnp.float32)
        values = values.reshape(values.shape[0] * values.shape[1], values.shape[2])
        for k in range(SEGMENT // 128):
            rows[k] = values[:, k * 128 : (k + 1) * 128]


def segment_rows(scratches, segment):
    parts = []
    for rows in scratches:
        height = 2 * SEGMENTS
        for t in range(2):
            at = pl.ds(t * SEGMENTS + segment, rows.shape[1] // height, stride=height)
            parts.append(
                jnp.concatenate([rows[k, at, :] for k in range(SEGMENT // 128)], axis=1)
            )
    return jnp.concatenate(parts, axis=0).astype(jnp.bfloat16)


def gate_kernel(place_ref, embedded_ref, gain_ref, gate_ref, up_ref, hidden_ref, own_ref):
    core, chip = place_ref[0], place_ref[1]
    embedded = embedded_ref[...]
    inverse = lax.rsqrt(jnp.mean(embedded * embedded, axis=1, keepdims=True) + eps)
    gain = gain_ref[...].astype(jnp.float32)
    lanes = SEGMENT // 128
    hidden = None
    for i in range(SEGMENTS):
        part = [gain[lanes * i + k : lanes * i + k + 1] for k in range(lanes)]
        columns = slice(i * SEGMENT, (i + 1) * SEGMENT)
        rows = embedded_ref[:, columns] * inverse * jnp.concatenate(part, axis=1)
        weight = jnp.concatenate([gate_ref[:, columns], up_ref[:, columns]], axis=0)
        term = row_product(weight, rows.astype(jnp.bfloat16))
        hidden = term if hidden is None else hidden + term
    low, high = hidden[:, :128], hidden[:, 128:]
    hidden_ref[:, :128] = jnp.where(core == 0, low, high)
    hidden_ref[:, 128:] = jnp.where(core == 0, high, low)
    for t in range(2):
        base = pl.multiple_of(core * 128 + t * 64 + (chip >> 3) * 8, 8)
        rows = embedded_ref[pl.ds(base, 8), :]
        mine = lax.broadcasted_iota(jnp.int32, rows.shape, 0) == (chip & 7)
        row = jnp.sum(jnp.where(mine, rows, 0.0), axis=0, keepdims=True)
        for i in range(SEGMENTS):
            own_ref[t * SEGMENTS + i : t * SEGMENTS + i + 1, :] = row[
                :, i * SEGMENT : (i + 1) * SEGMENT
            ]


def ffn_grad_kernel(
    own_ref, other_ref, down_ref, hidden_ref, gate_ref, up_ref, own_out, send_out, *scratches
):
    spread_rows((own_ref, other_ref), scratches)
    units = down_ref.shape[0]
    hidden, act_grad = hidden_ref[...], None
    for i in range(SEGMENTS):
        columns = slice(i * SEGMENT, (i + 1) * SEGMENT)
        term = row_product(down_ref[:, columns], segment_rows(scratches, i))
        act_grad = term if act_grad is None else act_grad + term
    gate, upper = hidden[:units, :], hidden[units:, :]
    sigmoid_gate = jax.nn.sigmoid(gate)
    gate_grad = act_grad * upper * sigmoid_gate * (1.0 + gate * (1.0 - sigmoid_gate))
    upper_grad = act_grad * gate * sigmoid_gate
    grads = jnp.concatenate([gate_grad, upper_grad], axis=0).astype(jnp.bfloat16)
    tokens = grads.shape[1]
    same = lax.broadcasted_iota(jnp.int32, (tokens, tokens), 0) == lax.broadcasted_iota(
        jnp.int32, (tokens, tokens), 1
    )
    grads = row_product(same.astype(jnp.bfloat16), grads).astype(jnp.bfloat16)
    for i in range(SEGMENTS):
        columns = slice(i * SEGMENT, (i + 1) * SEGMENT)
        weight = jnp.concatenate([gate_ref[:, columns], up_ref[:, columns]], axis=0)
        out = jnp.dot(grads, weight, preferred_element_type=jnp.float32)
        own_out[:, columns] = out[: tokens // 2]
        send_out[:, columns] = out[tokens // 2 :].astype(jnp.bfloat16)


def ffn_part(body, name, out_shape, blocks, *others):
    rows = blocks.shape[0] * blocks.shape[1]
    scratch = pltpu.VMEM((SEGMENT // 128, rows, 128), jnp.float32)
    return kernel_call(
        body,
        name,
        out_shape,
        limit=20,
        in_specs=[VMEM] * (2 + len(others)),
        out_specs=[VMEM] * len(out_shape),
        scratch_shapes=[scratch, scratch],
    )(blocks, swap_cores(blocks), *others)


def shards(
    teacher_states,
    teacher_gain,
    teacher_head,
    student_states,
    student_gain,
    student_head,
    token_ids,
    ffn_gain,
    gate_weight,
    up_weight,
    down_weight,
    token_weight,
):
    core = lax.axis_index("core")
    device = lax.axis_index(AXES)
    own_core = jnp.full((1,), core, jnp.int32)
    x, z, y = (lax.axis_index(line).astype(jnp.int32) for line in ("x", "z", ("yh", "yl")))
    teacher_gain, student_gain, ffn_gain = (
        gain.reshape(-1, 128) for gain in (teacher_gain, student_gain, ffn_gain)
    )
    student_head_t, teacher_head_t = student_head.T, teacher_head.T
    heads = (student_head_t, teacher_head_t)
    gate_t, up_t = gate_weight.T, up_weight.T

    width = sum(WIDTHS)
    half_shape = shape_of((2, width))
    keep, send = kernel_call(
        rows_kernel,
        "rows",
        [half_shape, half_shape],
        limit=56,
        in_specs=[SMEM] + [ANY] * 4,
        out_specs=[VMEM] * 2,
        scratch_shapes=[
            pltpu.VMEM(teacher_states.shape, jnp.bfloat16),
            pltpu.VMEM(student_states.shape, jnp.bfloat16),
            pltpu.VMEM(teacher_gain.shape, jnp.bfloat16),
            pltpu.VMEM(student_gain.shape, jnp.bfloat16),
            pltpu.VMEM((160, 128), jnp.float32),
            pltpu.SemaphoreType.DMA((4,)),
        ],
    )(own_core, teacher_states, teacher_gain, student_states, student_gain)
    (rows,) = in_pair(own_core, keep, swap_cores(send), (width,))

    ids = token_ids.reshape(1, 256)
    picked = pick_part(device.reshape(1).astype(jnp.int32), ids, student_head_t)
    rows, picked = lax.optimization_barrier((rows, picked))
    embedded = lax.psum(picked, AXES)

    (rows,) = in_pair((y & 1).reshape(1), rows, along(rows, ("yh", "yl"), 1), (width,))
    first, second = in_pair((y >> 1).reshape(1), rows, along(rows, ("yh", "yl"), 3), WIDTHS)
    for bit, mask in ((0, 1), (1, 3)):
        came = (along(first, "z", mask), along(second, "x", mask))
        bits = (jnp.stack([z, x]) >> bit) & 1
        first, second = in_pairs(bits, (first, came[0], second, came[1]))
    came = [along(first, "x", 1), along(first, "x", 3), along(second, "z", 1), along(second, "z", 3)]
    came = lax.optimization_barrier(came)
    halves = halves_of(came)
    far = [
        along(half, line, mask)
        for half, line, mask in zip(halves, ("x", "x", "z", "z"), (3, 1, 3, 1))
    ]
    far = lax.optimization_barrier(far)
    rows = (
        whole_rows(x.reshape(1), [first] + came[:2] + far[:2]),
        whole_rows(z.reshape(1), [second] + came[2:] + far[2:]),
    )
    others = tuple(swap_cores(part) for part in rows)
    sums = logits_part(own_core, rows, heads)
    student, teacher, stats = logits_part(1 - own_core, others, heads, sums)
    stats = kernel_call(
        chip_stats_kernel,
        "chip_stats",
        shape_of((64, 8, 128), jnp.float32),
        limit=2,
        in_specs=[VMEM] * 2,
        out_specs=VMEM,
    )(stats, swap_cores(stats))
    every = exchange(stats, CHIPS)

    weight = token_weight.reshape(2, 4, 2, 4, 2, 2).transpose(1, 3, 2, 4, 0, 5).reshape(1, 256)
    own, send, divergence = row_grad_part(
        own_core, every, weight, teacher, student, student_head_t
    )
    divergence = divergence.reshape(4, 4, 2, 2, 2, 2).transpose(4, 0, 2, 1, 3, 5).reshape(256)
    blocks = join_part(own, swap_cores(send))
    blocks = exchange(blocks, CHIPS)
    final_grad, blocks = kernel_call(
        final_kernel,
        "final",
        [shape_of(BLOCK, jnp.float32), shape_of(blocks.shape)],
        in_specs=[VMEM] * 3,
        out_specs=[VMEM] * 2,
        scratch_shapes=[pltpu.VMEM(BLOCK, jnp.float32)],
    )(blocks, student_states, student_gain)
    blocks = exchange(blocks, CHIPS)
    place = jnp.stack([core, lax.axis_index(CHIPS)]).astype(jnp.int32)
    hidden, embedded = kernel_call(
        gate_kernel,
        "gate_upper",
        [shape_of((2 * gate_t.shape[0], 256), jnp.float32), shape_of(BLOCK, jnp.float32)],
        limit=24,
        in_specs=[SMEM] + [VMEM] * 4,
        out_specs=[VMEM] * 2,
    )(place, embedded, ffn_gain, gate_t, up_t)
    shape = (128, 4096)
    own, send = ffn_part(
        ffn_grad_kernel,
        "ffn_grad",
        [shape_of(shape, jnp.float32), shape_of(shape)],
        blocks,
        down_weight,
        hidden,
        gate_t,
        up_t,
    )
    ffn_grad = exchange(join_part(own, swap_cores(send)), CHIPS)
    state_grad = kernel_call(
        state_kernel,
        "state",
        shape_of((2, 4096), jnp.float32),
        in_specs=[VMEM] * 4,
        out_specs=VMEM,
    )(ffn_grad, final_grad, embedded, ffn_gain)
    return (divergence, state_grad)


def solution(mesh):
    fine = Mesh(mesh.devices.reshape(SHAPE), AXES)
    in_specs = (
        P(AXES, None),
        P(),
        P(None, AXES),
        P(AXES, None),
        P(),
        P(None, AXES),
        P(),
        P(),
        P(None, AXES),
        P(None, AXES),
        P(AXES, None),
        P(),
    )
    out_specs = (P(), P(AXES, None))
    return jax.shard_map(shards, mesh=fine, in_specs=in_specs, out_specs=out_specs, check_vma=False)
```

```python
import functools

import jax
import jax.numpy as jnp
from jax import lax
from jax.experimental import pallas as pl
from jax.experimental.pallas import tpu as pltpu
from jax.sharding import Mesh
from jax.sharding import PartitionSpec as P

eps = 1e-05
SHAPE = (2, 4, 2, 4, 2)
AXES = ("core", "x", "yh", "z", "yl")
CHIPS = AXES[1:]
MIB = 1024 * 1024

VMEM = pl.BlockSpec(memory_space=pltpu.VMEM)
SMEM = pl.BlockSpec(memory_space=pltpu.SMEM)
ANY = pl.BlockSpec(memory_space=pl.ANY)
SEGMENTS = 8
SEGMENT = 512


def kernel_call(body, name, out_shape, limit=8, **options):
    return pl.pallas_call(
        body,
        name=name,
        out_shape=out_shape,
        compiler_params=pltpu.CompilerParams(vmem_limit_bytes=limit * MIB),
        cost_estimate=pl.CostEstimate(flops=1, bytes_accessed=1, transcendentals=0),
        **options,
    )


def shape_of(shape, dtype=jnp.bfloat16):
    return jax.ShapeDtypeStruct(shape, dtype)


def row_product(left, right):
    return lax.dot_general(
        left, right, (((1,), (1,)), ((), ())), preferred_element_type=jnp.float32
    )


def swap_cores(values):
    return lax.ppermute(values, "core", [(0, 1), (1, 0)])


def exchange(blocks, axes):
    return lax.all_to_all(blocks, axes, split_axis=0, concat_axis=0, tiled=True)


def rows_kernel(
    core_ref, teacher_from, teacher_gain, student_from, student_gain, keep_ref, send_ref,
    teacher_ref, student_ref, teacher_gains, student_gains, gains, sems,
):
    copies = [
        pltpu.make_async_copy(source, target, sems.at[i])
        for i, (source, target) in enumerate(
            (
                (student_gain, student_gains),
                (student_from, student_ref),
                (teacher_gain, teacher_gains),
                (teacher_from, teacher_ref),
            )
        )
    ]
    for copy in copies:
        copy.start()
    for copy in copies:
        copy.wait()
    first = student_gain.shape[0]
    gains[:first, :] = student_gains[...].astype(jnp.float32)
    gains[first:, :] = teacher_gains[...].astype(jnp.float32)
    column = 0
    for values, base in ((student_ref, 0), (teacher_ref, first)):
        half = values.shape[1] // 2
        every = values[...].astype(jnp.float32)
        inverse = lax.rsqrt(jnp.mean(every * every, axis=-1, keepdims=True) + eps)
        for part, out in ((core_ref[0], keep_ref), (1 - core_ref[0], send_ref)):
            for k in range(half // 128):
                place = pl.ds(pl.multiple_of(part * half + k * 128, 128), 128)
                rows = values[:, place].astype(jnp.float32) * inverse
                rows = rows * gains[pl.ds(base + part * (half // 128) + k, 1), :]
                out[:, column + k * 128 : column + (k + 1) * 128] = rows.astype(jnp.bfloat16)
        column = column + half


def pair_kernel(place_ref, own_ref, came_ref, *out_refs):
    own, came = own_ref[...].astype(jnp.float32), came_ref[...].astype(jnp.float32)
    first = place_ref[0] == 0
    rows = jnp.concatenate([jnp.where(first, own, came), jnp.where(first, came, own)], axis=0)
    rows = rows.astype(jnp.bfloat16)
    column = 0
    for out in out_refs:
        out[...] = rows[:, column : column + out.shape[1]]
        column = column + out.shape[1]


def in_pair(bit, own, came, widths):
    tokens = 2 * own.shape[0]
    return kernel_call(
        pair_kernel,
        "pair",
        [shape_of((tokens, w)) for w in widths],
        in_specs=[SMEM] + [VMEM] * 2,
        out_specs=[VMEM] * len(widths),
    )(bit, own, came)


def groups_kernel(place_ref, *refs):
    count = (len(refs) - 1) // 3
    sources, outs, sems = refs[: 2 * count], refs[2 * count : -1], refs[-1]
    copies = []
    for g, out in enumerate(outs):
        for i in range(2):
            source = sources[2 * g + i]
            tokens = source.shape[0]
            at = pl.multiple_of((place_ref[g] ^ i) * tokens, tokens)
            copy = pltpu.make_async_copy(source, out.at[pl.ds(at, tokens), :], sems.at[2 * g + i])
            copy.start()
            copies.append(copy)
    for copy in copies:
        copy.wait()


def in_pairs(bits, parts):
    tokens = 2 * parts[0].shape[0]
    return kernel_call(
        groups_kernel,
        "pairs",
        [shape_of((tokens, part.shape[1])) for part in parts[::2]],
        limit=4,
        in_specs=[SMEM] + [ANY] * len(parts),
        out_specs=[VMEM] * (len(parts) // 2),
        scratch_shapes=[pltpu.SemaphoreType.DMA((len(parts),))],
    )(bits, *parts)


def halves_kernel(*refs):
    count = (len(refs) - 1) // 2
    copies = []
    for i, (piece, out) in enumerate(zip(refs[:count], refs[count:])):
        rows = out.shape[0]
        copy = pltpu.make_async_copy(piece.at[pl.ds((i % 2) * rows, rows), :], out, refs[-1].at[i])
        copy.start()
        copies.append(copy)
    for copy in copies:
        copy.wait()


def halves_of(pieces):
    return kernel_call(
        halves_kernel,
        "halves",
        [shape_of((p.shape[0] // 2, p.shape[1])) for p in pieces],
        limit=4,
        in_specs=[ANY] * len(pieces),
        out_specs=[VMEM] * len(pieces),
        scratch_shapes=[pltpu.SemaphoreType.DMA((len(pieces),))],
    )(*pieces)


def along(block, line, mask):
    return lax.ppermute(block, line, [(i, i ^ mask) for i in range(4)])


def whole_kernel(place_ref, *refs):
    pieces, out, sems = refs[:5], refs[5], refs[6]
    tokens = pieces[0].shape[0]
    copies = []
    for i, (mask, half) in enumerate(((0, 0), (1, 0), (3, 0), (2, 0), (2, 1))):
        at = (place_ref[0] ^ mask) * tokens + half * (tokens // 2)
        at = pl.multiple_of(at, tokens // 2)
        rows = pieces[i].shape[0]
        copy = pltpu.make_async_copy(pieces[i], out.at[pl.ds(at, rows), :], sems.at[i])
        copy.start()
        copies.append(copy)
    for copy in copies:
        copy.wait()


def whole_rows(place, pieces):
    tokens, width = pieces[0].shape
    return kernel_call(
        whole_kernel,
        "whole",
        shape_of((4 * tokens, width)),
        limit=6,
        in_specs=[SMEM] + [ANY] * 5,
        out_specs=VMEM,
        scratch_shapes=[pltpu.SemaphoreType.DMA((5,))],
    )(place, *pieces)


GROUPS = (
    ((0, 0, 2048), (1, 0, 3072)),
    ((1, 3072, 2560), (1, 5632, 2560)),
)
WIDTHS = tuple(sum(p[2] for p in group) for group in GROUPS)


def reordered(values):
    source = lax.broadcasted_iota(jnp.int32, (256, 256), 0)
    place = lax.broadcasted_iota(jnp.int32, (256, 256), 1)
    wanted = (((place >> 4) & 3) << 6) | (((place >> 6) & 3) << 4) | (place & 15)
    moves = (source == wanted).astype(jnp.bfloat16)
    high = values.astype(jnp.bfloat16)
    rest = values - high.astype(jnp.float32)
    middle = rest.astype(jnp.bfloat16)
    low = (rest - middle.astype(jnp.float32)).astype(jnp.bfloat16)
    high, middle, low = (
        jnp.dot(part, moves, preferred_element_type=jnp.float32) for part in (high, middle, low)
    )
    return (high + middle) + low


def softmax_stats(teacher, student, stats_out):
    teacher_peak = jnp.max(teacher, axis=0, keepdims=True)
    student_peak = jnp.max(student, axis=0, keepdims=True)
    teacher_exp = jnp.exp(teacher - teacher_peak)
    teacher_total = jnp.sum(teacher_exp, axis=0, keepdims=True)
    student_total = jnp.sum(jnp.exp(student - student_peak), axis=0, keepdims=True)
    cross = jnp.sum(teacher_exp * (teacher - student), axis=0, keepdims=True)
    stats = (
        teacher_peak + jnp.log(teacher_total),
        student_peak + jnp.log(student_total),
        cross / teacher_total,
    )
    rows = [row[:, :128] for row in stats] + [row[:, 128:] for row in stats]
    stats_out[...] = jnp.concatenate(rows + [jnp.zeros((2, 128), jnp.float32)], axis=0)


def logits_kernel(last, place_ref, *refs):
    rows_from, heads, refs = refs[:2], refs[2:4], refs[4:]
    rows, head, row_sems, head_sems = refs[-4:]
    refs = refs[:-4]
    copies = []
    column = 0
    for group, source in zip(GROUPS, rows_from):
        base = column
        for kind, start, width in group:
            i = len(copies)
            columns = slice(column, column + width)
            size = heads[kind].shape[1] // 2
            start = pl.multiple_of(place_ref[0] * size + start, 128)
            pair = (
                pltpu.make_async_copy(
                    source.at[:, column - base : column - base + width],
                    rows.at[:, columns],
                    row_sems.at[i],
                ),
                pltpu.make_async_copy(
                    heads[kind].at[:, pl.ds(start, width)], head.at[:, columns], head_sems.at[i]
                ),
            )
            copies.append((kind + (base > 0), columns, pair))
            column = column + width
    ahead = 2
    for _, _, pair in copies[:ahead]:
        for copy in pair:
            copy.start()
    sums = [None, None, None]
    for i, (kind, columns, pair) in enumerate(copies):
        for copy in pair:
            copy.wait()
        if i + ahead < len(copies):
            for copy in copies[i + ahead][2]:
                copy.start()
        term = row_product(head[:, columns], rows[:, columns])
        sums[kind] = term if sums[kind] is None else sums[kind] + term
    if last:
        came, (student_out, teacher_out, stats_out) = refs[:3], refs[3:]
        student, teacher, second = (total + ref[...] for total, ref in zip(sums, came))
        teacher = teacher + reordered(second)
        student_out[...] = student
        teacher_out[...] = teacher
        softmax_stats(teacher, student, stats_out)
    else:
        for total, out in zip(sums, refs):
            out[...] = total


def logits_part(place, rows, heads, sums=()):
    vocab, tokens = heads[1].shape[0], rows[0].shape[0]
    shape = shape_of((vocab, tokens), jnp.float32)
    last = len(sums) > 0
    pieces = sum(len(group) for group in GROUPS)
    out_shape = [shape, shape, shape_of((8, 128), jnp.float32) if last else shape]
    return kernel_call(
        functools.partial(logits_kernel, last),
        "logits",
        out_shape,
        limit=48,
        in_specs=[SMEM] + [ANY] * 4 + [VMEM] * len(sums),
        out_specs=[VMEM] * 3,
        scratch_shapes=[
            pltpu.VMEM((tokens, sum(WIDTHS)), jnp.bfloat16),
            pltpu.VMEM((vocab, sum(WIDTHS)), jnp.bfloat16),
            pltpu.SemaphoreType.DMA((pieces,)),
            pltpu.SemaphoreType.DMA((pieces,)),
        ],
    )(place, *rows, *heads, *sums)


def one_hot_rows(core):
    place = lax.broadcasted_iota(jnp.int32, (256, 256), 0)
    column = lax.broadcasted_iota(jnp.int32, (256, 256), 1)
    x, yh, z, yl = (place >> 4) & 3, (place >> 3) & 1, (place >> 1) & 3, place & 1
    source = (x << 6) | (z << 4) | (yh << 3) | (yl << 2)
    source = source | (((place >> 7) ^ core) << 1) | ((place >> 6) & 1)
    return (column == source).astype(jnp.bfloat16)


def head_copies(source, head, sems):
    columns = head.shape[1] // sems.shape[0]
    parts = [slice(i * columns, (i + 1) * columns) for i in range(sems.shape[0])]
    copies = [
        pltpu.make_async_copy(source.at[:, part], head.at[:, part], sems.at[i])
        for i, part in enumerate(parts)
    ]
    for copy in copies:
        copy.start()
    return list(zip(parts, copies))


def merged_stats(every):
    peak = jnp.max(every, axis=0)
    scaled = jnp.exp(every - peak[None])
    total = jnp.sum(scaled, axis=0)
    cross = jnp.sum(scaled * pltpu.roll(every, 6, 1), axis=0) / total
    return peak + jnp.log(total), cross


def chip_stats_kernel(own_ref, came_ref, out_ref):
    lse, cross = merged_stats(jnp.concatenate([own_ref[...][None], came_ref[...][None]], axis=0))
    row = lax.broadcasted_iota(jnp.int32, lse.shape, 0)
    merged = jnp.where((row == 2) | (row == 5), pltpu.roll(cross, 2, 0), lse)
    out_ref[...] = jnp.broadcast_to(merged[None], out_ref.shape)


def row_grad_kernel(
    core_ref, every_ref, weight_ref, teacher_ref, student_ref, head_from,
    own_ref, send_ref, divergence_ref, head, sems,
):
    copies = head_copies(head_from, head, sems)
    lse, cross = merged_stats(every_ref[...])
    teacher_lse = jnp.concatenate([lse[0:1], lse[3:4]], axis=1)
    student_lse = jnp.concatenate([lse[1:2], lse[4:5]], axis=1)
    divergence_ref[...] = (
        jnp.concatenate([cross[0:1], cross[3:4]], axis=1) - teacher_lse + student_lse
    )
    logit_grad = weight_ref[...] * (
        jnp.exp(student_ref[...] - student_lse) - jnp.exp(teacher_ref[...] - teacher_lse)
    )
    grad = row_product(one_hot_rows(core_ref[0]), logit_grad.astype(jnp.bfloat16))
    grad = grad.astype(jnp.bfloat16)
    half = own_ref.shape[0]
    for columns, copy in copies:
        copy.wait()
        out = jnp.dot(grad, head[:, columns], preferred_element_type=jnp.float32)
        own_ref[:, columns] = out[:half]
        send_ref[:, columns] = out[half:].astype(jnp.bfloat16)


def row_grad_part(core, every, weight, teacher, student, student_head_t):
    vocab, width = student_head_t.shape
    tokens = weight.shape[1]
    return kernel_call(
        row_grad_kernel,
        "row_grad",
        [
            shape_of((tokens // 2, width), jnp.float32),
            shape_of((tokens // 2, width)),
            shape_of((1, tokens), jnp.float32),
        ],
        limit=48,
        in_specs=[SMEM] + [VMEM] * 4 + [ANY],
        out_specs=[VMEM] * 3,
        scratch_shapes=[
            pltpu.VMEM((vocab, width), jnp.bfloat16),
            pltpu.SemaphoreType.DMA((4,)),
        ],
    )(core, every, weight, teacher, student, student_head_t)


def pick_kernel(place_ref, ids_ref, head_from, own_ref, send_ref, head, sems):
    copies = head_copies(head_from, head, sems)
    vocab, tokens = head.shape[0], ids_ref.shape[1]
    entry = lax.broadcasted_iota(jnp.int32, (vocab, tokens), 0) + place_ref[1] * vocab
    place = lax.broadcasted_iota(jnp.int32, (tokens, tokens), 0)
    column = lax.broadcasted_iota(jnp.int32, (tokens, tokens), 1)
    source = (((place >> 7) ^ place_ref[0]) << 7) | ((place & 63) << 1) | ((place >> 6) & 1)
    chosen = row_product(
        (column == source).astype(jnp.bfloat16), (ids_ref[...] == entry).astype(jnp.bfloat16)
    ).astype(jnp.bfloat16)
    half = own_ref.shape[0]
    for columns, copy in copies:
        copy.wait()
        out = jnp.dot(chosen, head[:, columns], preferred_element_type=jnp.float32)
        own_ref[:, columns] = out[:half].astype(jnp.bfloat16)
        send_ref[:, columns] = out[half:].astype(jnp.bfloat16)


def pick_part(place, ids, student_head_t):
    vocab, width = student_head_t.shape
    shape = shape_of((ids.shape[1] // 2, width))
    return kernel_call(
        pick_kernel,
        "pick",
        [shape, shape],
        limit=48,
        in_specs=[SMEM, VMEM, ANY],
        out_specs=[VMEM] * 2,
        scratch_shapes=[
            pltpu.VMEM((vocab, width), jnp.bfloat16),
            pltpu.SemaphoreType.DMA((4,)),
        ],
    )(place, ids, student_head_t)


def join_kernel(*refs):
    pairs, out_ref, rows = refs[:-2], refs[-2], refs[-1]
    chips, height = out_ref.shape[0], 2 * SEGMENTS
    for base, (own_ref, came_ref) in enumerate(zip(pairs[::2], pairs[1::2])):
        for t in range(2):
            for i in range(SEGMENTS):
                for k in range(SEGMENT // 128):
                    part = slice(t * chips, (t + 1) * chips)
                    lanes = slice(i * SEGMENT + k * 128, i * SEGMENT + (k + 1) * 128)
                    total = own_ref[part, lanes].astype(jnp.float32)
                    total = total + came_ref[part, lanes].astype(jnp.float32)
                    at = pl.ds(t * SEGMENTS + i, chips, stride=height)
                    rows[k, at, :] = total
        for k in range(SEGMENT // 128):
            out_ref[:, base * height : (base + 1) * height, k * 128 : (k + 1) * 128] = (
                rows[k].reshape(chips, height, 128).astype(jnp.bfloat16)
            )


def join_part(*pairs):
    chips = pairs[0].shape[0] // 2
    height = 2 * SEGMENTS
    return kernel_call(
        join_kernel,
        "join",
        shape_of((chips, height * len(pairs) // 2, SEGMENT)),
        limit=14,
        in_specs=[VMEM] * len(pairs),
        out_specs=VMEM,
        scratch_shapes=[pltpu.VMEM((SEGMENT // 128, chips * height, 128), jnp.float32)],
    )(*pairs)


def block_gain(gain_ref):
    gain = gain_ref[...].astype(jnp.float32)
    lanes = SEGMENT // 128
    token = jnp.concatenate(
        [
            jnp.concatenate([gain[lanes * i + k : lanes * i + k + 1] for k in range(lanes)], axis=1)
            for i in range(SEGMENTS)
        ],
        axis=0,
    )
    return jnp.concatenate([token, token], axis=0)


def block_mean(values):
    means = []
    for t in range(2):
        part = values[t * SEGMENTS : (t + 1) * SEGMENTS]
        total = jnp.sum(jnp.sum(part, axis=0, keepdims=True), axis=1, keepdims=True)
        means.append(jnp.broadcast_to(total / (SEGMENTS * SEGMENT), (SEGMENTS, 1)))
    return jnp.concatenate(means, axis=0)


def block_inverse(values):
    return lax.rsqrt(block_mean(values * values) + eps)


def block_back(upstream, values, gain):
    inverse = block_inverse(values)
    gained = upstream * gain
    return inverse * gained - values * inverse**3 * block_mean(gained * values)


def block_sum(blocks_ref):
    return jnp.sum(blocks_ref[...].astype(jnp.float32), axis=0)


def embed_kernel(blocks_ref, gain_ref, embedded_ref, rows_ref):
    values = block_sum(blocks_ref)
    embedded_ref[...] = values
    rows = values * block_inverse(values) * block_gain(gain_ref)
    rows_ref[...] = rows.astype(jnp.bfloat16)


def final_kernel(blocks_ref, states_ref, gain_ref, rows_ref, grad_ref, out_ref, states):
    for i in range(SEGMENTS):
        part = states_ref[:, i * SEGMENT : (i + 1) * SEGMENT].astype(jnp.float32)
        for t in range(2):
            states[t * SEGMENTS + i : t * SEGMENTS + i + 1, :] = part[t : t + 1]
    grad = block_back(block_sum(blocks_ref), states[...], block_gain(gain_ref))
    grad_ref[...] = grad
    height = 2 * SEGMENTS
    half = (out_ref.shape[0], height, SEGMENT)
    out_ref[:, :height, :] = jnp.broadcast_to(grad.astype(jnp.bfloat16)[None], half)
    out_ref[:, height:, :] = jnp.broadcast_to(rows_ref[...][None], half)


def state_kernel(blocks_ref, grad_ref, embedded_ref, gain_ref, out_ref):
    back = block_back(block_sum(blocks_ref), embedded_ref[...], block_gain(gain_ref))
    grad = grad_ref[...] + back
    for t in range(2):
        for i in range(SEGMENTS):
            out_ref[t : t + 1, i * SEGMENT : (i + 1) * SEGMENT] = grad[
                t * SEGMENTS + i : t * SEGMENTS + i + 1
            ]


BLOCK = (2 * SEGMENTS, SEGMENT)


def segment_rows(rows, first):
    height = 4 * SEGMENTS
    parts = []
    for t in range(2):
        at = pl.ds(first + t * SEGMENTS, rows.shape[1] // height, stride=height)
        parts.append(jnp.concatenate([rows[k, at, :] for k in range(SEGMENT // 128)], axis=1))
    return jnp.concatenate(parts, axis=0).astype(jnp.bfloat16)


def ffn_grad_kernel(blocks_ref, down_ref, gate_ref, up_ref, out_ref, rows):
    values = blocks_ref[...].astype(jnp.float32)
    values = values.reshape(values.shape[0] * values.shape[1], values.shape[2])
    for k in range(SEGMENT // 128):
        rows[k] = values[:, k * 128 : (k + 1) * 128]
    units = down_ref.shape[0]
    hidden, act_grad = None, None
    for i in range(SEGMENTS):
        columns = slice(i * SEGMENT, (i + 1) * SEGMENT)
        weight = jnp.concatenate([gate_ref[:, columns], up_ref[:, columns]], axis=0)
        term = row_product(weight, segment_rows(rows, 2 * SEGMENTS + i))
        hidden = term if hidden is None else hidden + term
        term = row_product(down_ref[:, columns], segment_rows(rows, i))
        act_grad = term if act_grad is None else act_grad + term
    gate, upper = hidden[:units, :], hidden[units:, :]
    sigmoid_gate = jax.nn.sigmoid(gate)
    gate_grad = act_grad * upper * sigmoid_gate * (1.0 + gate * (1.0 - sigmoid_gate))
    upper_grad = act_grad * gate * sigmoid_gate
    grads = jnp.concatenate([gate_grad, upper_grad], axis=0).astype(jnp.bfloat16)
    tokens = grads.shape[1]
    same = lax.broadcasted_iota(jnp.int32, (tokens, tokens), 0) == lax.broadcasted_iota(
        jnp.int32, (tokens, tokens), 1
    )
    grads = row_product(same.astype(jnp.bfloat16), grads).astype(jnp.bfloat16)
    for i in range(SEGMENTS):
        columns = slice(i * SEGMENT, (i + 1) * SEGMENT)
        weight = jnp.concatenate([gate_ref[:, columns], up_ref[:, columns]], axis=0)
        out = jnp.dot(grads, weight, preferred_element_type=jnp.float32)
        out_ref[:, columns] = out.astype(out_ref.dtype)


def ffn_grad_part(blocks, dtype, *weights):
    chips, height, _ = blocks.shape
    return kernel_call(
        ffn_grad_kernel,
        "ffn_grad",
        shape_of((2 * chips, SEGMENTS * SEGMENT), dtype),
        limit=20,
        in_specs=[VMEM] * (1 + len(weights)),
        out_specs=VMEM,
        scratch_shapes=[pltpu.VMEM((SEGMENT // 128, chips * height, 128), jnp.float32)],
    )(blocks, *weights)


def shards(
    teacher_states,
    teacher_gain,
    teacher_head,
    student_states,
    student_gain,
    student_head,
    token_ids,
    ffn_gain,
    gate_weight,
    up_weight,
    down_weight,
    token_weight,
):
    core = lax.axis_index("core")
    device = lax.axis_index(AXES)
    own_core = jnp.full((1,), core, jnp.int32)
    x, z, y = (lax.axis_index(line).astype(jnp.int32) for line in ("x", "z", ("yh", "yl")))
    teacher_gain, student_gain, ffn_gain = (
        gain.reshape(-1, 128) for gain in (teacher_gain, student_gain, ffn_gain)
    )
    student_head_t, teacher_head_t = student_head.T, teacher_head.T
    heads = (student_head_t, teacher_head_t)
    gate_t, up_t = gate_weight.T, up_weight.T

    width = sum(WIDTHS)
    half_shape = shape_of((2, width))
    keep, send = kernel_call(
        rows_kernel,
        "rows",
        [half_shape, half_shape],
        limit=56,
        in_specs=[SMEM] + [ANY] * 4,
        out_specs=[VMEM] * 2,
        scratch_shapes=[
            pltpu.VMEM(teacher_states.shape, jnp.bfloat16),
            pltpu.VMEM(student_states.shape, jnp.bfloat16),
            pltpu.VMEM(teacher_gain.shape, jnp.bfloat16),
            pltpu.VMEM(student_gain.shape, jnp.bfloat16),
            pltpu.VMEM((160, 128), jnp.float32),
            pltpu.SemaphoreType.DMA((4,)),
        ],
    )(own_core, teacher_states, teacher_gain, student_states, student_gain)
    (rows,) = in_pair(own_core, keep, swap_cores(send), (width,))

    (rows,) = in_pair((y & 1).reshape(1), rows, along(rows, ("yh", "yl"), 1), (width,))
    first, second = in_pair((y >> 1).reshape(1), rows, along(rows, ("yh", "yl"), 3), WIDTHS)
    for bit, mask in ((0, 1), (1, 3)):
        came = (along(first, "z", mask), along(second, "x", mask))
        bits = (jnp.stack([z, x]) >> bit) & 1
        first, second = in_pairs(bits, (first, came[0], second, came[1]))
    came = [along(first, "x", 1), along(first, "x", 3), along(second, "z", 1), along(second, "z", 3)]
    place = jnp.stack([core, device]).astype(jnp.int32)
    own, send = pick_part(place, token_ids.reshape(1, 256), student_head_t)
    came, picked = lax.optimization_barrier((came, join_part(own, swap_cores(send))))
    halves = halves_of(came)
    far = [
        along(half, line, mask)
        for half, line, mask in zip(halves, ("x", "x", "z", "z"), (3, 1, 3, 1))
    ]
    far = lax.optimization_barrier(far)
    rows = (
        whole_rows(x.reshape(1), [first] + came[:2] + far[:2]),
        whole_rows(z.reshape(1), [second] + came[2:] + far[2:]),
    )
    rows, picked = lax.optimization_barrier((rows, picked))
    embedded, ffn_rows = kernel_call(
        embed_kernel,
        "embed",
        [shape_of(BLOCK, jnp.float32), shape_of(BLOCK)],
        in_specs=[VMEM] * 2,
        out_specs=[VMEM] * 2,
    )(exchange(picked, CHIPS), ffn_gain)
    others = tuple(swap_cores(part) for part in rows)
    sums = logits_part(own_core, rows, heads)
    student, teacher, stats = logits_part(1 - own_core, others, heads, sums)
    stats = kernel_call(
        chip_stats_kernel,
        "chip_stats",
        shape_of((64, 8, 128), jnp.float32),
        limit=2,
        in_specs=[VMEM] * 2,
        out_specs=VMEM,
    )(stats, swap_cores(stats))
    every = exchange(stats, CHIPS)

    weight = token_weight.reshape(2, 4, 2, 4, 2, 2).transpose(1, 3, 2, 4, 0, 5).reshape(1, 256)
    own, send, divergence = row_grad_part(
        own_core, every, weight, teacher, student, student_head_t
    )
    divergence = divergence.reshape(4, 4, 2, 2, 2, 2).transpose(4, 0, 2, 1, 3, 5).reshape(256)
    blocks = exchange(join_part(own, swap_cores(send)), CHIPS)
    final_grad, blocks = kernel_call(
        final_kernel,
        "final",
        [shape_of(BLOCK, jnp.float32), shape_of((64, 2 * BLOCK[0], BLOCK[1]))],
        limit=12,
        in_specs=[VMEM] * 4,
        out_specs=[VMEM] * 2,
        scratch_shapes=[pltpu.VMEM(BLOCK, jnp.float32)],
    )(blocks, student_states, student_gain, ffn_rows)
    blocks = exchange(blocks, CHIPS)
    weights = (down_weight, gate_t, up_t)
    others = swap_cores(blocks)
    own = ffn_grad_part(blocks, jnp.float32, *weights)
    send = ffn_grad_part(others, jnp.bfloat16, *weights)
    ffn_grad = exchange(join_part(own, swap_cores(send)), CHIPS)
    state_grad = kernel_call(
        state_kernel,
        "state",
        shape_of((2, 4096), jnp.float32),
        in_specs=[VMEM] * 4,
        out_specs=VMEM,
    )(ffn_grad, final_grad, embedded, ffn_gain)
    return (divergence, state_grad)


def solution(mesh):
    fine = Mesh(mesh.devices.reshape(SHAPE), AXES)
    in_specs = (
        P(AXES, None),
        P(),
        P(None, AXES),
        P(AXES, None),
        P(),
        P(None, AXES),
        P(),
        P(),
        P(None, AXES),
        P(None, AXES),
        P(AXES, None),
        P(),
    )
    out_specs = (P(), P(AXES, None))
    return jax.shard_map(shards, mesh=fine, in_specs=in_specs, out_specs=out_specs, check_vma=False)
```

```python
import functools

import jax
import jax.numpy as jnp
from jax import lax
from jax.experimental import pallas as pl
from jax.experimental.pallas import tpu as pltpu
from jax.sharding import Mesh
from jax.sharding import PartitionSpec as P

eps = 1e-05
SHAPE = (2, 4, 2, 4, 2)
AXES = ("core", "x", "yh", "z", "yl")
CHIPS = AXES[1:]
MIB = 1024 * 1024

VMEM = pl.BlockSpec(memory_space=pltpu.VMEM)
SMEM = pl.BlockSpec(memory_space=pltpu.SMEM)
ANY = pl.BlockSpec(memory_space=pl.ANY)
SEGMENTS = 8
SEGMENT = 512


def kernel_call(body, name, out_shape, limit=8, **options):
    return pl.pallas_call(
        body,
        name=name,
        out_shape=out_shape,
        compiler_params=pltpu.CompilerParams(vmem_limit_bytes=limit * MIB),
        cost_estimate=pl.CostEstimate(flops=1, bytes_accessed=1, transcendentals=0),
        **options,
    )


def shape_of(shape, dtype=jnp.bfloat16):
    return jax.ShapeDtypeStruct(shape, dtype)


def row_product(left, right):
    return lax.dot_general(
        left, right, (((1,), (1,)), ((), ())), preferred_element_type=jnp.float32
    )


def swap_cores(values):
    return lax.ppermute(values, "core", [(0, 1), (1, 0)])


def exchange(blocks, axes):
    return lax.all_to_all(blocks, axes, split_axis=0, concat_axis=0, tiled=True)


def rows_kernel(
    core_ref, teacher_from, teacher_gain, student_from, student_gain, keep_ref, send_ref,
    teacher_ref, student_ref, teacher_gains, student_gains, gains, sems,
):
    copies = [
        pltpu.make_async_copy(source, target, sems.at[i])
        for i, (source, target) in enumerate(
            (
                (student_gain, student_gains),
                (student_from, student_ref),
                (teacher_gain, teacher_gains),
                (teacher_from, teacher_ref),
            )
        )
    ]
    for copy in copies:
        copy.start()
    for copy in copies:
        copy.wait()
    first = student_gain.shape[0]
    gains[:first, :] = student_gains[...].astype(jnp.float32)
    gains[first:, :] = teacher_gains[...].astype(jnp.float32)
    column = 0
    for values, base in ((student_ref, 0), (teacher_ref, first)):
        half = values.shape[1] // 2
        every = values[...].astype(jnp.float32)
        inverse = lax.rsqrt(jnp.mean(every * every, axis=-1, keepdims=True) + eps)
        for part, out in ((core_ref[0], keep_ref), (1 - core_ref[0], send_ref)):
            for k in range(half // 128):
                place = pl.ds(pl.multiple_of(part * half + k * 128, 128), 128)
                rows = values[:, place].astype(jnp.float32) * inverse
                rows = rows * gains[pl.ds(base + part * (half // 128) + k, 1), :]
                out[:, column + k * 128 : column + (k + 1) * 128] = rows.astype(jnp.bfloat16)
        column = column + half


def pair_kernel(place_ref, own_ref, came_ref, *out_refs):
    own, came = own_ref[...].astype(jnp.float32), came_ref[...].astype(jnp.float32)
    first = place_ref[0] == 0
    rows = jnp.concatenate([jnp.where(first, own, came), jnp.where(first, came, own)], axis=0)
    rows = rows.astype(jnp.bfloat16)
    column = 0
    for out in out_refs:
        out[...] = rows[:, column : column + out.shape[1]]
        column = column + out.shape[1]


def in_pair(bit, own, came, widths):
    tokens = 2 * own.shape[0]
    return kernel_call(
        pair_kernel,
        "pair",
        [shape_of((tokens, w)) for w in widths],
        in_specs=[SMEM] + [VMEM] * 2,
        out_specs=[VMEM] * len(widths),
    )(bit, own, came)


def groups_kernel(place_ref, *refs):
    count = (len(refs) - 1) // 3
    sources, outs, sems = refs[: 2 * count], refs[2 * count : -1], refs[-1]
    copies = []
    for g, out in enumerate(outs):
        for i in range(2):
            source = sources[2 * g + i]
            tokens = source.shape[0]
            at = pl.multiple_of((place_ref[g] ^ i) * tokens, tokens)
            copy = pltpu.make_async_copy(source, out.at[pl.ds(at, tokens), :], sems.at[2 * g + i])
            copy.start()
            copies.append(copy)
    for copy in copies:
        copy.wait()


def in_pairs(bits, parts):
    tokens = 2 * parts[0].shape[0]
    return kernel_call(
        groups_kernel,
        "pairs",
        [shape_of((tokens, part.shape[1])) for part in parts[::2]],
        limit=4,
        in_specs=[SMEM] + [ANY] * len(parts),
        out_specs=[VMEM] * (len(parts) // 2),
        scratch_shapes=[pltpu.SemaphoreType.DMA((len(parts),))],
    )(bits, *parts)


def halves_kernel(*refs):
    count = (len(refs) - 1) // 2
    copies = []
    for i, (piece, out) in enumerate(zip(refs[:count], refs[count:])):
        rows = out.shape[0]
        copy = pltpu.make_async_copy(piece.at[pl.ds((i % 2) * rows, rows), :], out, refs[-1].at[i])
        copy.start()
        copies.append(copy)
    for copy in copies:
        copy.wait()


def halves_of(pieces):
    return kernel_call(
        halves_kernel,
        "halves",
        [shape_of((p.shape[0] // 2, p.shape[1])) for p in pieces],
        limit=4,
        in_specs=[ANY] * len(pieces),
        out_specs=[VMEM] * len(pieces),
        scratch_shapes=[pltpu.SemaphoreType.DMA((len(pieces),))],
    )(*pieces)


def along(block, line, mask):
    return lax.ppermute(block, line, [(i, i ^ mask) for i in range(4)])


def whole_kernel(place_ref, *refs):
    pieces, out, sems = refs[:5], refs[5], refs[6]
    tokens = pieces[0].shape[0]
    copies = []
    for i, (mask, half) in enumerate(((0, 0), (1, 0), (3, 0), (2, 0), (2, 1))):
        at = (place_ref[0] ^ mask) * tokens + half * (tokens // 2)
        at = pl.multiple_of(at, tokens // 2)
        rows = pieces[i].shape[0]
        copy = pltpu.make_async_copy(pieces[i], out.at[pl.ds(at, rows), :], sems.at[i])
        copy.start()
        copies.append(copy)
    for copy in copies:
        copy.wait()


def whole_rows(place, pieces):
    tokens, width = pieces[0].shape
    return kernel_call(
        whole_kernel,
        "whole",
        shape_of((4 * tokens, width)),
        limit=6,
        in_specs=[SMEM] + [ANY] * 5,
        out_specs=VMEM,
        scratch_shapes=[pltpu.SemaphoreType.DMA((5,))],
    )(place, *pieces)


GROUPS = (
    ((0, 0, 2048), (1, 0, 3072)),
    ((1, 3072, 2560), (1, 5632, 2560)),
)
WIDTHS = tuple(sum(p[2] for p in group) for group in GROUPS)


def reordered(values):
    source = lax.broadcasted_iota(jnp.int32, (256, 256), 0)
    place = lax.broadcasted_iota(jnp.int32, (256, 256), 1)
    wanted = (((place >> 4) & 3) << 6) | (((place >> 6) & 3) << 4) | (place & 15)
    moves = (source == wanted).astype(jnp.bfloat16)
    high = values.astype(jnp.bfloat16)
    rest = values - high.astype(jnp.float32)
    middle = rest.astype(jnp.bfloat16)
    low = (rest - middle.astype(jnp.float32)).astype(jnp.bfloat16)
    high, middle, low = (
        jnp.dot(part, moves, preferred_element_type=jnp.float32) for part in (high, middle, low)
    )
    return (high + middle) + low


def softmax_stats(teacher, student, stats_out):
    teacher_peak = jnp.max(teacher, axis=0, keepdims=True)
    student_peak = jnp.max(student, axis=0, keepdims=True)
    teacher_exp = jnp.exp(teacher - teacher_peak)
    teacher_total = jnp.sum(teacher_exp, axis=0, keepdims=True)
    student_total = jnp.sum(jnp.exp(student - student_peak), axis=0, keepdims=True)
    cross = jnp.sum(teacher_exp * (teacher - student), axis=0, keepdims=True)
    stats = (
        teacher_peak + jnp.log(teacher_total),
        student_peak + jnp.log(student_total),
        cross / teacher_total,
    )
    rows = [row[:, :128] for row in stats] + [row[:, 128:] for row in stats]
    stats_out[...] = jnp.concatenate(rows + [jnp.zeros((2, 128), jnp.float32)], axis=0)


def logits_kernel(last, place_ref, *refs):
    rows_from, heads, refs = refs[:2], refs[2:4], refs[4:]
    rows, head, row_sems, head_sems = refs[-4:]
    refs = refs[:-4]
    copies = []
    column = 0
    for group, source in zip(GROUPS, rows_from):
        base = column
        for kind, start, width in group:
            i = len(copies)
            columns = slice(column, column + width)
            size = heads[kind].shape[1] // 2
            start = pl.multiple_of(place_ref[0] * size + start, 128)
            pair = (
                pltpu.make_async_copy(
                    source.at[:, column - base : column - base + width],
                    rows.at[:, columns],
                    row_sems.at[i],
                ),
                pltpu.make_async_copy(
                    heads[kind].at[:, pl.ds(start, width)], head.at[:, columns], head_sems.at[i]
                ),
            )
            copies.append((kind + (base > 0), columns, pair))
            column = column + width
    ahead = 2
    for _, _, pair in copies[:ahead]:
        for copy in pair:
            copy.start()
    sums = [None, None, None]
    for i, (kind, columns, pair) in enumerate(copies):
        for copy in pair:
            copy.wait()
        if i + ahead < len(copies):
            for copy in copies[i + ahead][2]:
                copy.start()
        term = row_product(head[:, columns], rows[:, columns])
        sums[kind] = term if sums[kind] is None else sums[kind] + term
    if last:
        came, (student_out, teacher_out, stats_out) = refs[:3], refs[3:]
        student, teacher, second = (total + ref[...] for total, ref in zip(sums, came))
        teacher = teacher + reordered(second)
        student_out[...] = student
        teacher_out[...] = teacher
        softmax_stats(teacher, student, stats_out)
    else:
        for total, out in zip(sums, refs):
            out[...] = total


def logits_part(place, rows, heads, sums=()):
    vocab, tokens = heads[1].shape[0], rows[0].shape[0]
    shape = shape_of((vocab, tokens), jnp.float32)
    last = len(sums) > 0
    pieces = sum(len(group) for group in GROUPS)
    out_shape = [shape, shape, shape_of((8, 128), jnp.float32) if last else shape]
    return kernel_call(
        functools.partial(logits_kernel, last),
        "logits",
        out_shape,
        limit=48,
        in_specs=[SMEM] + [ANY] * 4 + [VMEM] * len(sums),
        out_specs=[VMEM] * 3,
        scratch_shapes=[
            pltpu.VMEM((tokens, sum(WIDTHS)), jnp.bfloat16),
            pltpu.VMEM((vocab, sum(WIDTHS)), jnp.bfloat16),
            pltpu.SemaphoreType.DMA((pieces,)),
            pltpu.SemaphoreType.DMA((pieces,)),
        ],
    )(place, *rows, *heads, *sums)


def one_hot_rows(core):
    place = lax.broadcasted_iota(jnp.int32, (256, 256), 0)
    column = lax.broadcasted_iota(jnp.int32, (256, 256), 1)
    x, yh, z, yl = (place >> 4) & 3, (place >> 3) & 1, (place >> 1) & 3, place & 1
    source = (x << 6) | (z << 4) | (yh << 3) | (yl << 2)
    source = source | (((place >> 7) ^ core) << 1) | ((place >> 6) & 1)
    return (column == source).astype(jnp.bfloat16)


def head_copies(source, head, sems):
    columns = head.shape[1] // sems.shape[0]
    parts = [slice(i * columns, (i + 1) * columns) for i in range(sems.shape[0])]
    copies = [
        pltpu.make_async_copy(source.at[:, part], head.at[:, part], sems.at[i])
        for i, part in enumerate(parts)
    ]
    for copy in copies:
        copy.start()
    return list(zip(parts, copies))


def merged_stats(every):
    peak = jnp.max(every, axis=0)
    scaled = jnp.exp(every - peak[None])
    total = jnp.sum(scaled, axis=0)
    cross = jnp.sum(scaled * pltpu.roll(every, 6, 1), axis=0) / total
    return peak + jnp.log(total), cross


def chip_stats_kernel(own_ref, came_ref, out_ref):
    lse, cross = merged_stats(jnp.concatenate([own_ref[...][None], came_ref[...][None]], axis=0))
    row = lax.broadcasted_iota(jnp.int32, lse.shape, 0)
    merged = jnp.where((row == 2) | (row == 5), pltpu.roll(cross, 2, 0), lse)
    out_ref[...] = jnp.broadcast_to(merged[None], out_ref.shape)


def row_grad_kernel(
    core_ref, every_ref, weight_ref, teacher_ref, student_ref, head_from,
    own_ref, send_ref, divergence_ref, head, sems,
):
    copies = head_copies(head_from, head, sems)
    lse, cross = merged_stats(every_ref[...])
    teacher_lse = jnp.concatenate([lse[0:1], lse[3:4]], axis=1)
    student_lse = jnp.concatenate([lse[1:2], lse[4:5]], axis=1)
    divergence_ref[...] = (
        jnp.concatenate([cross[0:1], cross[3:4]], axis=1) - teacher_lse + student_lse
    )
    logit_grad = weight_ref[...] * (
        jnp.exp(student_ref[...] - student_lse) - jnp.exp(teacher_ref[...] - teacher_lse)
    )
    grad = row_product(one_hot_rows(core_ref[0]), logit_grad.astype(jnp.bfloat16))
    grad = grad.astype(jnp.bfloat16)
    half = own_ref.shape[0]
    for columns, copy in copies:
        copy.wait()
        out = jnp.dot(grad, head[:, columns], preferred_element_type=jnp.float32)
        own_ref[:, columns] = out[:half]
        send_ref[:, columns] = out[half:].astype(jnp.bfloat16)


def row_grad_part(core, every, weight, teacher, student, student_head_t):
    vocab, width = student_head_t.shape
    tokens = weight.shape[1]
    return kernel_call(
        row_grad_kernel,
        "row_grad",
        [
            shape_of((tokens // 2, width), jnp.float32),
            shape_of((tokens // 2, width)),
            shape_of((1, tokens), jnp.float32),
        ],
        limit=48,
        in_specs=[SMEM] + [VMEM] * 4 + [ANY],
        out_specs=[VMEM] * 3,
        scratch_shapes=[
            pltpu.VMEM((vocab, width), jnp.bfloat16),
            pltpu.SemaphoreType.DMA((4,)),
        ],
    )(core, every, weight, teacher, student, student_head_t)


def pick_kernel(place_ref, ids_ref, head_from, own_ref, send_ref, head, sems):
    copies = head_copies(head_from, head, sems)
    vocab, tokens = head.shape[0], ids_ref.shape[1]
    entry = lax.broadcasted_iota(jnp.int32, (vocab, tokens), 0) + place_ref[1] * vocab
    place = lax.broadcasted_iota(jnp.int32, (tokens, tokens), 0)
    column = lax.broadcasted_iota(jnp.int32, (tokens, tokens), 1)
    source = (((place >> 7) ^ place_ref[0]) << 7) | ((place & 63) << 1) | ((place >> 6) & 1)
    chosen = row_product(
        (column == source).astype(jnp.bfloat16), (ids_ref[...] == entry).astype(jnp.bfloat16)
    ).astype(jnp.bfloat16)
    half = own_ref.shape[0]
    for columns, copy in copies:
        copy.wait()
        out = jnp.dot(chosen, head[:, columns], preferred_element_type=jnp.float32)
        own_ref[:, columns] = out[:half].astype(jnp.bfloat16)
        send_ref[:, columns] = out[half:].astype(jnp.bfloat16)


def pick_part(place, ids, student_head_t):
    vocab, width = student_head_t.shape
    shape = shape_of((ids.shape[1] // 2, width))
    return kernel_call(
        pick_kernel,
        "pick",
        [shape, shape],
        limit=48,
        in_specs=[SMEM, VMEM, ANY],
        out_specs=[VMEM] * 2,
        scratch_shapes=[
            pltpu.VMEM((vocab, width), jnp.bfloat16),
            pltpu.SemaphoreType.DMA((4,)),
        ],
    )(place, ids, student_head_t)


def join_kernel(*refs):
    pairs, out_ref, rows = refs[:-2], refs[-2], refs[-1]
    chips, height = out_ref.shape[0], 2 * SEGMENTS
    for base, (own_ref, came_ref) in enumerate(zip(pairs[::2], pairs[1::2])):
        for t in range(2):
            for i in range(SEGMENTS):
                for k in range(SEGMENT // 128):
                    part = slice(t * chips, (t + 1) * chips)
                    lanes = slice(i * SEGMENT + k * 128, i * SEGMENT + (k + 1) * 128)
                    total = own_ref[part, lanes].astype(jnp.float32)
                    total = total + came_ref[part, lanes].astype(jnp.float32)
                    at = pl.ds(t * SEGMENTS + i, chips, stride=height)
                    rows[k, at, :] = total
        for k in range(SEGMENT // 128):
            out_ref[:, base * height : (base + 1) * height, k * 128 : (k + 1) * 128] = (
                rows[k].reshape(chips, height, 128).astype(jnp.bfloat16)
            )


def join_part(*pairs):
    chips = pairs[0].shape[0] // 2
    height = 2 * SEGMENTS
    return kernel_call(
        join_kernel,
        "join",
        shape_of((chips, height * len(pairs) // 2, SEGMENT)),
        limit=14,
        in_specs=[VMEM] * len(pairs),
        out_specs=VMEM,
        scratch_shapes=[pltpu.VMEM((SEGMENT // 128, chips * height, 128), jnp.float32)],
    )(*pairs)


def block_gain(gain_ref):
    gain = gain_ref[...].astype(jnp.float32)
    lanes = SEGMENT // 128
    token = jnp.concatenate(
        [
            jnp.concatenate([gain[lanes * i + k : lanes * i + k + 1] for k in range(lanes)], axis=1)
            for i in range(SEGMENTS)
        ],
        axis=0,
    )
    return jnp.concatenate([token, token], axis=0)


def block_mean(values):
    means = []
    for t in range(2):
        part = values[t * SEGMENTS : (t + 1) * SEGMENTS]
        total = jnp.sum(jnp.sum(part, axis=0, keepdims=True), axis=1, keepdims=True)
        means.append(jnp.broadcast_to(total / (SEGMENTS * SEGMENT), (SEGMENTS, 1)))
    return jnp.concatenate(means, axis=0)


def block_inverse(values):
    return lax.rsqrt(block_mean(values * values) + eps)


def block_back(upstream, values, gain):
    inverse = block_inverse(values)
    gained = upstream * gain
    return inverse * gained - values * inverse**3 * block_mean(gained * values)


def block_sum(blocks_ref):
    return jnp.sum(blocks_ref[...].astype(jnp.float32), axis=0)


def embed_kernel(blocks_ref, gain_ref, embedded_ref, out_ref):
    values = block_sum(blocks_ref)
    embedded_ref[...] = values
    rows = (values * block_inverse(values) * block_gain(gain_ref)).astype(jnp.bfloat16)
    out_ref[...] = jnp.broadcast_to(rows[None], out_ref.shape)


def final_kernel(blocks_ref, states_ref, gain_ref, grad_ref, out_ref, states):
    for i in range(SEGMENTS):
        part = states_ref[:, i * SEGMENT : (i + 1) * SEGMENT].astype(jnp.float32)
        for t in range(2):
            states[t * SEGMENTS + i : t * SEGMENTS + i + 1, :] = part[t : t + 1]
    grad = block_back(block_sum(blocks_ref), states[...], block_gain(gain_ref))
    grad_ref[...] = grad
    out_ref[...] = jnp.broadcast_to(grad.astype(jnp.bfloat16)[None], out_ref.shape)


def state_kernel(blocks_ref, grad_ref, embedded_ref, gain_ref, out_ref):
    back = block_back(block_sum(blocks_ref), embedded_ref[...], block_gain(gain_ref))
    grad = grad_ref[...] + back
    for t in range(2):
        for i in range(SEGMENTS):
            out_ref[t : t + 1, i * SEGMENT : (i + 1) * SEGMENT] = grad[
                t * SEGMENTS + i : t * SEGMENTS + i + 1
            ]


BLOCK = (2 * SEGMENTS, SEGMENT)


def spread_rows(refs, scratches):
    for ref, rows in zip(refs, scratches):
        values = ref[...].astype(jnp.float32)
        values = values.reshape(values.shape[0] * values.shape[1], values.shape[2])
        for k in range(SEGMENT // 128):
            rows[k] = values[:, k * 128 : (k + 1) * 128]


def segment_rows(scratches, segment):
    parts = []
    for rows in scratches:
        height = 2 * SEGMENTS
        for t in range(2):
            at = pl.ds(t * SEGMENTS + segment, rows.shape[1] // height, stride=height)
            parts.append(
                jnp.concatenate([rows[k, at, :] for k in range(SEGMENT // 128)], axis=1)
            )
    return jnp.concatenate(parts, axis=0).astype(jnp.bfloat16)


def gate_kernel(own_ref, other_ref, gate_ref, up_ref, out_ref, *scratches):
    spread_rows((own_ref, other_ref), scratches)
    total = None
    for i in range(SEGMENTS):
        columns = slice(i * SEGMENT, (i + 1) * SEGMENT)
        weight = jnp.concatenate([gate_ref[:, columns], up_ref[:, columns]], axis=0)
        term = row_product(weight, segment_rows(scratches, i))
        total = term if total is None else total + term
    out_ref[...] = total


def ffn_grad_kernel(
    own_ref, other_ref, down_ref, hidden_ref, gate_ref, up_ref, own_out, send_out, *scratches
):
    spread_rows((own_ref, other_ref), scratches)
    units = down_ref.shape[0]
    hidden, act_grad = hidden_ref[...], None
    for i in range(SEGMENTS):
        columns = slice(i * SEGMENT, (i + 1) * SEGMENT)
        term = row_product(down_ref[:, columns], segment_rows(scratches, i))
        act_grad = term if act_grad is None else act_grad + term
    gate, upper = hidden[:units, :], hidden[units:, :]
    sigmoid_gate = jax.nn.sigmoid(gate)
    gate_grad = act_grad * upper * sigmoid_gate * (1.0 + gate * (1.0 - sigmoid_gate))
    upper_grad = act_grad * gate * sigmoid_gate
    grads = jnp.concatenate([gate_grad, upper_grad], axis=0).astype(jnp.bfloat16)
    tokens = grads.shape[1]
    same = lax.broadcasted_iota(jnp.int32, (tokens, tokens), 0) == lax.broadcasted_iota(
        jnp.int32, (tokens, tokens), 1
    )
    grads = row_product(same.astype(jnp.bfloat16), grads).astype(jnp.bfloat16)
    for i in range(SEGMENTS):
        columns = slice(i * SEGMENT, (i + 1) * SEGMENT)
        weight = jnp.concatenate([gate_ref[:, columns], up_ref[:, columns]], axis=0)
        out = jnp.dot(grads, weight, preferred_element_type=jnp.float32)
        own_out[:, columns] = out[: tokens // 2]
        send_out[:, columns] = out[tokens // 2 :].astype(jnp.bfloat16)


def ffn_part(body, name, out_shape, blocks, *others):
    rows = blocks.shape[0] * blocks.shape[1]
    scratch = pltpu.VMEM((SEGMENT // 128, rows, 128), jnp.float32)
    return kernel_call(
        body,
        name,
        out_shape,
        limit=20,
        in_specs=[VMEM] * (2 + len(others)),
        out_specs=[VMEM] * len(out_shape),
        scratch_shapes=[scratch, scratch],
    )(blocks, swap_cores(blocks), *others)


def shards(
    teacher_states,
    teacher_gain,
    teacher_head,
    student_states,
    student_gain,
    student_head,
    token_ids,
    ffn_gain,
    gate_weight,
    up_weight,
    down_weight,
    token_weight,
):
    core = lax.axis_index("core")
    device = lax.axis_index(AXES)
    own_core = jnp.full((1,), core, jnp.int32)
    x, z, y = (lax.axis_index(line).astype(jnp.int32) for line in ("x", "z", ("yh", "yl")))
    teacher_gain, student_gain, ffn_gain = (
        gain.reshape(-1, 128) for gain in (teacher_gain, student_gain, ffn_gain)
    )
    student_head_t, teacher_head_t = student_head.T, teacher_head.T
    heads = (student_head_t, teacher_head_t)
    gate_t, up_t = gate_weight.T, up_weight.T

    width = sum(WIDTHS)
    half_shape = shape_of((2, width))
    keep, send = kernel_call(
        rows_kernel,
        "rows",
        [half_shape, half_shape],
        limit=56,
        in_specs=[SMEM] + [ANY] * 4,
        out_specs=[VMEM] * 2,
        scratch_shapes=[
            pltpu.VMEM(teacher_states.shape, jnp.bfloat16),
            pltpu.VMEM(student_states.shape, jnp.bfloat16),
            pltpu.VMEM(teacher_gain.shape, jnp.bfloat16),
            pltpu.VMEM(student_gain.shape, jnp.bfloat16),
            pltpu.VMEM((160, 128), jnp.float32),
            pltpu.SemaphoreType.DMA((4,)),
        ],
    )(own_core, teacher_states, teacher_gain, student_states, student_gain)
    (rows,) = in_pair(own_core, keep, swap_cores(send), (width,))

    (rows,) = in_pair((y & 1).reshape(1), rows, along(rows, ("yh", "yl"), 1), (width,))
    first, second = in_pair((y >> 1).reshape(1), rows, along(rows, ("yh", "yl"), 3), WIDTHS)
    bits = jnp.stack([z, x])
    came = (along(first, "z", 1), along(second, "x", 1))
    first, second = in_pairs(bits & 1, (first, came[0], second, came[1]))
    came = (along(first, "z", 3), along(second, "x", 3))
    place = jnp.stack([core, device]).astype(jnp.int32)
    own, send = pick_part(place, token_ids.reshape(1, 256), student_head_t)
    came, picked = lax.optimization_barrier((came, join_part(own, swap_cores(send))))
    first, second = in_pairs(bits >> 1, (first, came[0], second, came[1]))
    came = [along(first, "x", 1), along(first, "x", 3), along(second, "z", 1), along(second, "z", 3)]
    picked = exchange(picked, CHIPS)
    came = lax.optimization_barrier(came)
    halves = halves_of(came)
    far = [
        along(half, line, mask)
        for half, line, mask in zip(halves, ("x", "x", "z", "z"), (3, 1, 3, 1))
    ]
    far, picked = lax.optimization_barrier((far, picked))
    rows = (
        whole_rows(x.reshape(1), [first] + came[:2] + far[:2]),
        whole_rows(z.reshape(1), [second] + came[2:] + far[2:]),
    )
    embedded, ffn_rows = kernel_call(
        embed_kernel,
        "embed",
        [shape_of(BLOCK, jnp.float32), shape_of(picked.shape)],
        in_specs=[VMEM] * 2,
        out_specs=[VMEM] * 2,
    )(picked, ffn_gain)
    rows, ffn_rows = lax.optimization_barrier((rows, ffn_rows))
    ffn_rows = exchange(ffn_rows, CHIPS)
    others = tuple(swap_cores(part) for part in rows)
    sums = logits_part(own_core, rows, heads)
    student, teacher, stats = logits_part(1 - own_core, others, heads, sums)
    stats = kernel_call(
        chip_stats_kernel,
        "chip_stats",
        shape_of((64, 8, 128), jnp.float32),
        limit=2,
        in_specs=[VMEM] * 2,
        out_specs=VMEM,
    )(stats, swap_cores(stats))
    every = exchange(stats, CHIPS)

    weight = token_weight.reshape(2, 4, 2, 4, 2, 2).transpose(1, 3, 2, 4, 0, 5).reshape(1, 256)
    own, send, divergence = row_grad_part(
        own_core, every, weight, teacher, student, student_head_t
    )
    divergence = divergence.reshape(4, 4, 2, 2, 2, 2).transpose(4, 0, 2, 1, 3, 5).reshape(256)
    blocks = join_part(own, swap_cores(send))
    (hidden,) = ffn_part(
        gate_kernel, "gate_upper", [shape_of((224, 256), jnp.float32)], ffn_rows, gate_t, up_t
    )
    blocks, hidden = lax.optimization_barrier((blocks, hidden))
    blocks = exchange(blocks, CHIPS)
    final_grad, blocks = kernel_call(
        final_kernel,
        "final",
        [shape_of(BLOCK, jnp.float32), shape_of(blocks.shape)],
        in_specs=[VMEM] * 3,
        out_specs=[VMEM] * 2,
        scratch_shapes=[pltpu.VMEM(BLOCK, jnp.float32)],
    )(blocks, student_states, student_gain)
    blocks = exchange(blocks, CHIPS)
    shape = (128, 4096)
    own, send = ffn_part(
        ffn_grad_kernel,
        "ffn_grad",
        [shape_of(shape, jnp.float32), shape_of(shape)],
        blocks,
        down_weight,
        hidden,
        gate_t,
        up_t,
    )
    ffn_grad = exchange(join_part(own, swap_cores(send)), CHIPS)
    state_grad = kernel_call(
        state_kernel,
        "state",
        shape_of((2, 4096), jnp.float32),
        in_specs=[VMEM] * 4,
        out_specs=VMEM,
    )(ffn_grad, final_grad, embedded, ffn_gain)
    return (divergence, state_grad)


def solution(mesh):
    fine = Mesh(mesh.devices.reshape(SHAPE), AXES)
    in_specs = (
        P(AXES, None),
        P(),
        P(None, AXES),
        P(AXES, None),
        P(),
        P(None, AXES),
        P(),
        P(),
        P(None, AXES),
        P(None, AXES),
        P(AXES, None),
        P(),
    )
    out_specs = (P(), P(AXES, None))
    return jax.shard_map(shards, mesh=fine, in_specs=in_specs, out_specs=out_specs, check_vma=False)
```

```python
import functools

import jax
import jax.numpy as jnp
from jax import lax
from jax.experimental import pallas as pl
from jax.experimental.pallas import tpu as pltpu
from jax.sharding import Mesh
from jax.sharding import PartitionSpec as P

eps = 1e-05
SHAPE = (2, 4, 2, 4, 2)
AXES = ("core", "x", "yh", "z", "yl")
CHIPS = AXES[1:]
MIB = 1024 * 1024

VMEM = pl.BlockSpec(memory_space=pltpu.VMEM)
SMEM = pl.BlockSpec(memory_space=pltpu.SMEM)
ANY = pl.BlockSpec(memory_space=pl.ANY)
SEGMENTS = 8
SEGMENT = 512


def kernel_call(body, name, out_shape, limit=8, **options):
    return pl.pallas_call(
        body,
        name=name,
        out_shape=out_shape,
        compiler_params=pltpu.CompilerParams(vmem_limit_bytes=limit * MIB),
        cost_estimate=pl.CostEstimate(flops=1, bytes_accessed=1, transcendentals=0),
        **options,
    )


def shape_of(shape, dtype=jnp.bfloat16):
    return jax.ShapeDtypeStruct(shape, dtype)


def row_product(left, right):
    return lax.dot_general(
        left, right, (((1,), (1,)), ((), ())), preferred_element_type=jnp.float32
    )


def swap_cores(values):
    return lax.ppermute(values, "core", [(0, 1), (1, 0)])


def exchange(blocks, axes):
    return lax.all_to_all(blocks, axes, split_axis=0, concat_axis=0, tiled=True)


def rows_kernel(
    core_ref, teacher_from, teacher_gain, student_from, student_gain, keep_ref, send_ref,
    teacher_ref, student_ref, teacher_gains, student_gains, gains, sems,
):
    copies = [
        pltpu.make_async_copy(source, target, sems.at[i])
        for i, (source, target) in enumerate(
            (
                (student_gain, student_gains),
                (student_from, student_ref),
                (teacher_gain, teacher_gains),
                (teacher_from, teacher_ref),
            )
        )
    ]
    for copy in copies:
        copy.start()
    for copy in copies:
        copy.wait()
    first = student_gain.shape[0]
    gains[:first, :] = student_gains[...].astype(jnp.float32)
    gains[first:, :] = teacher_gains[...].astype(jnp.float32)
    column = 0
    for values, base in ((student_ref, 0), (teacher_ref, first)):
        half = values.shape[1] // 2
        every = values[...].astype(jnp.float32)
        inverse = lax.rsqrt(jnp.mean(every * every, axis=-1, keepdims=True) + eps)
        for part, out in ((core_ref[0], keep_ref), (1 - core_ref[0], send_ref)):
            for k in range(half // 128):
                place = pl.ds(pl.multiple_of(part * half + k * 128, 128), 128)
                rows = values[:, place].astype(jnp.float32) * inverse
                rows = rows * gains[pl.ds(base + part * (half // 128) + k, 1), :]
                out[:, column + k * 128 : column + (k + 1) * 128] = rows.astype(jnp.bfloat16)
        column = column + half


def pair_kernel(place_ref, own_ref, came_ref, *out_refs):
    own, came = own_ref[...].astype(jnp.float32), came_ref[...].astype(jnp.float32)
    first = place_ref[0] == 0
    rows = jnp.concatenate([jnp.where(first, own, came), jnp.where(first, came, own)], axis=0)
    rows = rows.astype(jnp.bfloat16)
    column = 0
    for out in out_refs:
        out[...] = rows[:, column : column + out.shape[1]]
        column = column + out.shape[1]


def in_pair(bit, own, came, widths):
    tokens = 2 * own.shape[0]
    return kernel_call(
        pair_kernel,
        "pair",
        [shape_of((tokens, w)) for w in widths],
        in_specs=[SMEM] + [VMEM] * 2,
        out_specs=[VMEM] * len(widths),
    )(bit, own, came)


def groups_kernel(place_ref, *refs):
    count = (len(refs) - 1) // 3
    sources, outs, sems = refs[: 2 * count], refs[2 * count : -1], refs[-1]
    copies = []
    for g, out in enumerate(outs):
        for i in range(2):
            source = sources[2 * g + i]
            tokens = source.shape[0]
            at = pl.multiple_of((place_ref[g] ^ i) * tokens, tokens)
            copy = pltpu.make_async_copy(source, out.at[pl.ds(at, tokens), :], sems.at[2 * g + i])
            copy.start()
            copies.append(copy)
    for copy in copies:
        copy.wait()


def in_pairs(bits, parts):
    tokens = 2 * parts[0].shape[0]
    return kernel_call(
        groups_kernel,
        "pairs",
        [shape_of((tokens, part.shape[1])) for part in parts[::2]],
        limit=4,
        in_specs=[SMEM] + [ANY] * len(parts),
        out_specs=[VMEM] * (len(parts) // 2),
        scratch_shapes=[pltpu.SemaphoreType.DMA((len(parts),))],
    )(bits, *parts)


def halves_kernel(*refs):
    count = (len(refs) - 1) // 2
    copies = []
    for i, (piece, out) in enumerate(zip(refs[:count], refs[count:])):
        rows = out.shape[0]
        copy = pltpu.make_async_copy(piece.at[pl.ds((i % 2) * rows, rows), :], out, refs[-1].at[i])
        copy.start()
        copies.append(copy)
    for copy in copies:
        copy.wait()


def halves_of(pieces):
    return kernel_call(
        halves_kernel,
        "halves",
        [shape_of((p.shape[0] // 2, p.shape[1])) for p in pieces],
        limit=4,
        in_specs=[ANY] * len(pieces),
        out_specs=[VMEM] * len(pieces),
        scratch_shapes=[pltpu.SemaphoreType.DMA((len(pieces),))],
    )(*pieces)


def along(block, line, mask):
    return lax.ppermute(block, line, [(i, i ^ mask) for i in range(4)])


def whole_kernel(place_ref, *refs):
    pieces, out, sems = refs[:5], refs[5], refs[6]
    tokens = pieces[0].shape[0]
    copies = []
    for i, (mask, half) in enumerate(((0, 0), (1, 0), (3, 0), (2, 0), (2, 1))):
        at = (place_ref[0] ^ mask) * tokens + half * (tokens // 2)
        at = pl.multiple_of(at, tokens // 2)
        rows = pieces[i].shape[0]
        copy = pltpu.make_async_copy(pieces[i], out.at[pl.ds(at, rows), :], sems.at[i])
        copy.start()
        copies.append(copy)
    for copy in copies:
        copy.wait()


def whole_rows(place, pieces):
    tokens, width = pieces[0].shape
    return kernel_call(
        whole_kernel,
        "whole",
        shape_of((4 * tokens, width)),
        limit=6,
        in_specs=[SMEM] + [ANY] * 5,
        out_specs=VMEM,
        scratch_shapes=[pltpu.SemaphoreType.DMA((5,))],
    )(place, *pieces)


GROUPS = (
    ((0, 0, 2048), (1, 0, 3072)),
    ((1, 3072, 2560), (1, 5632, 2560)),
)
WIDTHS = tuple(sum(p[2] for p in group) for group in GROUPS)


def reordered(values):
    source = lax.broadcasted_iota(jnp.int32, (256, 256), 0)
    place = lax.broadcasted_iota(jnp.int32, (256, 256), 1)
    wanted = (((place >> 4) & 3) << 6) | (((place >> 6) & 3) << 4) | (place & 15)
    moves = (source == wanted).astype(jnp.bfloat16)
    high = values.astype(jnp.bfloat16)
    rest = values - high.astype(jnp.float32)
    middle = rest.astype(jnp.bfloat16)
    low = (rest - middle.astype(jnp.float32)).astype(jnp.bfloat16)
    high, middle, low = (
        jnp.dot(part, moves, preferred_element_type=jnp.float32) for part in (high, middle, low)
    )
    return (high + middle) + low


def softmax_stats(teacher, student, stats_out):
    teacher_peak = jnp.max(teacher, axis=0, keepdims=True)
    student_peak = jnp.max(student, axis=0, keepdims=True)
    teacher_exp = jnp.exp(teacher - teacher_peak)
    teacher_total = jnp.sum(teacher_exp, axis=0, keepdims=True)
    student_total = jnp.sum(jnp.exp(student - student_peak), axis=0, keepdims=True)
    cross = jnp.sum(teacher_exp * (teacher - student), axis=0, keepdims=True)
    stats = (
        teacher_peak + jnp.log(teacher_total),
        student_peak + jnp.log(student_total),
        cross / teacher_total,
    )
    rows = [row[:, :128] for row in stats] + [row[:, 128:] for row in stats]
    stats_out[...] = jnp.concatenate(rows + [jnp.zeros((2, 128), jnp.float32)], axis=0)


def logits_kernel(last, place_ref, *refs):
    rows_from, heads, refs = refs[:2], refs[2:4], refs[4:]
    rows, head, row_sems, head_sems = refs[-4:]
    refs = refs[:-4]
    copies = []
    column = 0
    for group, source in zip(GROUPS, rows_from):
        base = column
        for kind, start, width in group:
            i = len(copies)
            columns = slice(column, column + width)
            size = heads[kind].shape[1] // 2
            start = pl.multiple_of(place_ref[0] * size + start, 128)
            pair = (
                pltpu.make_async_copy(
                    source.at[:, column - base : column - base + width],
                    rows.at[:, columns],
                    row_sems.at[i],
                ),
                pltpu.make_async_copy(
                    heads[kind].at[:, pl.ds(start, width)], head.at[:, columns], head_sems.at[i]
                ),
            )
            copies.append((kind + (base > 0), columns, pair))
            column = column + width
    ahead = 2
    for _, _, pair in copies[:ahead]:
        for copy in pair:
            copy.start()
    sums = [None, None, None]
    for i, (kind, columns, pair) in enumerate(copies):
        for copy in pair:
            copy.wait()
        if i + ahead < len(copies):
            for copy in copies[i + ahead][2]:
                copy.start()
        term = row_product(head[:, columns], rows[:, columns])
        sums[kind] = term if sums[kind] is None else sums[kind] + term
    if last:
        came, (student_out, teacher_out, stats_out) = refs[:3], refs[3:]
        student, teacher, second = (total + ref[...] for total, ref in zip(sums, came))
        teacher = teacher + reordered(second)
        student_out[...] = student
        teacher_out[...] = teacher
        softmax_stats(teacher, student, stats_out)
    else:
        for total, out in zip(sums, refs):
            out[...] = total


def logits_part(place, rows, heads, sums=()):
    vocab, tokens = heads[1].shape[0], rows[0].shape[0]
    shape = shape_of((vocab, tokens), jnp.float32)
    last = len(sums) > 0
    pieces = sum(len(group) for group in GROUPS)
    out_shape = [shape, shape, shape_of((8, 128), jnp.float32) if last else shape]
    return kernel_call(
        functools.partial(logits_kernel, last),
        "logits",
        out_shape,
        limit=48,
        in_specs=[SMEM] + [ANY] * 4 + [VMEM] * len(sums),
        out_specs=[VMEM] * 3,
        scratch_shapes=[
            pltpu.VMEM((tokens, sum(WIDTHS)), jnp.bfloat16),
            pltpu.VMEM((vocab, sum(WIDTHS)), jnp.bfloat16),
            pltpu.SemaphoreType.DMA((pieces,)),
            pltpu.SemaphoreType.DMA((pieces,)),
        ],
    )(place, *rows, *heads, *sums)


def one_hot_rows(core):
    place = lax.broadcasted_iota(jnp.int32, (256, 256), 0)
    column = lax.broadcasted_iota(jnp.int32, (256, 256), 1)
    x, yh, z, yl = (place >> 4) & 3, (place >> 3) & 1, (place >> 1) & 3, place & 1
    source = (x << 6) | (z << 4) | (yh << 3) | (yl << 2)
    source = source | (((place >> 7) ^ core) << 1) | ((place >> 6) & 1)
    return (column == source).astype(jnp.bfloat16)


def head_copies(source, head, sems):
    columns = head.shape[1] // sems.shape[0]
    parts = [slice(i * columns, (i + 1) * columns) for i in range(sems.shape[0])]
    copies = [
        pltpu.make_async_copy(source.at[:, part], head.at[:, part], sems.at[i])
        for i, part in enumerate(parts)
    ]
    for copy in copies:
        copy.start()
    return list(zip(parts, copies))


def merged_stats(every):
    peak = jnp.max(every, axis=0)
    scaled = jnp.exp(every - peak[None])
    total = jnp.sum(scaled, axis=0)
    cross = jnp.sum(scaled * pltpu.roll(every, 6, 1), axis=0) / total
    return peak + jnp.log(total), cross


def chip_stats_kernel(own_ref, came_ref, out_ref):
    lse, cross = merged_stats(jnp.concatenate([own_ref[...][None], came_ref[...][None]], axis=0))
    row = lax.broadcasted_iota(jnp.int32, lse.shape, 0)
    merged = jnp.where((row == 2) | (row == 5), pltpu.roll(cross, 2, 0), lse)
    out_ref[...] = jnp.broadcast_to(merged[None], out_ref.shape)


def row_grad_kernel(
    core_ref, every_ref, weight_ref, teacher_ref, student_ref, head_from,
    own_ref, send_ref, divergence_ref, head, sems,
):
    copies = head_copies(head_from, head, sems)
    lse, cross = merged_stats(every_ref[...])
    teacher_lse = jnp.concatenate([lse[0:1], lse[3:4]], axis=1)
    student_lse = jnp.concatenate([lse[1:2], lse[4:5]], axis=1)
    divergence_ref[...] = (
        jnp.concatenate([cross[0:1], cross[3:4]], axis=1) - teacher_lse + student_lse
    )
    logit_grad = weight_ref[...] * (
        jnp.exp(student_ref[...] - student_lse) - jnp.exp(teacher_ref[...] - teacher_lse)
    )
    grad = row_product(one_hot_rows(core_ref[0]), logit_grad.astype(jnp.bfloat16))
    grad = grad.astype(jnp.bfloat16)
    half = own_ref.shape[0]
    for columns, copy in copies:
        copy.wait()
        out = jnp.dot(grad, head[:, columns], preferred_element_type=jnp.float32)
        own_ref[:, columns] = out[:half]
        send_ref[:, columns] = out[half:].astype(jnp.bfloat16)


def row_grad_part(core, every, weight, teacher, student, student_head_t):
    vocab, width = student_head_t.shape
    tokens = weight.shape[1]
    return kernel_call(
        row_grad_kernel,
        "row_grad",
        [
            shape_of((tokens // 2, width), jnp.float32),
            shape_of((tokens // 2, width)),
            shape_of((1, tokens), jnp.float32),
        ],
        limit=48,
        in_specs=[SMEM] + [VMEM] * 4 + [ANY],
        out_specs=[VMEM] * 3,
        scratch_shapes=[
            pltpu.VMEM((vocab, width), jnp.bfloat16),
            pltpu.SemaphoreType.DMA((4,)),
        ],
    )(core, every, weight, teacher, student, student_head_t)


def pick_kernel(place_ref, ids_ref, head_from, own_ref, send_ref, head, sems):
    copies = head_copies(head_from, head, sems)
    vocab, tokens = head.shape[0], ids_ref.shape[1]
    entry = lax.broadcasted_iota(jnp.int32, (vocab, tokens), 0) + place_ref[1] * vocab
    place = lax.broadcasted_iota(jnp.int32, (tokens, tokens), 0)
    column = lax.broadcasted_iota(jnp.int32, (tokens, tokens), 1)
    source = (((place >> 7) ^ place_ref[0]) << 7) | ((place & 63) << 1) | ((place >> 6) & 1)
    chosen = row_product(
        (column == source).astype(jnp.bfloat16), (ids_ref[...] == entry).astype(jnp.bfloat16)
    ).astype(jnp.bfloat16)
    half = own_ref.shape[0]
    for columns, copy in copies:
        copy.wait()
        out = jnp.dot(chosen, head[:, columns], preferred_element_type=jnp.float32)
        own_ref[:, columns] = out[:half].astype(jnp.bfloat16)
        send_ref[:, columns] = out[half:].astype(jnp.bfloat16)


def pick_part(place, ids, student_head_t):
    vocab, width = student_head_t.shape
    shape = shape_of((ids.shape[1] // 2, width))
    return kernel_call(
        pick_kernel,
        "pick",
        [shape, shape],
        limit=48,
        in_specs=[SMEM, VMEM, ANY],
        out_specs=[VMEM] * 2,
        scratch_shapes=[
            pltpu.VMEM((vocab, width), jnp.bfloat16),
            pltpu.SemaphoreType.DMA((4,)),
        ],
    )(place, ids, student_head_t)


def join_kernel(*refs):
    pairs, out_ref, rows = refs[:-2], refs[-2], refs[-1]
    chips, height = out_ref.shape[0], 2 * SEGMENTS
    for base, (own_ref, came_ref) in enumerate(zip(pairs[::2], pairs[1::2])):
        for t in range(2):
            for i in range(SEGMENTS):
                for k in range(SEGMENT // 128):
                    part = slice(t * chips, (t + 1) * chips)
                    lanes = slice(i * SEGMENT + k * 128, i * SEGMENT + (k + 1) * 128)
                    total = own_ref[part, lanes].astype(jnp.float32)
                    total = total + came_ref[part, lanes].astype(jnp.float32)
                    at = pl.ds(t * SEGMENTS + i, chips, stride=height)
                    rows[k, at, :] = total
        for k in range(SEGMENT // 128):
            out_ref[:, base * height : (base + 1) * height, k * 128 : (k + 1) * 128] = (
                rows[k].reshape(chips, height, 128).astype(jnp.bfloat16)
            )


def join_part(*pairs):
    chips = pairs[0].shape[0] // 2
    height = 2 * SEGMENTS
    return kernel_call(
        join_kernel,
        "join",
        shape_of((chips, height * len(pairs) // 2, SEGMENT)),
        limit=14,
        in_specs=[VMEM] * len(pairs),
        out_specs=VMEM,
        scratch_shapes=[pltpu.VMEM((SEGMENT // 128, chips * height, 128), jnp.float32)],
    )(*pairs)


def block_gain(gain_ref):
    gain = gain_ref[...].astype(jnp.float32)
    lanes = SEGMENT // 128
    token = jnp.concatenate(
        [
            jnp.concatenate([gain[lanes * i + k : lanes * i + k + 1] for k in range(lanes)], axis=1)
            for i in range(SEGMENTS)
        ],
        axis=0,
    )
    return jnp.concatenate([token, token], axis=0)


def block_mean(values):
    means = []
    for t in range(2):
        part = values[t * SEGMENTS : (t + 1) * SEGMENTS]
        total = jnp.sum(jnp.sum(part, axis=0, keepdims=True), axis=1, keepdims=True)
        means.append(jnp.broadcast_to(total / (SEGMENTS * SEGMENT), (SEGMENTS, 1)))
    return jnp.concatenate(means, axis=0)


def block_inverse(values):
    return lax.rsqrt(block_mean(values * values) + eps)


def block_back(upstream, values, gain):
    inverse = block_inverse(values)
    gained = upstream * gain
    return inverse * gained - values * inverse**3 * block_mean(gained * values)


def block_sum(blocks_ref):
    return jnp.sum(blocks_ref[...].astype(jnp.float32), axis=0)


def embed_kernel(blocks_ref, gain_ref, embedded_ref, rows_ref):
    values = block_sum(blocks_ref)
    embedded_ref[...] = values
    rows = values * block_inverse(values) * block_gain(gain_ref)
    rows_ref[...] = rows.astype(jnp.bfloat16)


def final_kernel(blocks_ref, states_ref, gain_ref, rows_ref, grad_ref, out_ref, states):
    for i in range(SEGMENTS):
        part = states_ref[:, i * SEGMENT : (i + 1) * SEGMENT].astype(jnp.float32)
        for t in range(2):
            states[t * SEGMENTS + i : t * SEGMENTS + i + 1, :] = part[t : t + 1]
    grad = block_back(block_sum(blocks_ref), states[...], block_gain(gain_ref))
    grad_ref[...] = grad
    height = 2 * SEGMENTS
    half = (out_ref.shape[0], height, SEGMENT)
    out_ref[:, :height, :] = jnp.broadcast_to(grad.astype(jnp.bfloat16)[None], half)
    out_ref[:, height:, :] = jnp.broadcast_to(rows_ref[...][None], half)


def state_kernel(blocks_ref, grad_ref, embedded_ref, gain_ref, out_ref):
    back = block_back(block_sum(blocks_ref), embedded_ref[...], block_gain(gain_ref))
    grad = grad_ref[...] + back
    for t in range(2):
        for i in range(SEGMENTS):
            out_ref[t : t + 1, i * SEGMENT : (i + 1) * SEGMENT] = grad[
                t * SEGMENTS + i : t * SEGMENTS + i + 1
            ]


BLOCK = (2 * SEGMENTS, SEGMENT)


def segment_rows(rows, first):
    height = 4 * SEGMENTS
    parts = []
    for t in range(2):
        at = pl.ds(first + t * SEGMENTS, rows.shape[1] // height, stride=height)
        parts.append(jnp.concatenate([rows[k, at, :] for k in range(SEGMENT // 128)], axis=1))
    return jnp.concatenate(parts, axis=0).astype(jnp.bfloat16)


def ffn_grad_kernel(blocks_ref, down_ref, gate_ref, up_ref, out_ref, rows):
    values = blocks_ref[...].astype(jnp.float32)
    values = values.reshape(values.shape[0] * values.shape[1], values.shape[2])
    for k in range(SEGMENT // 128):
        rows[k] = values[:, k * 128 : (k + 1) * 128]
    units = down_ref.shape[0]
    hidden, act_grad = None, None
    for i in range(SEGMENTS):
        columns = slice(i * SEGMENT, (i + 1) * SEGMENT)
        weight = jnp.concatenate([gate_ref[:, columns], up_ref[:, columns]], axis=0)
        term = row_product(weight, segment_rows(rows, 2 * SEGMENTS + i))
        hidden = term if hidden is None else hidden + term
        term = row_product(down_ref[:, columns], segment_rows(rows, i))
        act_grad = term if act_grad is None else act_grad + term
    gate, upper = hidden[:units, :], hidden[units:, :]
    sigmoid_gate = jax.nn.sigmoid(gate)
    gate_grad = act_grad * upper * sigmoid_gate * (1.0 + gate * (1.0 - sigmoid_gate))
    upper_grad = act_grad * gate * sigmoid_gate
    grads = jnp.concatenate([gate_grad, upper_grad], axis=0).astype(jnp.bfloat16)
    tokens = grads.shape[1]
    same = lax.broadcasted_iota(jnp.int32, (tokens, tokens), 0) == lax.broadcasted_iota(
        jnp.int32, (tokens, tokens), 1
    )
    grads = row_product(same.astype(jnp.bfloat16), grads).astype(jnp.bfloat16)
    for i in range(SEGMENTS):
        columns = slice(i * SEGMENT, (i + 1) * SEGMENT)
        weight = jnp.concatenate([gate_ref[:, columns], up_ref[:, columns]], axis=0)
        out = jnp.dot(grads, weight, preferred_element_type=jnp.float32)
        out_ref[:, columns] = out.astype(out_ref.dtype)


def ffn_grad_part(blocks, dtype, *weights):
    chips, height, _ = blocks.shape
    return kernel_call(
        ffn_grad_kernel,
        "ffn_grad",
        shape_of((2 * chips, SEGMENTS * SEGMENT), dtype),
        limit=20,
        in_specs=[VMEM] * (1 + len(weights)),
        out_specs=VMEM,
        scratch_shapes=[pltpu.VMEM((SEGMENT // 128, chips * height, 128), jnp.float32)],
    )(blocks, *weights)


def shards(
    teacher_states,
    teacher_gain,
    teacher_head,
    student_states,
    student_gain,
    student_head,
    token_ids,
    ffn_gain,
    gate_weight,
    up_weight,
    down_weight,
    token_weight,
):
    core = lax.axis_index("core")
    device = lax.axis_index(AXES)
    own_core = jnp.full((1,), core, jnp.int32)
    x, z, y = (lax.axis_index(line).astype(jnp.int32) for line in ("x", "z", ("yh", "yl")))
    teacher_gain, student_gain, ffn_gain = (
        gain.reshape(-1, 128) for gain in (teacher_gain, student_gain, ffn_gain)
    )
    student_head_t, teacher_head_t = student_head.T, teacher_head.T
    heads = (student_head_t, teacher_head_t)
    gate_t, up_t = gate_weight.T, up_weight.T

    width = sum(WIDTHS)
    half_shape = shape_of((2, width))
    keep, send = kernel_call(
        rows_kernel,
        "rows",
        [half_shape, half_shape],
        limit=56,
        in_specs=[SMEM] + [ANY] * 4,
        out_specs=[VMEM] * 2,
        scratch_shapes=[
            pltpu.VMEM(teacher_states.shape, jnp.bfloat16),
            pltpu.VMEM(student_states.shape, jnp.bfloat16),
            pltpu.VMEM(teacher_gain.shape, jnp.bfloat16),
            pltpu.VMEM(student_gain.shape, jnp.bfloat16),
            pltpu.VMEM((160, 128), jnp.float32),
            pltpu.SemaphoreType.DMA((4,)),
        ],
    )(own_core, teacher_states, teacher_gain, student_states, student_gain)
    (rows,) = in_pair(own_core, keep, swap_cores(send), (width,))

    (rows,) = in_pair((y & 1).reshape(1), rows, along(rows, ("yh", "yl"), 1), (width,))
    first, second = in_pair((y >> 1).reshape(1), rows, along(rows, ("yh", "yl"), 3), WIDTHS)
    for bit, mask in ((0, 1), (1, 3)):
        came = (along(first, "z", mask), along(second, "x", mask))
        bits = (jnp.stack([z, x]) >> bit) & 1
        first, second = in_pairs(bits, (first, came[0], second, came[1]))
    came = [along(first, "x", 1), along(first, "x", 3), along(second, "z", 1), along(second, "z", 3)]
    place = jnp.stack([core, device]).astype(jnp.int32)
    own, send = pick_part(place, token_ids.reshape(1, 256), student_head_t)
    came, picked = lax.optimization_barrier((came, join_part(own, swap_cores(send))))
    halves = halves_of(came)
    far = [
        along(half, line, mask)
        for half, line, mask in zip(halves, ("x", "x", "z", "z"), (3, 1, 3, 1))
    ]
    far = lax.optimization_barrier(far)
    rows = (
        whole_rows(x.reshape(1), [first] + came[:2] + far[:2]),
        whole_rows(z.reshape(1), [second] + came[2:] + far[2:]),
    )
    rows, picked = lax.optimization_barrier((rows, picked))
    embedded, ffn_rows = kernel_call(
        embed_kernel,
        "embed",
        [shape_of(BLOCK, jnp.float32), shape_of(BLOCK)],
        in_specs=[VMEM] * 2,
        out_specs=[VMEM] * 2,
    )(exchange(picked, CHIPS), ffn_gain)
    others = tuple(swap_cores(part) for part in rows)
    sums = logits_part(own_core, rows, heads)
    student, teacher, stats = logits_part(1 - own_core, others, heads, sums)
    stats = kernel_call(
        chip_stats_kernel,
        "chip_stats",
        shape_of((64, 8, 128), jnp.float32),
        limit=2,
        in_specs=[VMEM] * 2,
        out_specs=VMEM,
    )(stats, swap_cores(stats))
    stats, ffn_rows = lax.optimization_barrier((stats, ffn_rows))
    every = exchange(stats, CHIPS)

    weight = token_weight.reshape(2, 4, 2, 4, 2, 2).transpose(1, 3, 2, 4, 0, 5).reshape(1, 256)
    own, send, divergence = row_grad_part(
        own_core, every, weight, teacher, student, student_head_t
    )
    divergence = divergence.reshape(4, 4, 2, 2, 2, 2).transpose(4, 0, 2, 1, 3, 5).reshape(256)
    blocks = exchange(join_part(own, swap_cores(send)), CHIPS)
    final_grad, blocks = kernel_call(
        final_kernel,
        "final",
        [shape_of(BLOCK, jnp.float32), shape_of((64, 2 * BLOCK[0], BLOCK[1]))],
        limit=12,
        in_specs=[VMEM] * 4,
        out_specs=[VMEM] * 2,
        scratch_shapes=[pltpu.VMEM(BLOCK, jnp.float32)],
    )(blocks, student_states, student_gain, ffn_rows)
    blocks = exchange(blocks, CHIPS)
    weights = (down_weight, gate_t, up_t)
    others = swap_cores(blocks)
    own = ffn_grad_part(blocks, jnp.float32, *weights)
    others, own = lax.optimization_barrier((others, own))
    send = ffn_grad_part(others, jnp.bfloat16, *weights)
    ffn_grad = exchange(join_part(own, swap_cores(send)), CHIPS)
    state_grad = kernel_call(
        state_kernel,
        "state",
        shape_of((2, 4096), jnp.float32),
        in_specs=[VMEM] * 4,
        out_specs=VMEM,
    )(ffn_grad, final_grad, embedded, ffn_gain)
    return (divergence, state_grad)


def solution(mesh):
    fine = Mesh(mesh.devices.reshape(SHAPE), AXES)
    in_specs = (
        P(AXES, None),
        P(),
        P(None, AXES),
        P(AXES, None),
        P(),
        P(None, AXES),
        P(),
        P(),
        P(None, AXES),
        P(None, AXES),
        P(AXES, None),
        P(),
    )
    out_specs = (P(), P(AXES, None))
    return jax.shard_map(shards, mesh=fine, in_specs=in_specs, out_specs=out_specs, check_vma=False)
```

```python
import functools

import jax
import jax.numpy as jnp
from jax import lax
from jax.experimental import pallas as pl
from jax.experimental.pallas import tpu as pltpu
from jax.sharding import Mesh
from jax.sharding import PartitionSpec as P

eps = 1e-05
SHAPE = (2, 4, 2, 4, 2)
AXES = ("core", "x", "yh", "z", "yl")
CHIPS = AXES[1:]
MIB = 1024 * 1024

VMEM = pl.BlockSpec(memory_space=pltpu.VMEM)
SMEM = pl.BlockSpec(memory_space=pltpu.SMEM)
ANY = pl.BlockSpec(memory_space=pl.ANY)
SEGMENTS = 8
SEGMENT = 512


def kernel_call(body, name, out_shape, limit=8, **options):
    return pl.pallas_call(
        body,
        name=name,
        out_shape=out_shape,
        compiler_params=pltpu.CompilerParams(vmem_limit_bytes=limit * MIB),
        cost_estimate=pl.CostEstimate(flops=1, bytes_accessed=1, transcendentals=0),
        **options,
    )


def shape_of(shape, dtype=jnp.bfloat16):
    return jax.ShapeDtypeStruct(shape, dtype)


def row_product(left, right):
    return lax.dot_general(
        left, right, (((1,), (1,)), ((), ())), preferred_element_type=jnp.float32
    )


def swap_cores(values):
    return lax.ppermute(values, "core", [(0, 1), (1, 0)])


def exchange(blocks, axes):
    return lax.all_to_all(blocks, axes, split_axis=0, concat_axis=0, tiled=True)


def rows_kernel(
    core_ref, teacher_from, teacher_gain, student_from, student_gain, keep_ref, send_ref,
    teacher_ref, student_ref, teacher_gains, student_gains, gains, sems,
):
    copies = [
        pltpu.make_async_copy(source, target, sems.at[i])
        for i, (source, target) in enumerate(
            (
                (student_gain, student_gains),
                (student_from, student_ref),
                (teacher_gain, teacher_gains),
                (teacher_from, teacher_ref),
            )
        )
    ]
    for copy in copies:
        copy.start()
    for copy in copies:
        copy.wait()
    first = student_gain.shape[0]
    gains[:first, :] = student_gains[...].astype(jnp.float32)
    gains[first:, :] = teacher_gains[...].astype(jnp.float32)
    column = 0
    for values, base in ((student_ref, 0), (teacher_ref, first)):
        half = values.shape[1] // 2
        every = values[...].astype(jnp.float32)
        inverse = lax.rsqrt(jnp.mean(every * every, axis=-1, keepdims=True) + eps)
        for part, out in ((core_ref[0], keep_ref), (1 - core_ref[0], send_ref)):
            for k in range(half // 128):
                place = pl.ds(pl.multiple_of(part * half + k * 128, 128), 128)
                rows = values[:, place].astype(jnp.float32) * inverse
                rows = rows * gains[pl.ds(base + part * (half // 128) + k, 1), :]
                out[:, column + k * 128 : column + (k + 1) * 128] = rows.astype(jnp.bfloat16)
        column = column + half


def pair_kernel(place_ref, own_ref, came_ref, *out_refs):
    own, came = own_ref[...].astype(jnp.float32), came_ref[...].astype(jnp.float32)
    first = place_ref[0] == 0
    rows = jnp.concatenate([jnp.where(first, own, came), jnp.where(first, came, own)], axis=0)
    rows = rows.astype(jnp.bfloat16)
    column = 0
    for out in out_refs:
        out[...] = rows[:, column : column + out.shape[1]]
        column = column + out.shape[1]


def in_pair(bit, own, came, widths):
    tokens = 2 * own.shape[0]
    return kernel_call(
        pair_kernel,
        "pair",
        [shape_of((tokens, w)) for w in widths],
        in_specs=[SMEM] + [VMEM] * 2,
        out_specs=[VMEM] * len(widths),
    )(bit, own, came)


def groups_kernel(place_ref, *refs):
    count = (len(refs) - 1) // 3
    sources, outs, sems = refs[: 2 * count], refs[2 * count : -1], refs[-1]
    copies = []
    for g, out in enumerate(outs):
        for i in range(2):
            source = sources[2 * g + i]
            tokens = source.shape[0]
            at = pl.multiple_of((place_ref[g] ^ i) * tokens, tokens)
            copy = pltpu.make_async_copy(source, out.at[pl.ds(at, tokens), :], sems.at[2 * g + i])
            copy.start()
            copies.append(copy)
    for copy in copies:
        copy.wait()


def in_pairs(bits, parts):
    tokens = 2 * parts[0].shape[0]
    return kernel_call(
        groups_kernel,
        "pairs",
        [shape_of((tokens, part.shape[1])) for part in parts[::2]],
        limit=4,
        in_specs=[SMEM] + [ANY] * len(parts),
        out_specs=[VMEM] * (len(parts) // 2),
        scratch_shapes=[pltpu.SemaphoreType.DMA((len(parts),))],
    )(bits, *parts)


def halves_kernel(*refs):
    count = (len(refs) - 1) // 2
    copies = []
    for i, (piece, out) in enumerate(zip(refs[:count], refs[count:])):
        rows = out.shape[0]
        copy = pltpu.make_async_copy(piece.at[pl.ds((i % 2) * rows, rows), :], out, refs[-1].at[i])
        copy.start()
        copies.append(copy)
    for copy in copies:
        copy.wait()


def halves_of(pieces):
    return kernel_call(
        halves_kernel,
        "halves",
        [shape_of((p.shape[0] // 2, p.shape[1])) for p in pieces],
        limit=4,
        in_specs=[ANY] * len(pieces),
        out_specs=[VMEM] * len(pieces),
        scratch_shapes=[pltpu.SemaphoreType.DMA((len(pieces),))],
    )(*pieces)


def along(block, line, mask):
    return lax.ppermute(block, line, [(i, i ^ mask) for i in range(4)])


def whole_kernel(place_ref, *refs):
    pieces, out, sems = refs[:5], refs[5], refs[6]
    tokens = pieces[0].shape[0]
    copies = []
    for i, (mask, half) in enumerate(((0, 0), (1, 0), (3, 0), (2, 0), (2, 1))):
        at = (place_ref[0] ^ mask) * tokens + half * (tokens // 2)
        at = pl.multiple_of(at, tokens // 2)
        rows = pieces[i].shape[0]
        copy = pltpu.make_async_copy(pieces[i], out.at[pl.ds(at, rows), :], sems.at[i])
        copy.start()
        copies.append(copy)
    for copy in copies:
        copy.wait()


def whole_rows(place, pieces):
    tokens, width = pieces[0].shape
    return kernel_call(
        whole_kernel,
        "whole",
        shape_of((4 * tokens, width)),
        limit=6,
        in_specs=[SMEM] + [ANY] * 5,
        out_specs=VMEM,
        scratch_shapes=[pltpu.SemaphoreType.DMA((5,))],
    )(place, *pieces)


GROUPS = (
    ((0, 0, 2048), (1, 0, 3072)),
    ((1, 3072, 2560), (1, 5632, 2560)),
)
WIDTHS = tuple(sum(p[2] for p in group) for group in GROUPS)


def reordered(values):
    source = lax.broadcasted_iota(jnp.int32, (256, 256), 0)
    place = lax.broadcasted_iota(jnp.int32, (256, 256), 1)
    wanted = (((place >> 4) & 3) << 6) | (((place >> 6) & 3) << 4) | (place & 15)
    moves = (source == wanted).astype(jnp.bfloat16)
    high = values.astype(jnp.bfloat16)
    rest = values - high.astype(jnp.float32)
    middle = rest.astype(jnp.bfloat16)
    low = (rest - middle.astype(jnp.float32)).astype(jnp.bfloat16)
    high, middle, low = (
        jnp.dot(part, moves, preferred_element_type=jnp.float32) for part in (high, middle, low)
    )
    return (high + middle) + low


def softmax_stats(teacher, student, stats_out):
    teacher_peak = jnp.max(teacher, axis=0, keepdims=True)
    student_peak = jnp.max(student, axis=0, keepdims=True)
    teacher_exp = jnp.exp(teacher - teacher_peak)
    teacher_total = jnp.sum(teacher_exp, axis=0, keepdims=True)
    student_total = jnp.sum(jnp.exp(student - student_peak), axis=0, keepdims=True)
    cross = jnp.sum(teacher_exp * (teacher - student), axis=0, keepdims=True)
    stats = (
        teacher_peak + jnp.log(teacher_total),
        student_peak + jnp.log(student_total),
        cross / teacher_total,
    )
    rows = [row[:, :128] for row in stats] + [row[:, 128:] for row in stats]
    stats_out[...] = jnp.concatenate(rows + [jnp.zeros((2, 128), jnp.float32)], axis=0)


def logits_kernel(last, place_ref, *refs):
    rows_from, heads, refs = refs[:2], refs[2:4], refs[4:]
    rows, head, row_sems, head_sems = refs[-4:]
    refs = refs[:-4]
    copies = []
    column = 0
    for group, source in zip(GROUPS, rows_from):
        base = column
        for kind, start, width in group:
            i = len(copies)
            columns = slice(column, column + width)
            size = heads[kind].shape[1] // 2
            start = pl.multiple_of(place_ref[0] * size + start, 128)
            pair = (
                pltpu.make_async_copy(
                    source.at[:, column - base : column - base + width],
                    rows.at[:, columns],
                    row_sems.at[i],
                ),
                pltpu.make_async_copy(
                    heads[kind].at[:, pl.ds(start, width)], head.at[:, columns], head_sems.at[i]
                ),
            )
            copies.append((kind + (base > 0), columns, pair))
            column = column + width
    ahead = 2
    for _, _, pair in copies[:ahead]:
        for copy in pair:
            copy.start()
    sums = [None, None, None]
    for i, (kind, columns, pair) in enumerate(copies):
        for copy in pair:
            copy.wait()
        if i + ahead < len(copies):
            for copy in copies[i + ahead][2]:
                copy.start()
        term = row_product(head[:, columns], rows[:, columns])
        sums[kind] = term if sums[kind] is None else sums[kind] + term
    if last:
        came, (student_out, teacher_out, stats_out) = refs[:3], refs[3:]
        student, teacher, second = (total + ref[...] for total, ref in zip(sums, came))
        teacher = teacher + reordered(second)
        student_out[...] = student
        teacher_out[...] = teacher
        softmax_stats(teacher, student, stats_out)
    else:
        for total, out in zip(sums, refs):
            out[...] = total


def logits_part(place, rows, heads, sums=()):
    vocab, tokens = heads[1].shape[0], rows[0].shape[0]
    shape = shape_of((vocab, tokens), jnp.float32)
    last = len(sums) > 0
    pieces = sum(len(group) for group in GROUPS)
    out_shape = [shape, shape, shape_of((8, 128), jnp.float32) if last else shape]
    return kernel_call(
        functools.partial(logits_kernel, last),
        "logits",
        out_shape,
        limit=48,
        in_specs=[SMEM] + [ANY] * 4 + [VMEM] * len(sums),
        out_specs=[VMEM] * 3,
        scratch_shapes=[
            pltpu.VMEM((tokens, sum(WIDTHS)), jnp.bfloat16),
            pltpu.VMEM((vocab, sum(WIDTHS)), jnp.bfloat16),
            pltpu.SemaphoreType.DMA((pieces,)),
            pltpu.SemaphoreType.DMA((pieces,)),
        ],
    )(place, *rows, *heads, *sums)


def one_hot_rows(core):
    place = lax.broadcasted_iota(jnp.int32, (256, 256), 0)
    column = lax.broadcasted_iota(jnp.int32, (256, 256), 1)
    x, yh, z, yl = (place >> 4) & 3, (place >> 3) & 1, (place >> 1) & 3, place & 1
    source = (x << 6) | (z << 4) | (yh << 3) | (yl << 2)
    source = source | (((place >> 7) ^ core) << 1) | ((place >> 6) & 1)
    return (column == source).astype(jnp.bfloat16)


def head_copies(source, head, sems):
    columns = head.shape[1] // sems.shape[0]
    parts = [slice(i * columns, (i + 1) * columns) for i in range(sems.shape[0])]
    copies = [
        pltpu.make_async_copy(source.at[:, part], head.at[:, part], sems.at[i])
        for i, part in enumerate(parts)
    ]
    for copy in copies:
        copy.start()
    return list(zip(parts, copies))


def merged_stats(every):
    peak = jnp.max(every, axis=0)
    scaled = jnp.exp(every - peak[None])
    total = jnp.sum(scaled, axis=0)
    cross = jnp.sum(scaled * pltpu.roll(every, 6, 1), axis=0) / total
    return peak + jnp.log(total), cross


def chip_stats_kernel(own_ref, came_ref, out_ref):
    lse, cross = merged_stats(jnp.concatenate([own_ref[...][None], came_ref[...][None]], axis=0))
    row = lax.broadcasted_iota(jnp.int32, lse.shape, 0)
    merged = jnp.where((row == 2) | (row == 5), pltpu.roll(cross, 2, 0), lse)
    out_ref[...] = jnp.broadcast_to(merged[None], out_ref.shape)


def row_grad_kernel(
    core_ref, every_ref, weight_ref, teacher_ref, student_ref, head_from,
    own_ref, send_ref, divergence_ref, head, sems,
):
    copies = head_copies(head_from, head, sems)
    lse, cross = merged_stats(every_ref[...])
    teacher_lse = jnp.concatenate([lse[0:1], lse[3:4]], axis=1)
    student_lse = jnp.concatenate([lse[1:2], lse[4:5]], axis=1)
    divergence_ref[...] = (
        jnp.concatenate([cross[0:1], cross[3:4]], axis=1) - teacher_lse + student_lse
    )
    logit_grad = weight_ref[...] * (
        jnp.exp(student_ref[...] - student_lse) - jnp.exp(teacher_ref[...] - teacher_lse)
    )
    grad = row_product(one_hot_rows(core_ref[0]), logit_grad.astype(jnp.bfloat16))
    grad = grad.astype(jnp.bfloat16)
    half = own_ref.shape[0]
    for columns, copy in copies:
        copy.wait()
        out = jnp.dot(grad, head[:, columns], preferred_element_type=jnp.float32)
        own_ref[:, columns] = out[:half]
        send_ref[:, columns] = out[half:].astype(jnp.bfloat16)


def row_grad_part(core, every, weight, teacher, student, student_head_t):
    vocab, width = student_head_t.shape
    tokens = weight.shape[1]
    return kernel_call(
        row_grad_kernel,
        "row_grad",
        [
            shape_of((tokens // 2, width), jnp.float32),
            shape_of((tokens // 2, width)),
            shape_of((1, tokens), jnp.float32),
        ],
        limit=48,
        in_specs=[SMEM] + [VMEM] * 4 + [ANY],
        out_specs=[VMEM] * 3,
        scratch_shapes=[
            pltpu.VMEM((vocab, width), jnp.bfloat16),
            pltpu.SemaphoreType.DMA((4,)),
        ],
    )(core, every, weight, teacher, student, student_head_t)


def pick_kernel(place_ref, ids_ref, head_from, own_ref, send_ref, head, sems):
    copies = head_copies(head_from, head, sems)
    vocab, tokens = head.shape[0], ids_ref.shape[1]
    entry = lax.broadcasted_iota(jnp.int32, (vocab, tokens), 0) + place_ref[1] * vocab
    place = lax.broadcasted_iota(jnp.int32, (tokens, tokens), 0)
    column = lax.broadcasted_iota(jnp.int32, (tokens, tokens), 1)
    source = (((place >> 7) ^ place_ref[0]) << 7) | ((place & 63) << 1) | ((place >> 6) & 1)
    chosen = row_product(
        (column == source).astype(jnp.bfloat16), (ids_ref[...] == entry).astype(jnp.bfloat16)
    ).astype(jnp.bfloat16)
    half = own_ref.shape[0]
    for columns, copy in copies:
        copy.wait()
        out = jnp.dot(chosen, head[:, columns], preferred_element_type=jnp.float32)
        own_ref[:, columns] = out[:half].astype(jnp.bfloat16)
        send_ref[:, columns] = out[half:].astype(jnp.bfloat16)


def pick_part(place, ids, student_head_t):
    vocab, width = student_head_t.shape
    shape = shape_of((ids.shape[1] // 2, width))
    return kernel_call(
        pick_kernel,
        "pick",
        [shape, shape],
        limit=48,
        in_specs=[SMEM, VMEM, ANY],
        out_specs=[VMEM] * 2,
        scratch_shapes=[
            pltpu.VMEM((vocab, width), jnp.bfloat16),
            pltpu.SemaphoreType.DMA((4,)),
        ],
    )(place, ids, student_head_t)


def join_kernel(*refs):
    pairs, out_ref, rows = refs[:-2], refs[-2], refs[-1]
    chips, height = out_ref.shape[0], 2 * SEGMENTS
    for base, (own_ref, came_ref) in enumerate(zip(pairs[::2], pairs[1::2])):
        for t in range(2):
            for i in range(SEGMENTS):
                for k in range(SEGMENT // 128):
                    part = slice(t * chips, (t + 1) * chips)
                    lanes = slice(i * SEGMENT + k * 128, i * SEGMENT + (k + 1) * 128)
                    total = own_ref[part, lanes].astype(jnp.float32)
                    total = total + came_ref[part, lanes].astype(jnp.float32)
                    at = pl.ds(t * SEGMENTS + i, chips, stride=height)
                    rows[k, at, :] = total
        for k in range(SEGMENT // 128):
            out_ref[:, base * height : (base + 1) * height, k * 128 : (k + 1) * 128] = (
                rows[k].reshape(chips, height, 128).astype(jnp.bfloat16)
            )


def join_part(*pairs):
    chips = pairs[0].shape[0] // 2
    height = 2 * SEGMENTS
    return kernel_call(
        join_kernel,
        "join",
        shape_of((chips, height * len(pairs) // 2, SEGMENT)),
        limit=14,
        in_specs=[VMEM] * len(pairs),
        out_specs=VMEM,
        scratch_shapes=[pltpu.VMEM((SEGMENT // 128, chips * height, 128), jnp.float32)],
    )(*pairs)


def block_gain(gain_ref):
    gain = gain_ref[...].astype(jnp.float32)
    lanes = SEGMENT // 128
    token = jnp.concatenate(
        [
            jnp.concatenate([gain[lanes * i + k : lanes * i + k + 1] for k in range(lanes)], axis=1)
            for i in range(SEGMENTS)
        ],
        axis=0,
    )
    return jnp.concatenate([token, token], axis=0)


def block_mean(values):
    means = []
    for t in range(2):
        part = values[t * SEGMENTS : (t + 1) * SEGMENTS]
        total = jnp.sum(jnp.sum(part, axis=0, keepdims=True), axis=1, keepdims=True)
        means.append(jnp.broadcast_to(total / (SEGMENTS * SEGMENT), (SEGMENTS, 1)))
    return jnp.concatenate(means, axis=0)


def block_inverse(values):
    return lax.rsqrt(block_mean(values * values) + eps)


def block_back(upstream, values, gain):
    inverse = block_inverse(values)
    gained = upstream * gain
    return inverse * gained - values * inverse**3 * block_mean(gained * values)


def block_sum(blocks_ref):
    return jnp.sum(blocks_ref[...].astype(jnp.float32), axis=0)


def embed_kernel(blocks_ref, gain_ref, embedded_ref, rows_ref):
    values = block_sum(blocks_ref)
    embedded_ref[...] = values
    rows = values * block_inverse(values) * block_gain(gain_ref)
    rows_ref[...] = rows.astype(jnp.bfloat16)


def final_kernel(blocks_ref, states_ref, gain_ref, rows_ref, grad_ref, out_ref, states):
    for i in range(SEGMENTS):
        part = states_ref[:, i * SEGMENT : (i + 1) * SEGMENT].astype(jnp.float32)
        for t in range(2):
            states[t * SEGMENTS + i : t * SEGMENTS + i + 1, :] = part[t : t + 1]
    grad = block_back(block_sum(blocks_ref), states[...], block_gain(gain_ref))
    grad_ref[...] = grad
    height = 2 * SEGMENTS
    half = (out_ref.shape[0], height, SEGMENT)
    out_ref[:, :height, :] = jnp.broadcast_to(grad.astype(jnp.bfloat16)[None], half)
    out_ref[:, height:, :] = jnp.broadcast_to(rows_ref[...][None], half)


def state_kernel(blocks_ref, grad_ref, embedded_ref, gain_ref, out_ref):
    back = block_back(block_sum(blocks_ref), embedded_ref[...], block_gain(gain_ref))
    grad = grad_ref[...] + back
    for t in range(2):
        for i in range(SEGMENTS):
            out_ref[t : t + 1, i * SEGMENT : (i + 1) * SEGMENT] = grad[
                t * SEGMENTS + i : t * SEGMENTS + i + 1
            ]


BLOCK = (2 * SEGMENTS, SEGMENT)


def segment_rows(rows, first):
    height = 4 * SEGMENTS
    parts = []
    for t in range(2):
        at = pl.ds(first + t * SEGMENTS, rows.shape[1] // height, stride=height)
        parts.append(jnp.concatenate([rows[k, at, :] for k in range(SEGMENT // 128)], axis=1))
    return jnp.concatenate(parts, axis=0).astype(jnp.bfloat16)


def ffn_grad_kernel(blocks_ref, down_ref, gate_ref, up_ref, out_ref, rows):
    values = blocks_ref[...].astype(jnp.float32)
    values = values.reshape(values.shape[0] * values.shape[1], values.shape[2])
    for k in range(SEGMENT // 128):
        rows[k] = values[:, k * 128 : (k + 1) * 128]
    units = down_ref.shape[0]
    hidden, act_grad = None, None
    for i in range(SEGMENTS):
        columns = slice(i * SEGMENT, (i + 1) * SEGMENT)
        weight = jnp.concatenate([gate_ref[:, columns], up_ref[:, columns]], axis=0)
        term = row_product(weight, segment_rows(rows, 2 * SEGMENTS + i))
        hidden = term if hidden is None else hidden + term
        term = row_product(down_ref[:, columns], segment_rows(rows, i))
        act_grad = term if act_grad is None else act_grad + term
    gate, upper = hidden[:units, :], hidden[units:, :]
    sigmoid_gate = jax.nn.sigmoid(gate)
    gate_grad = act_grad * upper * sigmoid_gate * (1.0 + gate * (1.0 - sigmoid_gate))
    upper_grad = act_grad * gate * sigmoid_gate
    grads = jnp.concatenate([gate_grad, upper_grad], axis=0).astype(jnp.bfloat16)
    tokens = grads.shape[1]
    same = lax.broadcasted_iota(jnp.int32, (tokens, tokens), 0) == lax.broadcasted_iota(
        jnp.int32, (tokens, tokens), 1
    )
    grads = row_product(same.astype(jnp.bfloat16), grads).astype(jnp.bfloat16)
    for i in range(SEGMENTS):
        columns = slice(i * SEGMENT, (i + 1) * SEGMENT)
        weight = jnp.concatenate([gate_ref[:, columns], up_ref[:, columns]], axis=0)
        out = jnp.dot(grads, weight, preferred_element_type=jnp.float32)
        out_ref[:, columns] = out.astype(out_ref.dtype)


def ffn_grad_part(blocks, dtype, *weights):
    chips, height, _ = blocks.shape
    return kernel_call(
        ffn_grad_kernel,
        "ffn_grad",
        shape_of((2 * chips, SEGMENTS * SEGMENT), dtype),
        limit=20,
        in_specs=[VMEM] * (1 + len(weights)),
        out_specs=VMEM,
        scratch_shapes=[pltpu.VMEM((SEGMENT // 128, chips * height, 128), jnp.float32)],
    )(blocks, *weights)


def shards(
    teacher_states,
    teacher_gain,
    teacher_head,
    student_states,
    student_gain,
    student_head,
    token_ids,
    ffn_gain,
    gate_weight,
    up_weight,
    down_weight,
    token_weight,
):
    core = lax.axis_index("core")
    device = lax.axis_index(AXES)
    own_core = jnp.full((1,), core, jnp.int32)
    x, z, y = (lax.axis_index(line).astype(jnp.int32) for line in ("x", "z", ("yh", "yl")))
    teacher_gain, student_gain, ffn_gain = (
        gain.reshape(-1, 128) for gain in (teacher_gain, student_gain, ffn_gain)
    )
    student_head_t, teacher_head_t = student_head.T, teacher_head.T
    heads = (student_head_t, teacher_head_t)
    gate_t, up_t = gate_weight.T, up_weight.T

    width = sum(WIDTHS)
    half_shape = shape_of((2, width))
    keep, send = kernel_call(
        rows_kernel,
        "rows",
        [half_shape, half_shape],
        limit=56,
        in_specs=[SMEM] + [ANY] * 4,
        out_specs=[VMEM] * 2,
        scratch_shapes=[
            pltpu.VMEM(teacher_states.shape, jnp.bfloat16),
            pltpu.VMEM(student_states.shape, jnp.bfloat16),
            pltpu.VMEM(teacher_gain.shape, jnp.bfloat16),
            pltpu.VMEM(student_gain.shape, jnp.bfloat16),
            pltpu.VMEM((160, 128), jnp.float32),
            pltpu.SemaphoreType.DMA((4,)),
        ],
    )(own_core, teacher_states, teacher_gain, student_states, student_gain)
    (rows,) = in_pair(own_core, keep, swap_cores(send), (width,))

    (rows,) = in_pair((y & 1).reshape(1), rows, along(rows, ("yh", "yl"), 1), (width,))
    first, second = in_pair((y >> 1).reshape(1), rows, along(rows, ("yh", "yl"), 3), WIDTHS)
    for bit, mask in ((0, 1), (1, 3)):
        came = (along(first, "z", mask), along(second, "x", mask))
        bits = (jnp.stack([z, x]) >> bit) & 1
        first, second = in_pairs(bits, (first, came[0], second, came[1]))
    ids = token_ids.reshape(1, 256)
    ids, first, second = lax.optimization_barrier((ids, first, second))
    came = [along(first, "x", 1), along(first, "x", 3), along(second, "z", 1), along(second, "z", 3)]
    place = jnp.stack([core, device]).astype(jnp.int32)
    own, send = pick_part(place, ids, student_head_t)
    came, picked = lax.optimization_barrier((came, join_part(own, swap_cores(send))))
    halves = halves_of(came)
    far = [
        along(half, line, mask)
        for half, line, mask in zip(halves, ("x", "x", "z", "z"), (3, 1, 3, 1))
    ]
    far = lax.optimization_barrier(far)
    rows = (
        whole_rows(x.reshape(1), [first] + came[:2] + far[:2]),
        whole_rows(z.reshape(1), [second] + came[2:] + far[2:]),
    )
    rows, picked = lax.optimization_barrier((rows, picked))
    picked = exchange(picked, CHIPS)
    others = tuple(swap_cores(part) for part in rows)
    sums = logits_part(own_core, rows, heads)
    student, teacher, stats = logits_part(1 - own_core, others, heads, sums)
    stats = kernel_call(
        chip_stats_kernel,
        "chip_stats",
        shape_of((64, 8, 128), jnp.float32),
        limit=2,
        in_specs=[VMEM] * 2,
        out_specs=VMEM,
    )(stats, swap_cores(stats))
    stats, picked = lax.optimization_barrier((stats, picked))
    every = exchange(stats, CHIPS)
    embedded, ffn_rows = kernel_call(
        embed_kernel,
        "embed",
        [shape_of(BLOCK, jnp.float32), shape_of(BLOCK)],
        in_specs=[VMEM] * 2,
        out_specs=[VMEM] * 2,
    )(picked, ffn_gain)

    weight = token_weight.reshape(2, 4, 2, 4, 2, 2).transpose(1, 3, 2, 4, 0, 5).reshape(1, 256)
    own, send, divergence = row_grad_part(
        own_core, every, weight, teacher, student, student_head_t
    )
    divergence = divergence.reshape(4, 4, 2, 2, 2, 2).transpose(4, 0, 2, 1, 3, 5).reshape(256)
    blocks = exchange(join_part(own, swap_cores(send)), CHIPS)
    final_grad, blocks = kernel_call(
        final_kernel,
        "final",
        [shape_of(BLOCK, jnp.float32), shape_of((64, 2 * BLOCK[0], BLOCK[1]))],
        limit=12,
        in_specs=[VMEM] * 4,
        out_specs=[VMEM] * 2,
        scratch_shapes=[pltpu.VMEM(BLOCK, jnp.float32)],
    )(blocks, student_states, student_gain, ffn_rows)
    blocks = exchange(blocks, CHIPS)
    weights = (down_weight, gate_t, up_t)
    others = swap_cores(blocks)
    own = ffn_grad_part(blocks, jnp.float32, *weights)
    others, own = lax.optimization_barrier((others, own))
    send = ffn_grad_part(others, jnp.bfloat16, *weights)
    ffn_grad = exchange(join_part(own, swap_cores(send)), CHIPS)
    state_grad = kernel_call(
        state_kernel,
        "state",
        shape_of((2, 4096), jnp.float32),
        in_specs=[VMEM] * 4,
        out_specs=VMEM,
    )(ffn_grad, final_grad, embedded, ffn_gain)
    return (divergence, state_grad)


def solution(mesh):
    fine = Mesh(mesh.devices.reshape(SHAPE), AXES)
    in_specs = (
        P(AXES, None),
        P(),
        P(None, AXES),
        P(AXES, None),
        P(),
        P(None, AXES),
        P(),
        P(),
        P(None, AXES),
        P(None, AXES),
        P(AXES, None),
        P(),
    )
    out_specs = (P(), P(AXES, None))
    return jax.shard_map(shards, mesh=fine, in_specs=in_specs, out_specs=out_specs, check_vma=False)
```

```python
import functools

import jax
import jax.numpy as jnp
from jax import lax
from jax.experimental import pallas as pl
from jax.experimental.pallas import tpu as pltpu
from jax.sharding import Mesh
from jax.sharding import PartitionSpec as P

eps = 1e-05
SHAPE = (2, 4, 2, 4, 2)
AXES = ("core", "x", "yh", "z", "yl")
CHIPS = AXES[1:]
MIB = 1024 * 1024

VMEM = pl.BlockSpec(memory_space=pltpu.VMEM)
SMEM = pl.BlockSpec(memory_space=pltpu.SMEM)
ANY = pl.BlockSpec(memory_space=pl.ANY)
SEGMENTS = 8
SEGMENT = 512


def kernel_call(body, name, out_shape, limit=8, **options):
    return pl.pallas_call(
        body,
        name=name,
        out_shape=out_shape,
        compiler_params=pltpu.CompilerParams(vmem_limit_bytes=limit * MIB),
        cost_estimate=pl.CostEstimate(flops=1, bytes_accessed=1, transcendentals=0),
        **options,
    )


def shape_of(shape, dtype=jnp.bfloat16):
    return jax.ShapeDtypeStruct(shape, dtype)


def row_product(left, right):
    return lax.dot_general(
        left, right, (((1,), (1,)), ((), ())), preferred_element_type=jnp.float32
    )


def swap_cores(values):
    return lax.ppermute(values, "core", [(0, 1), (1, 0)])


def exchange(blocks, axes):
    return lax.all_to_all(blocks, axes, split_axis=0, concat_axis=0, tiled=True)


def rows_kernel(
    core_ref, teacher_from, teacher_gain, student_from, student_gain, keep_ref, send_ref,
    teacher_ref, student_ref, teacher_gains, student_gains, gains, sems,
):
    copies = [
        pltpu.make_async_copy(source, target, sems.at[i])
        for i, (source, target) in enumerate(
            (
                (student_gain, student_gains),
                (student_from, student_ref),
                (teacher_gain, teacher_gains),
                (teacher_from, teacher_ref),
            )
        )
    ]
    for copy in copies:
        copy.start()
    for copy in copies:
        copy.wait()
    first = student_gain.shape[0]
    gains[:first, :] = student_gains[...].astype(jnp.float32)
    gains[first:, :] = teacher_gains[...].astype(jnp.float32)
    column = 0
    for values, base in ((student_ref, 0), (teacher_ref, first)):
        half = values.shape[1] // 2
        every = values[...].astype(jnp.float32)
        inverse = lax.rsqrt(jnp.mean(every * every, axis=-1, keepdims=True) + eps)
        for part, out in ((core_ref[0], keep_ref), (1 - core_ref[0], send_ref)):
            for k in range(half // 128):
                place = pl.ds(pl.multiple_of(part * half + k * 128, 128), 128)
                rows = values[:, place].astype(jnp.float32) * inverse
                rows = rows * gains[pl.ds(base + part * (half // 128) + k, 1), :]
                out[:, column + k * 128 : column + (k + 1) * 128] = rows.astype(jnp.bfloat16)
        column = column + half


def pair_kernel(place_ref, own_ref, came_ref, *out_refs):
    own, came = own_ref[...].astype(jnp.float32), came_ref[...].astype(jnp.float32)
    first = place_ref[0] == 0
    rows = jnp.concatenate([jnp.where(first, own, came), jnp.where(first, came, own)], axis=0)
    rows = rows.astype(jnp.bfloat16)
    column = 0
    for out in out_refs:
        out[...] = rows[:, column : column + out.shape[1]]
        column = column + out.shape[1]


def in_pair(bit, own, came, widths):
    tokens = 2 * own.shape[0]
    return kernel_call(
        pair_kernel,
        "pair",
        [shape_of((tokens, w)) for w in widths],
        in_specs=[SMEM] + [VMEM] * 2,
        out_specs=[VMEM] * len(widths),
    )(bit, own, came)


def groups_kernel(place_ref, *refs):
    count = (len(refs) - 1) // 3
    sources, outs, sems = refs[: 2 * count], refs[2 * count : -1], refs[-1]
    copies = []
    for g, out in enumerate(outs):
        for i in range(2):
            source = sources[2 * g + i]
            tokens = source.shape[0]
            at = pl.multiple_of((place_ref[g] ^ i) * tokens, tokens)
            copy = pltpu.make_async_copy(source, out.at[pl.ds(at, tokens), :], sems.at[2 * g + i])
            copy.start()
            copies.append(copy)
    for copy in copies:
        copy.wait()


def in_pairs(bits, parts):
    tokens = 2 * parts[0].shape[0]
    return kernel_call(
        groups_kernel,
        "pairs",
        [shape_of((tokens, part.shape[1])) for part in parts[::2]],
        limit=4,
        in_specs=[SMEM] + [ANY] * len(parts),
        out_specs=[VMEM] * (len(parts) // 2),
        scratch_shapes=[pltpu.SemaphoreType.DMA((len(parts),))],
    )(bits, *parts)


def halves_kernel(*refs):
    count = (len(refs) - 1) // 2
    copies = []
    for i, (piece, out) in enumerate(zip(refs[:count], refs[count:])):
        rows = out.shape[0]
        copy = pltpu.make_async_copy(piece.at[pl.ds((i % 2) * rows, rows), :], out, refs[-1].at[i])
        copy.start()
        copies.append(copy)
    for copy in copies:
        copy.wait()


def halves_of(pieces):
    return kernel_call(
        halves_kernel,
        "halves",
        [shape_of((p.shape[0] // 2, p.shape[1])) for p in pieces],
        limit=4,
        in_specs=[ANY] * len(pieces),
        out_specs=[VMEM] * len(pieces),
        scratch_shapes=[pltpu.SemaphoreType.DMA((len(pieces),))],
    )(*pieces)


def along(block, line, mask):
    return lax.ppermute(block, line, [(i, i ^ mask) for i in range(4)])


def whole_kernel(place_ref, *refs):
    pieces, out, sems = refs[:5], refs[5], refs[6]
    tokens = pieces[0].shape[0]
    copies = []
    for i, (mask, half) in enumerate(((0, 0), (1, 0), (3, 0), (2, 0), (2, 1))):
        at = (place_ref[0] ^ mask) * tokens + half * (tokens // 2)
        at = pl.multiple_of(at, tokens // 2)
        rows = pieces[i].shape[0]
        copy = pltpu.make_async_copy(pieces[i], out.at[pl.ds(at, rows), :], sems.at[i])
        copy.start()
        copies.append(copy)
    for copy in copies:
        copy.wait()


def whole_rows(place, pieces):
    tokens, width = pieces[0].shape
    return kernel_call(
        whole_kernel,
        "whole",
        shape_of((4 * tokens, width)),
        limit=6,
        in_specs=[SMEM] + [ANY] * 5,
        out_specs=VMEM,
        scratch_shapes=[pltpu.SemaphoreType.DMA((5,))],
    )(place, *pieces)


GROUPS = (
    ((0, 0, 2048), (1, 0, 3072)),
    ((1, 3072, 2560), (1, 5632, 2560)),
)
WIDTHS = tuple(sum(p[2] for p in group) for group in GROUPS)


def reordered(values):
    source = lax.broadcasted_iota(jnp.int32, (256, 256), 0)
    place = lax.broadcasted_iota(jnp.int32, (256, 256), 1)
    wanted = (((place >> 4) & 3) << 6) | (((place >> 6) & 3) << 4) | (place & 15)
    moves = (source == wanted).astype(jnp.bfloat16)
    high = values.astype(jnp.bfloat16)
    rest = values - high.astype(jnp.float32)
    middle = rest.astype(jnp.bfloat16)
    low = (rest - middle.astype(jnp.float32)).astype(jnp.bfloat16)
    high, middle, low = (
        jnp.dot(part, moves, preferred_element_type=jnp.float32) for part in (high, middle, low)
    )
    return (high + middle) + low


def softmax_stats(teacher, student, stats_out):
    teacher_peak = jnp.max(teacher, axis=0, keepdims=True)
    student_peak = jnp.max(student, axis=0, keepdims=True)
    teacher_exp = jnp.exp(teacher - teacher_peak)
    teacher_total = jnp.sum(teacher_exp, axis=0, keepdims=True)
    student_total = jnp.sum(jnp.exp(student - student_peak), axis=0, keepdims=True)
    cross = jnp.sum(teacher_exp * (teacher - student), axis=0, keepdims=True)
    stats = (
        teacher_peak + jnp.log(teacher_total),
        student_peak + jnp.log(student_total),
        cross / teacher_total,
    )
    rows = [row[:, :128] for row in stats] + [row[:, 128:] for row in stats]
    stats_out[...] = jnp.concatenate(rows + [jnp.zeros((2, 128), jnp.float32)], axis=0)


def logits_kernel(last, place_ref, *refs):
    rows_from, heads, refs = refs[:2], refs[2:4], refs[4:]
    rows, head, row_sems, head_sems = refs[-4:]
    refs = refs[:-4]
    copies = []
    column = 0
    for group, source in zip(GROUPS, rows_from):
        base = column
        for kind, start, width in group:
            i = len(copies)
            columns = slice(column, column + width)
            size = heads[kind].shape[1] // 2
            start = pl.multiple_of(place_ref[0] * size + start, 128)
            pair = (
                pltpu.make_async_copy(
                    source.at[:, column - base : column - base + width],
                    rows.at[:, columns],
                    row_sems.at[i],
                ),
                pltpu.make_async_copy(
                    heads[kind].at[:, pl.ds(start, width)], head.at[:, columns], head_sems.at[i]
                ),
            )
            copies.append((kind + (base > 0), columns, pair))
            column = column + width
    ahead = 2
    for _, _, pair in copies[:ahead]:
        for copy in pair:
            copy.start()
    sums = [None, None, None]
    for i, (kind, columns, pair) in enumerate(copies):
        for copy in pair:
            copy.wait()
        if i + ahead < len(copies):
            for copy in copies[i + ahead][2]:
                copy.start()
        term = row_product(head[:, columns], rows[:, columns])
        sums[kind] = term if sums[kind] is None else sums[kind] + term
    if last:
        came, (student_out, teacher_out, stats_out) = refs[:3], refs[3:]
        student, teacher, second = (total + ref[...] for total, ref in zip(sums, came))
        teacher = teacher + reordered(second)
        student_out[...] = student
        teacher_out[...] = teacher
        softmax_stats(teacher, student, stats_out)
    else:
        for total, out in zip(sums, refs):
            out[...] = total


def logits_part(place, rows, heads, sums=()):
    vocab, tokens = heads[1].shape[0], rows[0].shape[0]
    shape = shape_of((vocab, tokens), jnp.float32)
    last = len(sums) > 0
    pieces = sum(len(group) for group in GROUPS)
    out_shape = [shape, shape, shape_of((8, 128), jnp.float32) if last else shape]
    return kernel_call(
        functools.partial(logits_kernel, last),
        "logits",
        out_shape,
        limit=48,
        in_specs=[SMEM] + [ANY] * 4 + [VMEM] * len(sums),
        out_specs=[VMEM] * 3,
        scratch_shapes=[
            pltpu.VMEM((tokens, sum(WIDTHS)), jnp.bfloat16),
            pltpu.VMEM((vocab, sum(WIDTHS)), jnp.bfloat16),
            pltpu.SemaphoreType.DMA((pieces,)),
            pltpu.SemaphoreType.DMA((pieces,)),
        ],
    )(place, *rows, *heads, *sums)


def one_hot_rows(core):
    place = lax.broadcasted_iota(jnp.int32, (256, 256), 0)
    column = lax.broadcasted_iota(jnp.int32, (256, 256), 1)
    x, yh, z, yl = (place >> 4) & 3, (place >> 3) & 1, (place >> 1) & 3, place & 1
    source = (x << 6) | (z << 4) | (yh << 3) | (yl << 2)
    source = source | (((place >> 7) ^ core) << 1) | ((place >> 6) & 1)
    return (column == source).astype(jnp.bfloat16)


def head_copies(source, head, sems):
    columns = head.shape[1] // sems.shape[0]
    parts = [slice(i * columns, (i + 1) * columns) for i in range(sems.shape[0])]
    copies = [
        pltpu.make_async_copy(source.at[:, part], head.at[:, part], sems.at[i])
        for i, part in enumerate(parts)
    ]
    for copy in copies:
        copy.start()
    return list(zip(parts, copies))


def merged_stats(every):
    peak = jnp.max(every, axis=0)
    scaled = jnp.exp(every - peak[None])
    total = jnp.sum(scaled, axis=0)
    cross = jnp.sum(scaled * pltpu.roll(every, 6, 1), axis=0) / total
    return peak + jnp.log(total), cross


def chip_stats_kernel(own_ref, came_ref, out_ref):
    lse, cross = merged_stats(jnp.concatenate([own_ref[...][None], came_ref[...][None]], axis=0))
    row = lax.broadcasted_iota(jnp.int32, lse.shape, 0)
    merged = jnp.where((row == 2) | (row == 5), pltpu.roll(cross, 2, 0), lse)
    out_ref[...] = jnp.broadcast_to(merged[None], out_ref.shape)


def row_grad_kernel(
    core_ref, every_ref, weight_ref, teacher_ref, student_ref, head_from,
    own_ref, send_ref, divergence_ref, head, sems,
):
    copies = head_copies(head_from, head, sems)
    lse, cross = merged_stats(every_ref[...])
    teacher_lse = jnp.concatenate([lse[0:1], lse[3:4]], axis=1)
    student_lse = jnp.concatenate([lse[1:2], lse[4:5]], axis=1)
    divergence_ref[...] = (
        jnp.concatenate([cross[0:1], cross[3:4]], axis=1) - teacher_lse + student_lse
    )
    logit_grad = weight_ref[...] * (
        jnp.exp(student_ref[...] - student_lse) - jnp.exp(teacher_ref[...] - teacher_lse)
    )
    grad = row_product(one_hot_rows(core_ref[0]), logit_grad.astype(jnp.bfloat16))
    grad = grad.astype(jnp.bfloat16)
    half = own_ref.shape[0]
    for columns, copy in copies:
        copy.wait()
        out = jnp.dot(grad, head[:, columns], preferred_element_type=jnp.float32)
        own_ref[:, columns] = out[:half]
        send_ref[:, columns] = out[half:].astype(jnp.bfloat16)


def row_grad_part(core, every, weight, teacher, student, student_head_t):
    vocab, width = student_head_t.shape
    tokens = weight.shape[1]
    return kernel_call(
        row_grad_kernel,
        "row_grad",
        [
            shape_of((tokens // 2, width), jnp.float32),
            shape_of((tokens // 2, width)),
            shape_of((1, tokens), jnp.float32),
        ],
        limit=48,
        in_specs=[SMEM] + [VMEM] * 4 + [ANY],
        out_specs=[VMEM] * 3,
        scratch_shapes=[
            pltpu.VMEM((vocab, width), jnp.bfloat16),
            pltpu.SemaphoreType.DMA((4,)),
        ],
    )(core, every, weight, teacher, student, student_head_t)


def pick_kernel(place_ref, ids_ref, head_from, own_ref, send_ref, head, sems):
    copies = head_copies(head_from, head, sems)
    vocab, tokens = head.shape[0], ids_ref.shape[1]
    entry = lax.broadcasted_iota(jnp.int32, (vocab, tokens), 0) + place_ref[1] * vocab
    place = lax.broadcasted_iota(jnp.int32, (tokens, tokens), 0)
    column = lax.broadcasted_iota(jnp.int32, (tokens, tokens), 1)
    source = (((place >> 7) ^ place_ref[0]) << 7) | ((place & 63) << 1) | ((place >> 6) & 1)
    chosen = row_product(
        (column == source).astype(jnp.bfloat16), (ids_ref[...] == entry).astype(jnp.bfloat16)
    ).astype(jnp.bfloat16)
    half = own_ref.shape[0]
    for columns, copy in copies:
        copy.wait()
        out = jnp.dot(chosen, head[:, columns], preferred_element_type=jnp.float32)
        own_ref[:, columns] = out[:half].astype(jnp.bfloat16)
        send_ref[:, columns] = out[half:].astype(jnp.bfloat16)


def pick_part(place, ids, student_head_t):
    vocab, width = student_head_t.shape
    shape = shape_of((ids.shape[1] // 2, width))
    return kernel_call(
        pick_kernel,
        "pick",
        [shape, shape],
        limit=48,
        in_specs=[SMEM, VMEM, ANY],
        out_specs=[VMEM] * 2,
        scratch_shapes=[
            pltpu.VMEM((vocab, width), jnp.bfloat16),
            pltpu.SemaphoreType.DMA((4,)),
        ],
    )(place, ids, student_head_t)


def join_kernel(own_ref, came_ref, *refs):
    out_ref, rows = refs[-2:]
    chips, height = out_ref.shape[0], 2 * SEGMENTS
    for t in range(2):
        for i in range(SEGMENTS):
            for k in range(SEGMENT // 128):
                part = slice(t * chips, (t + 1) * chips)
                lanes = slice(i * SEGMENT + k * 128, i * SEGMENT + (k + 1) * 128)
                total = own_ref[part, lanes].astype(jnp.float32)
                total = total + came_ref[part, lanes].astype(jnp.float32)
                rows[k, pl.ds(t * SEGMENTS + i, chips, stride=height), :] = total
    for k in range(SEGMENT // 128):
        out_ref[:, :height, k * 128 : (k + 1) * 128] = (
            rows[k].reshape(chips, height, 128).astype(jnp.bfloat16)
        )
    if len(refs) > 2:
        out_ref[:, height:, :] = jnp.broadcast_to(refs[0][...][None], (chips, height, SEGMENT))


def join_part(own, came, *every):
    chips, height = own.shape[0] // 2, 2 * SEGMENTS
    return kernel_call(
        join_kernel,
        "join",
        shape_of((chips, height * (1 + len(every)), SEGMENT)),
        limit=14,
        in_specs=[VMEM] * (2 + len(every)),
        out_specs=VMEM,
        scratch_shapes=[pltpu.VMEM((SEGMENT // 128, chips * height, 128), jnp.float32)],
    )(own, came, *every)


def block_gain(gain_ref):
    gain = gain_ref[...].astype(jnp.float32)
    lanes = SEGMENT // 128
    token = jnp.concatenate(
        [
            jnp.concatenate([gain[lanes * i + k : lanes * i + k + 1] for k in range(lanes)], axis=1)
            for i in range(SEGMENTS)
        ],
        axis=0,
    )
    return jnp.concatenate([token, token], axis=0)


def block_mean(values):
    means = []
    for t in range(2):
        part = values[t * SEGMENTS : (t + 1) * SEGMENTS]
        total = jnp.sum(jnp.sum(part, axis=0, keepdims=True), axis=1, keepdims=True)
        means.append(jnp.broadcast_to(total / (SEGMENTS * SEGMENT), (SEGMENTS, 1)))
    return jnp.concatenate(means, axis=0)


def block_inverse(values):
    return lax.rsqrt(block_mean(values * values) + eps)


def block_back(upstream, values, gain):
    inverse = block_inverse(values)
    gained = upstream * gain
    return inverse * gained - values * inverse**3 * block_mean(gained * values)


def block_sum(blocks_ref):
    return jnp.sum(blocks_ref[:, : 2 * SEGMENTS, :].astype(jnp.float32), axis=0)


def embed_kernel(blocks_ref, gain_ref, embedded_ref, rows_ref):
    values = block_sum(blocks_ref)
    embedded_ref[...] = values
    rows = values * block_inverse(values) * block_gain(gain_ref)
    rows_ref[...] = rows.astype(jnp.bfloat16)


def final_kernel(blocks_ref, states_ref, gain_ref, grad_ref, out_ref, states):
    for i in range(SEGMENTS):
        part = states_ref[:, i * SEGMENT : (i + 1) * SEGMENT].astype(jnp.float32)
        for t in range(2):
            states[t * SEGMENTS + i : t * SEGMENTS + i + 1, :] = part[t : t + 1]
    grad = block_back(block_sum(blocks_ref), states[...], block_gain(gain_ref))
    grad_ref[...] = grad
    out_ref[...] = jnp.broadcast_to(grad.astype(jnp.bfloat16)[None], out_ref.shape)


def state_kernel(blocks_ref, grad_ref, embedded_ref, gain_ref, out_ref):
    back = block_back(block_sum(blocks_ref), embedded_ref[...], block_gain(gain_ref))
    grad = grad_ref[...] + back
    for t in range(2):
        for i in range(SEGMENTS):
            out_ref[t : t + 1, i * SEGMENT : (i + 1) * SEGMENT] = grad[
                t * SEGMENTS + i : t * SEGMENTS + i + 1
            ]


BLOCK = (2 * SEGMENTS, SEGMENT)


def spread_rows(values, rows):
    values = values.astype(jnp.float32)
    values = values.reshape(values.shape[0] * values.shape[1], values.shape[2])
    for k in range(SEGMENT // 128):
        rows[k] = values[:, k * 128 : (k + 1) * 128]


def segment_rows(rows, segment):
    height = 2 * SEGMENTS
    parts = []
    for t in range(2):
        at = pl.ds(t * SEGMENTS + segment, rows.shape[1] // height, stride=height)
        parts.append(jnp.concatenate([rows[k, at, :] for k in range(SEGMENT // 128)], axis=1))
    return jnp.concatenate(parts, axis=0).astype(jnp.bfloat16)


def gate_kernel(own_ref, other_ref, gate_ref, up_ref, *refs):
    rows = refs[-1]
    for ref, out in zip((own_ref, other_ref), refs):
        spread_rows(ref[:, 2 * SEGMENTS :, :], rows)
        hidden = None
        for i in range(SEGMENTS):
            columns = slice(i * SEGMENT, (i + 1) * SEGMENT)
            weight = jnp.concatenate([gate_ref[:, columns], up_ref[:, columns]], axis=0)
            term = row_product(weight, segment_rows(rows, i))
            hidden = term if hidden is None else hidden + term
        out[...] = hidden


def ffn_grad_kernel(blocks_ref, hidden_ref, down_ref, gate_ref, up_ref, out_ref, rows):
    spread_rows(blocks_ref[...], rows)
    units = down_ref.shape[0]
    act_grad = None
    for i in range(SEGMENTS):
        columns = slice(i * SEGMENT, (i + 1) * SEGMENT)
        term = row_product(down_ref[:, columns], segment_rows(rows, i))
        act_grad = term if act_grad is None else act_grad + term
    gate, upper = hidden_ref[:units, :], hidden_ref[units:, :]
    sigmoid_gate = jax.nn.sigmoid(gate)
    gate_grad = act_grad * upper * sigmoid_gate * (1.0 + gate * (1.0 - sigmoid_gate))
    upper_grad = act_grad * gate * sigmoid_gate
    grads = jnp.concatenate([gate_grad, upper_grad], axis=0).astype(jnp.bfloat16)
    tokens = grads.shape[1]
    same = lax.broadcasted_iota(jnp.int32, (tokens, tokens), 0) == lax.broadcasted_iota(
        jnp.int32, (tokens, tokens), 1
    )
    grads = row_product(same.astype(jnp.bfloat16), grads).astype(jnp.bfloat16)
    for i in range(SEGMENTS):
        columns = slice(i * SEGMENT, (i + 1) * SEGMENT)
        weight = jnp.concatenate([gate_ref[:, columns], up_ref[:, columns]], axis=0)
        out = jnp.dot(grads, weight, preferred_element_type=jnp.float32)
        out_ref[:, columns] = out.astype(out_ref.dtype)


def ffn_part(body, name, out_shape, *operands):
    return kernel_call(
        body,
        name,
        out_shape,
        limit=20,
        in_specs=[VMEM] * len(operands),
        out_specs=[VMEM] * len(out_shape),
        scratch_shapes=[pltpu.VMEM((SEGMENT // 128, 64 * 2 * SEGMENTS, 128), jnp.float32)],
    )(*operands)


def shards(
    teacher_states,
    teacher_gain,
    teacher_head,
    student_states,
    student_gain,
    student_head,
    token_ids,
    ffn_gain,
    gate_weight,
    up_weight,
    down_weight,
    token_weight,
):
    core = lax.axis_index("core")
    device = lax.axis_index(AXES)
    own_core = jnp.full((1,), core, jnp.int32)
    x, z, y = (lax.axis_index(line).astype(jnp.int32) for line in ("x", "z", ("yh", "yl")))
    teacher_gain, student_gain, ffn_gain = (
        gain.reshape(-1, 128) for gain in (teacher_gain, student_gain, ffn_gain)
    )
    student_head_t, teacher_head_t = student_head.T, teacher_head.T
    heads = (student_head_t, teacher_head_t)
    gate_t, up_t = gate_weight.T, up_weight.T

    width = sum(WIDTHS)
    half_shape = shape_of((2, width))
    keep, send = kernel_call(
        rows_kernel,
        "rows",
        [half_shape, half_shape],
        limit=56,
        in_specs=[SMEM] + [ANY] * 4,
        out_specs=[VMEM] * 2,
        scratch_shapes=[
            pltpu.VMEM(teacher_states.shape, jnp.bfloat16),
            pltpu.VMEM(student_states.shape, jnp.bfloat16),
            pltpu.VMEM(teacher_gain.shape, jnp.bfloat16),
            pltpu.VMEM(student_gain.shape, jnp.bfloat16),
            pltpu.VMEM((160, 128), jnp.float32),
            pltpu.SemaphoreType.DMA((4,)),
        ],
    )(own_core, teacher_states, teacher_gain, student_states, student_gain)
    (rows,) = in_pair(own_core, keep, swap_cores(send), (width,))

    (rows,) = in_pair((y & 1).reshape(1), rows, along(rows, ("yh", "yl"), 1), (width,))
    first, second = in_pair((y >> 1).reshape(1), rows, along(rows, ("yh", "yl"), 3), WIDTHS)
    for bit, mask in ((0, 1), (1, 3)):
        came = (along(first, "z", mask), along(second, "x", mask))
        bits = (jnp.stack([z, x]) >> bit) & 1
        first, second = in_pairs(bits, (first, came[0], second, came[1]))
    came = [along(first, "x", 1), along(first, "x", 3), along(second, "z", 1), along(second, "z", 3)]
    place = jnp.stack([core, device]).astype(jnp.int32)
    own, send = pick_part(place, token_ids.reshape(1, 256), student_head_t)
    came, picked = lax.optimization_barrier((came, join_part(own, swap_cores(send))))
    halves = halves_of(came)
    far = [
        along(half, line, mask)
        for half, line, mask in zip(halves, ("x", "x", "z", "z"), (3, 1, 3, 1))
    ]
    far = lax.optimization_barrier(far)
    rows = (
        whole_rows(x.reshape(1), [first] + came[:2] + far[:2]),
        whole_rows(z.reshape(1), [second] + came[2:] + far[2:]),
    )
    rows, picked = lax.optimization_barrier((rows, picked))
    picked = exchange(picked, CHIPS)
    others = tuple(swap_cores(part) for part in rows)
    sums = logits_part(own_core, rows, heads)
    student, teacher, stats = logits_part(1 - own_core, others, heads, sums)
    stats = kernel_call(
        chip_stats_kernel,
        "chip_stats",
        shape_of((64, 8, 128), jnp.float32),
        limit=2,
        in_specs=[VMEM] * 2,
        out_specs=VMEM,
    )(stats, swap_cores(stats))
    stats, picked = lax.optimization_barrier((stats, picked))
    every = exchange(stats, CHIPS)
    embedded, ffn_rows = kernel_call(
        embed_kernel,
        "embed",
        [shape_of(BLOCK, jnp.float32), shape_of(BLOCK)],
        in_specs=[VMEM] * 2,
        out_specs=[VMEM] * 2,
    )(picked, ffn_gain)

    weight = token_weight.reshape(2, 4, 2, 4, 2, 2).transpose(1, 3, 2, 4, 0, 5).reshape(1, 256)
    own, send, divergence = row_grad_part(
        own_core, every, weight, teacher, student, student_head_t
    )
    divergence = divergence.reshape(4, 4, 2, 2, 2, 2).transpose(4, 0, 2, 1, 3, 5).reshape(256)
    blocks = exchange(join_part(own, swap_cores(send), ffn_rows), CHIPS)
    final_grad, halves = kernel_call(
        final_kernel,
        "final",
        [shape_of(BLOCK, jnp.float32), shape_of((64,) + BLOCK)],
        limit=12,
        in_specs=[VMEM] * 3,
        out_specs=[VMEM] * 2,
        scratch_shapes=[pltpu.VMEM(BLOCK, jnp.float32)],
    )(blocks, student_states, student_gain)
    hidden = ffn_part(
        gate_kernel,
        "gate_upper",
        [shape_of((2 * gate_t.shape[0], 128), jnp.float32)] * 2,
        blocks,
        swap_cores(blocks),
        gate_t,
        up_t,
    )
    halves = exchange(halves, CHIPS)
    weights = (down_weight, gate_t, up_t)
    shape = (128, SEGMENTS * SEGMENT)
    others = swap_cores(halves)
    (own,) = ffn_part(
        ffn_grad_kernel, "ffn_grad", [shape_of(shape, jnp.float32)], halves, hidden[0], *weights
    )
    others, own = lax.optimization_barrier((others, own))
    (send,) = ffn_part(ffn_grad_kernel, "ffn_grad", [shape_of(shape)], others, hidden[1], *weights)
    ffn_grad = exchange(join_part(own, swap_cores(send)), CHIPS)
    state_grad = kernel_call(
        state_kernel,
        "state",
        shape_of((2, 4096), jnp.float32),
        in_specs=[VMEM] * 4,
        out_specs=VMEM,
    )(ffn_grad, final_grad, embedded, ffn_gain)
    return (divergence, state_grad)


def solution(mesh):
    fine = Mesh(mesh.devices.reshape(SHAPE), AXES)
    in_specs = (
        P(AXES, None),
        P(),
        P(None, AXES),
        P(AXES, None),
        P(),
        P(None, AXES),
        P(),
        P(),
        P(None, AXES),
        P(None, AXES),
        P(AXES, None),
        P(),
    )
    out_specs = (P(), P(AXES, None))
    return jax.shard_map(shards, mesh=fine, in_specs=in_specs, out_specs=out_specs, check_vma=False)
```

```python
import functools

import jax
import jax.numpy as jnp
from jax import lax
from jax.experimental import pallas as pl
from jax.experimental.pallas import tpu as pltpu
from jax.sharding import Mesh
from jax.sharding import PartitionSpec as P

eps = 1e-05
SHAPE = (2, 4, 2, 4, 2)
AXES = ("core", "x", "yh", "z", "yl")
CHIPS = AXES[1:]
MIB = 1024 * 1024

VMEM = pl.BlockSpec(memory_space=pltpu.VMEM)
SMEM = pl.BlockSpec(memory_space=pltpu.SMEM)
ANY = pl.BlockSpec(memory_space=pl.ANY)
SEGMENTS = 8
SEGMENT = 512


def kernel_call(body, name, out_shape, limit=8, **options):
    return pl.pallas_call(
        body,
        name=name,
        out_shape=out_shape,
        compiler_params=pltpu.CompilerParams(vmem_limit_bytes=limit * MIB),
        cost_estimate=pl.CostEstimate(flops=1, bytes_accessed=1, transcendentals=0),
        **options,
    )


def shape_of(shape, dtype=jnp.bfloat16):
    return jax.ShapeDtypeStruct(shape, dtype)


def row_product(left, right):
    return lax.dot_general(
        left, right, (((1,), (1,)), ((), ())), preferred_element_type=jnp.float32
    )


def swap_cores(values):
    return lax.ppermute(values, "core", [(0, 1), (1, 0)])


def exchange(blocks, axes):
    return lax.all_to_all(blocks, axes, split_axis=0, concat_axis=0, tiled=True)


def rows_kernel(
    core_ref, teacher_from, teacher_gain, student_from, student_gain, keep_ref, send_ref,
    teacher_ref, student_ref, teacher_gains, student_gains, gains, sems,
):
    copies = [
        pltpu.make_async_copy(source, target, sems.at[i])
        for i, (source, target) in enumerate(
            (
                (student_gain, student_gains),
                (student_from, student_ref),
                (teacher_gain, teacher_gains),
                (teacher_from, teacher_ref),
            )
        )
    ]
    for copy in copies:
        copy.start()
    for copy in copies:
        copy.wait()
    first = student_gain.shape[0]
    gains[:first, :] = student_gains[...].astype(jnp.float32)
    gains[first:, :] = teacher_gains[...].astype(jnp.float32)
    column = 0
    for values, base in ((student_ref, 0), (teacher_ref, first)):
        half = values.shape[1] // 2
        every = values[...].astype(jnp.float32)
        inverse = lax.rsqrt(jnp.mean(every * every, axis=-1, keepdims=True) + eps)
        for part, out in ((core_ref[0], keep_ref), (1 - core_ref[0], send_ref)):
            for k in range(half // 128):
                place = pl.ds(pl.multiple_of(part * half + k * 128, 128), 128)
                rows = values[:, place].astype(jnp.float32) * inverse
                rows = rows * gains[pl.ds(base + part * (half // 128) + k, 1), :]
                out[:, column + k * 128 : column + (k + 1) * 128] = rows.astype(jnp.bfloat16)
        column = column + half


def pair_kernel(place_ref, own_ref, came_ref, *out_refs):
    own, came = own_ref[...].astype(jnp.float32), came_ref[...].astype(jnp.float32)
    first = place_ref[0] == 0
    rows = jnp.concatenate([jnp.where(first, own, came), jnp.where(first, came, own)], axis=0)
    rows = rows.astype(jnp.bfloat16)
    column = 0
    for out in out_refs:
        out[...] = rows[:, column : column + out.shape[1]]
        column = column + out.shape[1]


def in_pair(bit, own, came, widths):
    tokens = 2 * own.shape[0]
    return kernel_call(
        pair_kernel,
        "pair",
        [shape_of((tokens, w)) for w in widths],
        in_specs=[SMEM] + [VMEM] * 2,
        out_specs=[VMEM] * len(widths),
    )(bit, own, came)


def groups_kernel(place_ref, *refs):
    count = (len(refs) - 1) // 3
    sources, outs, sems = refs[: 2 * count], refs[2 * count : -1], refs[-1]
    copies = []
    for g, out in enumerate(outs):
        for i in range(2):
            source = sources[2 * g + i]
            tokens = source.shape[0]
            at = pl.multiple_of((place_ref[g] ^ i) * tokens, tokens)
            copy = pltpu.make_async_copy(source, out.at[pl.ds(at, tokens), :], sems.at[2 * g + i])
            copy.start()
            copies.append(copy)
    for copy in copies:
        copy.wait()


def in_pairs(bits, parts):
    tokens = 2 * parts[0].shape[0]
    return kernel_call(
        groups_kernel,
        "pairs",
        [shape_of((tokens, part.shape[1])) for part in parts[::2]],
        limit=4,
        in_specs=[SMEM] + [ANY] * len(parts),
        out_specs=[VMEM] * (len(parts) // 2),
        scratch_shapes=[pltpu.SemaphoreType.DMA((len(parts),))],
    )(bits, *parts)


def halves_kernel(*refs):
    count = (len(refs) - 1) // 2
    copies = []
    for i, (piece, out) in enumerate(zip(refs[:count], refs[count:])):
        rows = out.shape[0]
        copy = pltpu.make_async_copy(piece.at[pl.ds((i % 2) * rows, rows), :], out, refs[-1].at[i])
        copy.start()
        copies.append(copy)
    for copy in copies:
        copy.wait()


def halves_of(pieces):
    return kernel_call(
        halves_kernel,
        "halves",
        [shape_of((p.shape[0] // 2, p.shape[1])) for p in pieces],
        limit=4,
        in_specs=[ANY] * len(pieces),
        out_specs=[VMEM] * len(pieces),
        scratch_shapes=[pltpu.SemaphoreType.DMA((len(pieces),))],
    )(*pieces)


def along(block, line, mask):
    return lax.ppermute(block, line, [(i, i ^ mask) for i in range(4)])


def whole_kernel(place_ref, *refs):
    pieces, out, sems = refs[:5], refs[5], refs[6]
    tokens = pieces[0].shape[0]
    copies = []
    for i, (mask, half) in enumerate(((0, 0), (1, 0), (3, 0), (2, 0), (2, 1))):
        at = (place_ref[0] ^ mask) * tokens + half * (tokens // 2)
        at = pl.multiple_of(at, tokens // 2)
        rows = pieces[i].shape[0]
        copy = pltpu.make_async_copy(pieces[i], out.at[pl.ds(at, rows), :], sems.at[i])
        copy.start()
        copies.append(copy)
    for copy in copies:
        copy.wait()


def whole_rows(place, pieces):
    tokens, width = pieces[0].shape
    return kernel_call(
        whole_kernel,
        "whole",
        shape_of((4 * tokens, width)),
        limit=6,
        in_specs=[SMEM] + [ANY] * 5,
        out_specs=VMEM,
        scratch_shapes=[pltpu.SemaphoreType.DMA((5,))],
    )(place, *pieces)


GROUPS = (
    ((0, 0, 2048), (1, 0, 3072)),
    ((1, 3072, 2560), (1, 5632, 2560)),
)
WIDTHS = tuple(sum(p[2] for p in group) for group in GROUPS)


def reordered(values):
    source = lax.broadcasted_iota(jnp.int32, (256, 256), 0)
    place = lax.broadcasted_iota(jnp.int32, (256, 256), 1)
    wanted = (((place >> 4) & 3) << 6) | (((place >> 6) & 3) << 4) | (place & 15)
    moves = (source == wanted).astype(jnp.bfloat16)
    high = values.astype(jnp.bfloat16)
    rest = values - high.astype(jnp.float32)
    middle = rest.astype(jnp.bfloat16)
    low = (rest - middle.astype(jnp.float32)).astype(jnp.bfloat16)
    high, middle, low = (
        jnp.dot(part, moves, preferred_element_type=jnp.float32) for part in (high, middle, low)
    )
    return (high + middle) + low


def softmax_stats(teacher, student, stats_out):
    teacher_peak = jnp.max(teacher, axis=0, keepdims=True)
    student_peak = jnp.max(student, axis=0, keepdims=True)
    teacher_exp = jnp.exp(teacher - teacher_peak)
    teacher_total = jnp.sum(teacher_exp, axis=0, keepdims=True)
    student_total = jnp.sum(jnp.exp(student - student_peak), axis=0, keepdims=True)
    cross = jnp.sum(teacher_exp * (teacher - student), axis=0, keepdims=True)
    stats = (
        teacher_peak + jnp.log(teacher_total),
        student_peak + jnp.log(student_total),
        cross / teacher_total,
    )
    rows = [row[:, :128] for row in stats] + [row[:, 128:] for row in stats]
    stats_out[...] = jnp.concatenate(rows + [jnp.zeros((2, 128), jnp.float32)], axis=0)


def logits_kernel(last, place_ref, *refs):
    rows_from, heads, refs = refs[:2], refs[2:4], refs[4:]
    rows, head, row_sems, head_sems = refs[-4:]
    refs = refs[:-4]
    copies = []
    column = 0
    for group, source in zip(GROUPS, rows_from):
        base = column
        for kind, start, width in group:
            i = len(copies)
            columns = slice(column, column + width)
            size = heads[kind].shape[1] // 2
            start = pl.multiple_of(place_ref[0] * size + start, 128)
            pair = (
                pltpu.make_async_copy(
                    source.at[:, column - base : column - base + width],
                    rows.at[:, columns],
                    row_sems.at[i],
                ),
                pltpu.make_async_copy(
                    heads[kind].at[:, pl.ds(start, width)], head.at[:, columns], head_sems.at[i]
                ),
            )
            copies.append((kind + (base > 0), columns, pair))
            column = column + width
    ahead = 2
    for _, _, pair in copies[:ahead]:
        for copy in pair:
            copy.start()
    sums = [None, None, None]
    for i, (kind, columns, pair) in enumerate(copies):
        for copy in pair:
            copy.wait()
        if i + ahead < len(copies):
            for copy in copies[i + ahead][2]:
                copy.start()
        term = row_product(head[:, columns], rows[:, columns])
        sums[kind] = term if sums[kind] is None else sums[kind] + term
    if last:
        came, (student_out, teacher_out, stats_out) = refs[:3], refs[3:]
        student, teacher, second = (total + ref[...] for total, ref in zip(sums, came))
        teacher = teacher + reordered(second)
        student_out[...] = student
        teacher_out[...] = teacher
        softmax_stats(teacher, student, stats_out)
    else:
        for total, out in zip(sums, refs):
            out[...] = total


def logits_part(place, rows, heads, sums=()):
    vocab, tokens = heads[1].shape[0], rows[0].shape[0]
    shape = shape_of((vocab, tokens), jnp.float32)
    last = len(sums) > 0
    pieces = sum(len(group) for group in GROUPS)
    out_shape = [shape, shape, shape_of((8, 128), jnp.float32) if last else shape]
    return kernel_call(
        functools.partial(logits_kernel, last),
        "logits",
        out_shape,
        limit=48,
        in_specs=[SMEM] + [ANY] * 4 + [VMEM] * len(sums),
        out_specs=[VMEM] * 3,
        scratch_shapes=[
            pltpu.VMEM((tokens, sum(WIDTHS)), jnp.bfloat16),
            pltpu.VMEM((vocab, sum(WIDTHS)), jnp.bfloat16),
            pltpu.SemaphoreType.DMA((pieces,)),
            pltpu.SemaphoreType.DMA((pieces,)),
        ],
    )(place, *rows, *heads, *sums)


def one_hot_rows(core):
    place = lax.broadcasted_iota(jnp.int32, (256, 256), 0)
    column = lax.broadcasted_iota(jnp.int32, (256, 256), 1)
    x, yh, z, yl = (place >> 4) & 3, (place >> 3) & 1, (place >> 1) & 3, place & 1
    source = (x << 6) | (z << 4) | (yh << 3) | (yl << 2)
    source = source | (((place >> 7) ^ core) << 1) | ((place >> 6) & 1)
    return (column == source).astype(jnp.bfloat16)


def head_copies(source, head, sems):
    columns = head.shape[1] // sems.shape[0]
    parts = [slice(i * columns, (i + 1) * columns) for i in range(sems.shape[0])]
    copies = [
        pltpu.make_async_copy(source.at[:, part], head.at[:, part], sems.at[i])
        for i, part in enumerate(parts)
    ]
    for copy in copies:
        copy.start()
    return list(zip(parts, copies))


def merged_stats(every):
    peak = jnp.max(every, axis=0)
    scaled = jnp.exp(every - peak[None])
    total = jnp.sum(scaled, axis=0)
    cross = jnp.sum(scaled * pltpu.roll(every, 6, 1), axis=0) / total
    return peak + jnp.log(total), cross


def chip_stats_kernel(own_ref, came_ref, out_ref):
    lse, cross = merged_stats(jnp.concatenate([own_ref[...][None], came_ref[...][None]], axis=0))
    row = lax.broadcasted_iota(jnp.int32, lse.shape, 0)
    merged = jnp.where((row == 2) | (row == 5), pltpu.roll(cross, 2, 0), lse)
    out_ref[...] = jnp.broadcast_to(merged[None], out_ref.shape)


def row_grad_kernel(
    core_ref, every_ref, weight_ref, teacher_ref, student_ref, head_from,
    own_ref, send_ref, divergence_ref, head, sems,
):
    copies = head_copies(head_from, head, sems)
    lse, cross = merged_stats(every_ref[...])
    teacher_lse = jnp.concatenate([lse[0:1], lse[3:4]], axis=1)
    student_lse = jnp.concatenate([lse[1:2], lse[4:5]], axis=1)
    divergence_ref[...] = (
        jnp.concatenate([cross[0:1], cross[3:4]], axis=1) - teacher_lse + student_lse
    )
    logit_grad = weight_ref[...] * (
        jnp.exp(student_ref[...] - student_lse) - jnp.exp(teacher_ref[...] - teacher_lse)
    )
    grad = row_product(one_hot_rows(core_ref[0]), logit_grad.astype(jnp.bfloat16))
    grad = grad.astype(jnp.bfloat16)
    half = own_ref.shape[0]
    for columns, copy in copies:
        copy.wait()
        out = jnp.dot(grad, head[:, columns], preferred_element_type=jnp.float32)
        own_ref[:, columns] = out[:half]
        send_ref[:, columns] = out[half:].astype(jnp.bfloat16)


def row_grad_part(core, every, weight, teacher, student, student_head_t):
    vocab, width = student_head_t.shape
    tokens = weight.shape[1]
    return kernel_call(
        row_grad_kernel,
        "row_grad",
        [
            shape_of((tokens // 2, width), jnp.float32),
            shape_of((tokens // 2, width)),
            shape_of((1, tokens), jnp.float32),
        ],
        limit=48,
        in_specs=[SMEM] + [VMEM] * 4 + [ANY],
        out_specs=[VMEM] * 3,
        scratch_shapes=[
            pltpu.VMEM((vocab, width), jnp.bfloat16),
            pltpu.SemaphoreType.DMA((4,)),
        ],
    )(core, every, weight, teacher, student, student_head_t)


def pick_kernel(place_ref, ids_ref, head_from, own_ref, send_ref, head, sems):
    copies = head_copies(head_from, head, sems)
    vocab, tokens = head.shape[0], ids_ref.shape[1]
    entry = lax.broadcasted_iota(jnp.int32, (vocab, tokens), 0) + place_ref[1] * vocab
    place = lax.broadcasted_iota(jnp.int32, (tokens, tokens), 0)
    column = lax.broadcasted_iota(jnp.int32, (tokens, tokens), 1)
    source = (((place >> 7) ^ place_ref[0]) << 7) | ((place & 63) << 1) | ((place >> 6) & 1)
    chosen = row_product(
        (column == source).astype(jnp.bfloat16), (ids_ref[...] == entry).astype(jnp.bfloat16)
    ).astype(jnp.bfloat16)
    half = own_ref.shape[0]
    for columns, copy in copies:
        copy.wait()
        out = jnp.dot(chosen, head[:, columns], preferred_element_type=jnp.float32)
        own_ref[:, columns] = out[:half].astype(jnp.bfloat16)
        send_ref[:, columns] = out[half:].astype(jnp.bfloat16)


def pick_part(place, ids, student_head_t):
    vocab, width = student_head_t.shape
    shape = shape_of((ids.shape[1] // 2, width))
    return kernel_call(
        pick_kernel,
        "pick",
        [shape, shape],
        limit=48,
        in_specs=[SMEM, VMEM, ANY],
        out_specs=[VMEM] * 2,
        scratch_shapes=[
            pltpu.VMEM((vocab, width), jnp.bfloat16),
            pltpu.SemaphoreType.DMA((4,)),
        ],
    )(place, ids, student_head_t)


def join_kernel(own_ref, came_ref, *refs):
    out_ref, rows = refs[-2:]
    chips, height = out_ref.shape[0], 2 * SEGMENTS
    for t in range(2):
        for i in range(SEGMENTS):
            for k in range(SEGMENT // 128):
                part = slice(t * chips, (t + 1) * chips)
                lanes = slice(i * SEGMENT + k * 128, i * SEGMENT + (k + 1) * 128)
                total = own_ref[part, lanes].astype(jnp.float32)
                total = total + came_ref[part, lanes].astype(jnp.float32)
                rows[k, pl.ds(t * SEGMENTS + i, chips, stride=height), :] = total
    for k in range(SEGMENT // 128):
        out_ref[:, :height, k * 128 : (k + 1) * 128] = (
            rows[k].reshape(chips, height, 128).astype(jnp.bfloat16)
        )
    if len(refs) > 2:
        out_ref[:, height:, :] = jnp.broadcast_to(refs[0][...][None], (chips, height, SEGMENT))


def join_part(own, came, *every):
    chips, height = own.shape[0] // 2, 2 * SEGMENTS
    return kernel_call(
        join_kernel,
        "join",
        shape_of((chips, height * (1 + len(every)), SEGMENT)),
        limit=14,
        in_specs=[VMEM] * (2 + len(every)),
        out_specs=VMEM,
        scratch_shapes=[pltpu.VMEM((SEGMENT // 128, chips * height, 128), jnp.float32)],
    )(own, came, *every)


def block_gain(gain_ref):
    gain = gain_ref[...].astype(jnp.float32)
    lanes = SEGMENT // 128
    token = jnp.concatenate(
        [
            jnp.concatenate([gain[lanes * i + k : lanes * i + k + 1] for k in range(lanes)], axis=1)
            for i in range(SEGMENTS)
        ],
        axis=0,
    )
    return jnp.concatenate([token, token], axis=0)


def block_mean(values):
    means = []
    for t in range(2):
        part = values[t * SEGMENTS : (t + 1) * SEGMENTS]
        total = jnp.sum(jnp.sum(part, axis=0, keepdims=True), axis=1, keepdims=True)
        means.append(jnp.broadcast_to(total / (SEGMENTS * SEGMENT), (SEGMENTS, 1)))
    return jnp.concatenate(means, axis=0)


def block_inverse(values):
    return lax.rsqrt(block_mean(values * values) + eps)


def block_back(upstream, values, gain):
    inverse = block_inverse(values)
    gained = upstream * gain
    return inverse * gained - values * inverse**3 * block_mean(gained * values)


def block_sum(blocks_ref):
    return jnp.sum(blocks_ref[:, : 2 * SEGMENTS, :].astype(jnp.float32), axis=0)


def embed_kernel(blocks_ref, gain_ref, embedded_ref, rows_ref):
    values = block_sum(blocks_ref)
    embedded_ref[...] = values
    rows = values * block_inverse(values) * block_gain(gain_ref)
    rows_ref[...] = rows.astype(jnp.bfloat16)


def final_kernel(blocks_ref, states_ref, gain_ref, grad_ref, out_ref, states):
    for i in range(SEGMENTS):
        part = states_ref[:, i * SEGMENT : (i + 1) * SEGMENT].astype(jnp.float32)
        for t in range(2):
            states[t * SEGMENTS + i : t * SEGMENTS + i + 1, :] = part[t : t + 1]
    grad = block_back(block_sum(blocks_ref), states[...], block_gain(gain_ref))
    grad_ref[...] = grad
    out_ref[...] = jnp.broadcast_to(grad.astype(jnp.bfloat16)[None], out_ref.shape)


def state_kernel(blocks_ref, grad_ref, embedded_ref, gain_ref, out_ref):
    back = block_back(block_sum(blocks_ref), embedded_ref[...], block_gain(gain_ref))
    grad = grad_ref[...] + back
    for t in range(2):
        for i in range(SEGMENTS):
            out_ref[t : t + 1, i * SEGMENT : (i + 1) * SEGMENT] = grad[
                t * SEGMENTS + i : t * SEGMENTS + i + 1
            ]


BLOCK = (2 * SEGMENTS, SEGMENT)


def spread_rows(values, rows):
    values = values.astype(jnp.float32)
    values = values.reshape(values.shape[0] * values.shape[1], values.shape[2])
    for k in range(SEGMENT // 128):
        rows[k] = values[:, k * 128 : (k + 1) * 128]


def segment_rows(rows, segment):
    height = 2 * SEGMENTS
    parts = []
    for t in range(2):
        at = pl.ds(t * SEGMENTS + segment, rows.shape[1] // height, stride=height)
        parts.append(jnp.concatenate([rows[k, at, :] for k in range(SEGMENT // 128)], axis=1))
    return jnp.concatenate(parts, axis=0).astype(jnp.bfloat16)


def gate_kernel(own_ref, other_ref, gate_ref, up_ref, *refs):
    rows = refs[-1]
    for ref, out in zip((own_ref, other_ref), refs):
        spread_rows(ref[:, 2 * SEGMENTS :, :], rows)
        hidden = None
        for i in range(SEGMENTS):
            columns = slice(i * SEGMENT, (i + 1) * SEGMENT)
            weight = jnp.concatenate([gate_ref[:, columns], up_ref[:, columns]], axis=0)
            term = row_product(weight, segment_rows(rows, i))
            hidden = term if hidden is None else hidden + term
        out[...] = hidden


def ffn_grad_kernel(blocks_ref, hidden_ref, down_ref, gate_ref, up_ref, out_ref, rows):
    spread_rows(blocks_ref[...], rows)
    units = down_ref.shape[0]
    act_grad = None
    for i in range(SEGMENTS):
        columns = slice(i * SEGMENT, (i + 1) * SEGMENT)
        term = row_product(down_ref[:, columns], segment_rows(rows, i))
        act_grad = term if act_grad is None else act_grad + term
    gate, upper = hidden_ref[:units, :], hidden_ref[units:, :]
    sigmoid_gate = jax.nn.sigmoid(gate)
    gate_grad = act_grad * upper * sigmoid_gate * (1.0 + gate * (1.0 - sigmoid_gate))
    upper_grad = act_grad * gate * sigmoid_gate
    grads = jnp.concatenate([gate_grad, upper_grad], axis=0).astype(jnp.bfloat16)
    tokens = grads.shape[1]
    same = lax.broadcasted_iota(jnp.int32, (tokens, tokens), 0) == lax.broadcasted_iota(
        jnp.int32, (tokens, tokens), 1
    )
    grads = row_product(same.astype(jnp.bfloat16), grads).astype(jnp.bfloat16)
    for i in range(SEGMENTS):
        columns = slice(i * SEGMENT, (i + 1) * SEGMENT)
        weight = jnp.concatenate([gate_ref[:, columns], up_ref[:, columns]], axis=0)
        out = jnp.dot(grads, weight, preferred_element_type=jnp.float32)
        out_ref[:, columns] = out.astype(out_ref.dtype)


def ffn_part(body, name, out_shape, *operands):
    return kernel_call(
        body,
        name,
        out_shape,
        limit=20,
        in_specs=[VMEM] * len(operands),
        out_specs=[VMEM] * len(out_shape),
        scratch_shapes=[pltpu.VMEM((SEGMENT // 128, 64 * 2 * SEGMENTS, 128), jnp.float32)],
    )(*operands)


def shards(
    teacher_states,
    teacher_gain,
    teacher_head,
    student_states,
    student_gain,
    student_head,
    token_ids,
    ffn_gain,
    gate_weight,
    up_weight,
    down_weight,
    token_weight,
):
    core = lax.axis_index("core")
    device = lax.axis_index(AXES)
    own_core = jnp.full((1,), core, jnp.int32)
    x, z, y = (lax.axis_index(line).astype(jnp.int32) for line in ("x", "z", ("yh", "yl")))
    teacher_gain, student_gain, ffn_gain = (
        gain.reshape(-1, 128) for gain in (teacher_gain, student_gain, ffn_gain)
    )
    student_head_t, teacher_head_t = student_head.T, teacher_head.T
    heads = (student_head_t, teacher_head_t)
    gate_t, up_t = gate_weight.T, up_weight.T

    width = sum(WIDTHS)
    half_shape = shape_of((2, width))
    keep, send = kernel_call(
        rows_kernel,
        "rows",
        [half_shape, half_shape],
        limit=56,
        in_specs=[SMEM] + [ANY] * 4,
        out_specs=[VMEM] * 2,
        scratch_shapes=[
            pltpu.VMEM(teacher_states.shape, jnp.bfloat16),
            pltpu.VMEM(student_states.shape, jnp.bfloat16),
            pltpu.VMEM(teacher_gain.shape, jnp.bfloat16),
            pltpu.VMEM(student_gain.shape, jnp.bfloat16),
            pltpu.VMEM((160, 128), jnp.float32),
            pltpu.SemaphoreType.DMA((4,)),
        ],
    )(own_core, teacher_states, teacher_gain, student_states, student_gain)
    (rows,) = in_pair(own_core, keep, swap_cores(send), (width,))

    (rows,) = in_pair((y & 1).reshape(1), rows, along(rows, ("yh", "yl"), 1), (width,))
    first, second = in_pair((y >> 1).reshape(1), rows, along(rows, ("yh", "yl"), 3), WIDTHS)
    for bit, mask in ((0, 1), (1, 3)):
        came = (along(first, "z", mask), along(second, "x", mask))
        bits = (jnp.stack([z, x]) >> bit) & 1
        first, second = in_pairs(bits, (first, came[0], second, came[1]))
    place = jnp.stack([core, device]).astype(jnp.int32)
    own, send = pick_part(place, token_ids.reshape(1, 256), student_head_t)
    send, first, second = lax.optimization_barrier((send, first, second))
    came = [along(first, "x", 1), along(first, "x", 3), along(second, "z", 1), along(second, "z", 3)]
    came, picked = lax.optimization_barrier((came, join_part(own, swap_cores(send))))
    halves = halves_of(came)
    far = [
        along(half, line, mask)
        for half, line, mask in zip(halves, ("x", "x", "z", "z"), (3, 1, 3, 1))
    ]
    far = lax.optimization_barrier(far)
    rows = (
        whole_rows(x.reshape(1), [first] + came[:2] + far[:2]),
        whole_rows(z.reshape(1), [second] + came[2:] + far[2:]),
    )
    rows, picked = lax.optimization_barrier((rows, picked))
    picked = exchange(picked, CHIPS)
    others = tuple(swap_cores(part) for part in rows)
    sums = logits_part(own_core, rows, heads)
    student, teacher, stats = logits_part(1 - own_core, others, heads, sums)
    stats = kernel_call(
        chip_stats_kernel,
        "chip_stats",
        shape_of((64, 8, 128), jnp.float32),
        limit=2,
        in_specs=[VMEM] * 2,
        out_specs=VMEM,
    )(stats, swap_cores(stats))
    stats, picked = lax.optimization_barrier((stats, picked))
    every = exchange(stats, CHIPS)
    embedded, ffn_rows = kernel_call(
        embed_kernel,
        "embed",
        [shape_of(BLOCK, jnp.float32), shape_of(BLOCK)],
        in_specs=[VMEM] * 2,
        out_specs=[VMEM] * 2,
    )(picked, ffn_gain)

    weight = token_weight.reshape(2, 4, 2, 4, 2, 2).transpose(1, 3, 2, 4, 0, 5).reshape(1, 256)
    own, send, divergence = row_grad_part(
        own_core, every, weight, teacher, student, student_head_t
    )
    divergence = divergence.reshape(4, 4, 2, 2, 2, 2).transpose(4, 0, 2, 1, 3, 5).reshape(256)
    blocks = exchange(join_part(own, swap_cores(send), ffn_rows), CHIPS)
    final_grad, halves = kernel_call(
        final_kernel,
        "final",
        [shape_of(BLOCK, jnp.float32), shape_of((64,) + BLOCK)],
        limit=12,
        in_specs=[VMEM] * 3,
        out_specs=[VMEM] * 2,
        scratch_shapes=[pltpu.VMEM(BLOCK, jnp.float32)],
    )(blocks, student_states, student_gain)
    hidden = ffn_part(
        gate_kernel,
        "gate_upper",
        [shape_of((2 * gate_t.shape[0], 128), jnp.float32)] * 2,
        blocks,
        swap_cores(blocks),
        gate_t,
        up_t,
    )
    halves = exchange(halves, CHIPS)
    weights = (down_weight, gate_t, up_t)
    shape = (128, SEGMENTS * SEGMENT)
    others = swap_cores(halves)
    (own,) = ffn_part(
        ffn_grad_kernel, "ffn_grad", [shape_of(shape, jnp.float32)], halves, hidden[0], *weights
    )
    others, own = lax.optimization_barrier((others, own))
    (send,) = ffn_part(ffn_grad_kernel, "ffn_grad", [shape_of(shape)], others, hidden[1], *weights)
    ffn_grad = exchange(join_part(own, swap_cores(send)), CHIPS)
    state_grad = kernel_call(
        state_kernel,
        "state",
        shape_of((2, 4096), jnp.float32),
        in_specs=[VMEM] * 4,
        out_specs=VMEM,
    )(ffn_grad, final_grad, embedded, ffn_gain)
    return (divergence, state_grad)


def solution(mesh):
    fine = Mesh(mesh.devices.reshape(SHAPE), AXES)
    in_specs = (
        P(AXES, None),
        P(),
        P(None, AXES),
        P(AXES, None),
        P(),
        P(None, AXES),
        P(),
        P(),
        P(None, AXES),
        P(None, AXES),
        P(AXES, None),
        P(),
    )
    out_specs = (P(), P(AXES, None))
    return jax.shard_map(shards, mesh=fine, in_specs=in_specs, out_specs=out_specs, check_vma=False)
```
